128 devices in a mesh: section: 2 (over core), tp: 4 (over x), rep: 16 (over z, y).
Axes of the slice: x: 4, y: 4, z: 4, core: 2. Of those that a mesh axis runs over, the one named last changes fastest.
Arguments:
- embeddings: bfloat16 [1024, 4096], P(None, 'tp')
- norm_gain: float32 [2, 4096], P('section'), may hold values from 0.25 to 1.75
- query_weight: bfloat16 [2, 4096, 2048], P('section', 'rep', 'tp')
- key_weight: bfloat16 [2, 4096, 1024], P('section', 'rep', 'tp')
- value_weight: bfloat16 [2, 4096, 1024], P('section', 'rep', 'tp'), may hold values from -0.09375 to 0.09375
- out_weight: bfloat16 [2, 2048, 4096], P('section', 'rep', 'tp'), may hold values from -0.25 to 0.25
- group_blocks: int32 [8], replicated, may hold values from 1 to 16, 64 in all
Outputs:
- final_state: bfloat16 [1024, 4096], P('section', 'tp')
The draws below stay inside these ranges and needn't reach their ends.
Inputs may be any that keep to these rules, and one draw needn't show every extreme that they name: `group_blocks`: the entries sum to 64, and the largest is exactly 16.
All inputs are finite; a program needn't handle non-finite values.
Results may differ from the reference program's by a relative error of at most 0.027.
Values may be sent and summed in bfloat16 or wider, within the bound.
A program may use at most 64 MiB of HBM per device.

```python
import math
import jax
import jax.numpy as jnp
import numpy as np
from jax import lax

D = 4096
HEAD = 128
KVH = 8
QH = 16
GROUPS = 8
UNIT = 16
LOOK = 2
SEQ = 1024
LAYERS = 2


def draw_query_weight(key, part):
    key = jax.random.fold_in(key, 11)
    fresh = jax.random.normal(key, (LAYERS, D, QH * HEAD), jnp.float32) / math.sqrt(D)
    return fresh.astype(jnp.bfloat16)


def draw_key_weight(key, part):
    key = jax.random.fold_in(key, 12)
    fresh = jax.random.normal(key, (LAYERS, D, KVH * HEAD), jnp.float32) / math.sqrt(D)
    return fresh.astype(jnp.bfloat16)


def draw_embeddings(key, part):
    key = jax.random.fold_in(key, 13)
    row_key, column_key, entry_key = jax.random.split(key, 3)
    row_scale = 0.3 * jnp.exp(jax.random.uniform(row_key, (SEQ, 1), jnp.float32, 0.0, math.log(10.0)))
    column_scale = jnp.exp(jax.random.uniform(column_key, (1, D), jnp.float32, math.log(0.5), math.log(2.0)))
    entries = jax.random.normal(entry_key, (SEQ, D), jnp.float32)
    return (entries * row_scale * column_scale).astype(jnp.bfloat16)


def steps_of(key, shape, cuts, smallest, top_value):
    level = 1.0
    for axis_at, shards_of in cuts:
        draws = jax.random.uniform(jax.random.fold_in(jax.random.fold_in(key, 6), axis_at), (shards_of,), jnp.float32, smallest / len(cuts), top_value / len(cuts))
        level = level * jnp.repeat(jnp.exp(draws), shape[axis_at] // shards_of).reshape((-1,) + (1,) * (len(shape) - 1 - axis_at))
    return level


def length_profile(number_of, total, most, skew):
    weights = [(1 << 20) // math.isqrt(rank ** skew) + 1 for rank in range(2, number_of + 1)]
    spare, counts = total - most - (number_of - 1), [1] * (number_of - 1)
    while spare > 0:
        movable = [i for i in range(number_of - 1) if counts[i] < most]
        whole, left = sum([weights[i] for i in movable]), spare
        for i in movable:
            extra = min(most - counts[i], max(1, left * weights[i] // whole), spare)
            counts[i] = counts[i] + extra
            spare = spare - extra
    return np.array([most] + counts)


def uneven_parts(key, number_of, total, reach, skew):
    if number_of == 2:
        one = jax.random.randint(key, (), max(1, total - reach), min(reach, total - 1) + 1)
        return jnp.stack([one, total - one])
    sizes = jnp.asarray(length_profile(number_of, total, reach, skew), jnp.int32)
    couples = (number_of - 1) // 2
    giver, taker = sizes[1:1 + 2 * couples:2], sizes[2:2 + 2 * couples:2]
    slack = jnp.minimum(giver - 1, reach - taker)
    moved = jax.random.randint(jax.random.fold_in(key, 1), (couples,), 0, 1 << 20) % (slack + 1)
    sizes = sizes.at[1:1 + 2 * couples:2].set(giver - moved).at[2:2 + 2 * couples:2].set(taker + moved)
    return sizes[jax.random.permutation(jax.random.fold_in(key, 2), number_of)]


def noise(own_key, shape, scale, limit, cuts=(), kind=jnp.bfloat16):
    array = jax.random.normal(own_key, shape, jnp.float32) * scale
    if len(cuts) > 0:
        array = steps_of(own_key, shape, cuts, -0.22, 0.18) * array
    return jnp.clip(array, min=-limit, max=limit).astype(kind)


def setup_inputs(seed: int = 0) -> dict:
    seeds = jax.random.split(jax.random.key(seed), 8)
    embeddings = draw_embeddings(jax.random.fold_in(seeds[7], 71), 0)
    norm_gain = jnp.clip(1.0 + 0.15 * jax.random.normal(seeds[1], (LAYERS, D), jnp.float32), 0.25, 1.75)
    query_weight = draw_query_weight(jax.random.fold_in(seeds[7], 71), 0)
    key_weight = draw_key_weight(jax.random.fold_in(seeds[7], 71), 0)
    value_weight = noise(seeds[4], (LAYERS, D, KVH * HEAD), D ** -0.5, 0.09375, ((0, 2), (1, 16), (2, 4)))
    out_weight = noise(seeds[5], (LAYERS, QH * HEAD, D), (QH * HEAD // 4) ** -0.5, 0.25, ((0, 2), (1, 16), (2, 4)))
    group_blocks = uneven_parts(seeds[6], GROUPS, SEQ // UNIT, SEQ // UNIT // 4, 1).astype(jnp.int32)
    return dict(embeddings=embeddings, norm_gain=norm_gain, query_weight=query_weight, key_weight=key_weight, value_weight=value_weight, out_weight=out_weight, group_blocks=group_blocks)


def group_numbers(group_blocks, count):
    lengths = group_blocks.astype(jnp.int32) * UNIT
    starts = (jnp.cumsum(lengths) - lengths).astype(jnp.int32)
    places = jnp.arange(count, dtype=jnp.int32)
    return lax.optimization_barrier(jnp.sum((places[:, None] >= starts[None, 1:]).astype(jnp.int32), axis=1)).astype(jnp.int32)

def reference(embeddings, norm_gain, query_weight, key_weight, value_weight, out_weight, group_blocks):
    group_of = group_numbers(group_blocks, SEQ)
    places = jnp.arange(SEQ, dtype=jnp.int32)
    allowed = (places[None, :] <= places[:, None]) & (group_of[None, :] >= group_of[:, None] - LOOK)
    score_scale = 1.0 / math.sqrt(HEAD)
    hidden_rows = embeddings
    for layer_index in range(LAYERS):
        widened = hidden_rows.astype(jnp.float32)
        inverse = lax.rsqrt(lax.optimization_barrier(jnp.mean(widened * widened, axis=1, keepdims=True)) + 1e-05)
        normed = (widened * inverse * norm_gain[layer_index].astype(jnp.float32)).astype(jnp.bfloat16)
        queries = jnp.dot(normed, query_weight[layer_index], preferred_element_type=jnp.float32).astype(jnp.bfloat16)
        key_rows = jnp.dot(normed, key_weight[layer_index], preferred_element_type=jnp.float32).astype(jnp.bfloat16)
        value_rows = jnp.dot(normed, value_weight[layer_index], preferred_element_type=jnp.float32).astype(jnp.bfloat16)
        query_wide = queries.astype(jnp.float32).reshape(SEQ, KVH, 2, HEAD)
        key_wide = key_rows.astype(jnp.float32).reshape(SEQ, KVH, HEAD)
        value_wide = value_rows.astype(jnp.float32).reshape(SEQ, KVH, HEAD)
        scores = jnp.einsum('qgrd,kgd->grqk', query_wide, key_wide) * score_scale
        scores = jnp.where(allowed, scores, -jnp.inf)
        weights = jax.nn.softmax(scores, axis=-1).astype(jnp.bfloat16)
        attended = jnp.einsum('grqk,kgd->qgrd', weights.astype(jnp.float32), value_wide)
        attended = attended.astype(jnp.bfloat16).reshape(SEQ, QH * HEAD)
        projected = jnp.dot(attended, out_weight[layer_index], preferred_element_type=jnp.float32)
        hidden_rows = (hidden_rows.astype(jnp.float32) + projected).astype(jnp.bfloat16)
    return hidden_rows
```

```python
import math

import jax
import jax.numpy as jnp
from jax import lax
from jax.experimental import pallas as pl
from jax.experimental.pallas import tpu as pltpu
from jax.sharding import PartitionSpec as P

MESH = pl.DeviceIdType.MESH
BF = jnp.bfloat16
F32 = jnp.float32
D = 4096
GROUPS = 8
UNIT = 16
SCALE = 1.0 / math.sqrt(128)

W_LEFT, W_RIGHT, W_FAR = 0, 3, 6
O_LEFT, O_RIGHT, O_FAR = 9, 10, 11
X_IN = 13
RS_IN, SQ_IN = 17, 20
KV_IN = 23
AT_IN = 30
RO_IN = 34
RES_IN = 37
FA_IN, FAY_IN = 38, 42
FB_IN, FBZ_IN = 45, 49
N_RECV = 55
N_SEND = 72
N_LOCAL = 8


def kernel(
    emb, gain, wq, wk, wv, wo, blocks, out,
    WQ, WK, WV, WO, X, XG, ACC, PS, PR, SQ, SQR, KV, AT, ATR, OS, OR, RES, ST, FIN,
    send_sems, recv_sems, local_sems, go,
):
    s = lax.axis_index("section")
    t = lax.axis_index("tp")
    r = lax.axis_index("rep")
    z = r // 4
    y = r % 4
    g = z // 2
    zh = z % 2
    first = s == 0
    second = s == 1

    def dev(s_, t_, z_, y_):
        return (s_, t_, z_ * 4 + y_)

    def up(v, d):
        return (v + d) % 4

    pending = []

    def send(src, dst, ridx, device, when=None):
        c = pltpu.make_async_remote_copy(
            src_ref=src, dst_ref=dst, send_sem=send_sems.at[len(pending)],
            recv_sem=recv_sems.at[ridx], device_id=device, device_id_type=MESH,
        )
        if when is None:
            c.start()
        else:
            pl.when(when)(c.start)
        pending.append((c, when))

    def arrived(ref, ridx, when=None):
        c = pltpu.make_async_remote_copy(
            src_ref=ref, dst_ref=ref, send_sem=send_sems.at[0],
            recv_sem=recv_sems.at[ridx], device_id=dev(1 - s, t, z, y), device_id_type=MESH,
        )
        if when is None:
            c.wait_recv()
        else:
            pl.when(when)(c.wait_recv)

    def rows(start, size):
        return pl.ds(pl.multiple_of(start, size), size)

    KV[...] = jnp.zeros_like(KV)

    own = [
        pltpu.make_async_copy(wq.at[0], WQ.at[rows(256 * y, 256)], local_sems.at[0]),
        pltpu.make_async_copy(wk.at[0], WK.at[rows(256 * y, 256)], local_sems.at[1]),
        pltpu.make_async_copy(wv.at[0], WV.at[rows(256 * y, 256)], local_sems.at[2]),
        pltpu.make_async_copy(wo.at[0], WO.at[rows(128 * y, 128)], local_sems.at[3]),
    ]
    for c in own:
        c.start()
    x_source = first & (t == z)
    own_x = pltpu.make_async_copy(emb.at[rows(256 * y, 256)], X, local_sems.at[4])
    own_res = pltpu.make_async_copy(emb.at[rows(256 * y + 64 * z, 64)], RES, local_sems.at[5])
    pl.when(x_source)(own_x.start)
    pl.when(first)(own_res.start)

    barrier = pltpu.get_barrier_semaphore()

    def greet(device):
        pl.semaphore_signal(barrier, inc=1, device_id=device, device_id_type=MESH)

    diagonal = z == t
    for d in (1, 2, 3):
        greet(dev(s, t, z, up(y, d)))
        greet(dev(s, t, up(z, d), y))
        greet(dev(s, t, z + 1 - 2 * zh, up(y, d)))
        greet(dev(1 - s, t, z, up(y, d)))
        greet(dev(1 - s, t, up(z, d), y))
        greet(dev(s, up(t, d), t, y))
        greet(dev(s, z, up(z, d), y))
    greet(dev(1 - s, t, z, y))
    greet(dev(s, up(t, 1), z, y))
    greet(dev(s, up(t, 3), z, y))

    @pl.when(jnp.logical_not(diagonal))
    def _():
        greet(dev(s, t, t, y))
        greet(dev(s, z, z, y))

    for d in range(4):
        @pl.when(first)
        def _():
            greet(dev(1, d, t, y))

        @pl.when(second)
        def _():
            greet(dev(0, z, d, y))
    pl.semaphore_wait(barrier, 21 + 1 + 2 + 4 + 2 * (1 - diagonal.astype(jnp.int32)))

    right, left = up(y, 1), up(y, 3)
    dev_r, dev_l = dev(s, t, z, right), dev(s, t, z, left)
    far = up(y, 2)

    half = (X.at[0:128], X.at[128:256])
    dx = (t - z + 4) % 4
    x_right, x_left = dev(s, up(t, 1), z, y), dev(s, up(t, 3), z, y)
    source = [emb.at[rows(256 * y, 128)], emb.at[rows(256 * y + 128, 128)]]
    for i in range(2):
        send(source[i], half[i], X_IN + i, x_right, x_source)
        send(source[1 - i], half[1 - i], X_IN + 1 - i, x_left, x_source)

    @pl.when(second)
    def _():
        pl.semaphore_wait(go, 1)

    at_y = rows(256 * y, 256)
    send(wq.at[0], WQ.at[at_y], W_LEFT, dev_r)
    send(wk.at[0], WK.at[at_y], W_RIGHT + 1, dev_l)
    send(wv.at[0], WV.at[at_y], W_RIGHT + 2, dev_l)
    send(wk.at[0], WK.at[at_y], W_LEFT + 1, dev_r)
    send(wv.at[0], WV.at[at_y], W_LEFT + 2, dev_r)
    send(wq.at[0], WQ.at[at_y], W_RIGHT, dev_l)

    near_right, near_left, opposite = first & (dx == 1), first & (dx == 3), first & (dx == 2)
    arrived(half[0], X_IN, near_right)
    send(half[0], half[0], X_IN, x_right, near_right)
    arrived(half[1], X_IN + 1, near_left)
    send(half[1], half[1], X_IN + 1, x_left, near_left)

    at_l, at_r, at_f = rows(256 * left, 256), rows(256 * right, 256), rows(256 * far, 256)
    arrived(WQ.at[at_l], W_LEFT)
    send(WQ.at[at_l], WQ.at[at_l], W_FAR, dev_r)
    arrived(WK.at[at_r], W_RIGHT + 1)
    send(WK.at[at_r], WK.at[at_r], W_FAR + 1, dev_l)
    arrived(WV.at[at_r], W_RIGHT + 2)
    send(WV.at[at_r], WV.at[at_r], W_FAR + 2, dev_l)

    ow_y = rows(128 * y, 128)
    send(wo.at[0], WO.at[ow_y], O_LEFT, dev_r)
    send(wo.at[0], WO.at[ow_y], O_RIGHT, dev_l)

    pl.when(x_source)(own_x.wait)
    arrived(half[1], X_IN + 1, near_right)
    arrived(half[0], X_IN, near_left)
    arrived(half[0], X_IN, opposite)
    arrived(half[1], X_IN + 1, opposite)
    for c in own:
        c.wait()

    ow_l, ow_r, ow_f = rows(128 * left, 128), rows(128 * right, 128), rows(128 * far, 128)
    lower = lambda start: rows(128 * start, 64)
    upper = lambda start: rows(128 * start + 64, 64)

    def rest_of_out_weights():
        arrived(WO.at[ow_l], O_LEFT)
        arrived(WO.at[ow_r], O_RIGHT)
        send(WO.at[lower(left)], WO.at[lower(left)], O_FAR, dev_r)
        send(WO.at[upper(right)], WO.at[upper(right)], O_FAR + 1, dev_l)

    for zp in range(4):
        arrived(X.at[pl.ds(64 * zp, 64)], X_IN + zp, second)

    x = X[...].astype(F32)
    XG[...] = (x * gain[:, rows(1024 * z, 1024)]).astype(BF)
    squares = jnp.sum(x * x, axis=1, keepdims=True)
    for h in range(2):
        column = jnp.broadcast_to(squares[128 * h:128 * h + 128], (128, 128))
        SQ[h] = jnp.transpose(column)[0:8]

    def multiply(block, start):
        at = rows(256 * block, 256)
        part = XG[:, at]
        for ref, lo, hi in ((WQ, 0, 512), (WK, 512, 768), (WV, 768, 1024)):
            product = jnp.dot(part, ref[at, :], preferred_element_type=F32)
            if start:
                ACC[:, lo:hi] = product
            else:
                ACC[:, lo:hi] += product

    multiply(y, True)
    arrived(WK.at[at_l], W_LEFT + 1)
    arrived(WV.at[at_l], W_LEFT + 2)
    multiply(left, False)
    arrived(WQ.at[at_r], W_RIGHT)
    multiply(right, False)
    arrived(WQ.at[at_f], W_FAR)
    arrived(WK.at[at_f], W_FAR + 1)
    arrived(WV.at[at_f], W_FAR + 2)
    multiply(far, False)
    for gg in range(2):
        for hh in range(2):
            part = ACC[128 * hh:128 * hh + 128, :]
            slot = 2 * gg + hh
            PS[slot, :, 0:256] = part[:, 256 * gg:256 * gg + 256].astype(BF)
            PS[slot, :, 256:384] = part[:, 512 + 128 * gg:640 + 128 * gg].astype(BF)
            PS[slot, :, 384:512] = part[:, 768 + 128 * gg:896 + 128 * gg].astype(BF)

    for d in (2, 1, 3):
        other = up(z, d)
        send(SQ.at[other % 2], SQR.at[d - 1], SQ_IN + d - 1, dev(s, t, other, y))
        send(PS.at[other], PR.at[d - 1], RS_IN + d - 1, dev(s, t, other, y))
    total = PS[z].astype(F32)
    square = SQ[zh]
    rest_of_out_weights()
    for d in (1, 3, 2):
        arrived(SQR.at[d - 1], SQ_IN + d - 1)
        square = square + SQR[d - 1]
        arrived(PR.at[d - 1], RS_IN + d - 1)
        total = total + PR[d - 1].astype(F32)
    inverse_row = lax.rsqrt(square * (1.0 / D) + 1e-5)
    inverse = jnp.transpose(jnp.broadcast_to(inverse_row[0:1], (128, 128)))
    wide = jnp.concatenate([inverse, inverse], axis=1)
    queries = (total[:, 0:256] * wide).astype(BF)
    block = 2 * y + zh
    KV[rows(128 * block, 128), :] = (total[:, 256:512] * wide).astype(BF)

    mine = KV.at[rows(128 * block, 128)]
    for dy in (2, 1, 3, 0):
        for dz in range(2):
            if dy + dz == 0:
                continue
            y_to = up(y, dy)
            h_to = zh if dz == 0 else 1 - zh
            send(mine, mine, KV_IN + 2 * dy + dz - 1, dev(s, t, 2 * g + h_to, y_to), 2 * y_to + h_to > block)

    places = 256 * y + 128 * zh + lax.broadcasted_iota(jnp.int32, (128, 1), 0)
    starts = []
    run = jnp.int32(0)
    for c in range(GROUPS):
        starts.append(run)
        run = run + blocks[c] * UNIT
    lowest = jnp.zeros((128, 1), jnp.int32)
    for c in range(GROUPS - 2):
        lowest = jnp.where(places >= starts[c + 2], starts[c], lowest)
    keys_at = lax.broadcasted_iota(jnp.int32, (128, 1024), 1)
    allowed = (keys_at <= places) & (keys_at >= lowest)

    for dy in (1, 3, 2, 0):
        for dz in range(2):
            if dy + dz == 0:
                continue
            y_from = up(y, 4 - dy)
            h_from = zh if dz == 0 else 1 - zh
            theirs = 2 * y_from + h_from
            arrived(KV.at[rows(128 * theirs, 128)], KV_IN + 2 * dy + dz - 1, theirs < block)

    @pl.when(first)
    def _():
        pl.semaphore_signal(go, inc=1, device_id=dev(1, t, z, y), device_id_type=MESH)

    keys = KV[:, 0:128]
    values = KV[:, 128:256]
    for h in range(2):
        scores = lax.dot_general(
            queries[:, 128 * h:128 * h + 128], keys, (((1,), (1,)), ((), ())), preferred_element_type=F32
        ) * SCALE
        scores = jnp.where(allowed, scores, -jnp.inf)
        exps = jnp.exp(scores - jnp.max(scores, axis=1, keepdims=True))
        norm = jnp.sum(exps, axis=1, keepdims=True)
        heads = jnp.dot(exps.astype(BF), values, preferred_element_type=F32) / norm
        AT[:, 128 * h:128 * h + 128] = heads.astype(BF)

    for d in (2, 1, 3):
        send(AT, ATR.at[z], AT_IN + z, dev(s, up(t, d), t, y))
    send(AT, ATR.at[z], AT_IN + z, dev(s, t, t, y), jnp.logical_not(diagonal))

    @pl.when(diagonal)
    def _():
        ATR[z] = AT[...]
    arrived(WO.at[lower(far)], O_FAR)
    arrived(WO.at[upper(far)], O_FAR + 1)
    for zp in range(4):
        arrived(ATR.at[zp], AT_IN + zp, jnp.logical_not(diagonal & (z == zp)))
    for hh in range(2):
        product = jnp.dot(ATR[hh], WO[0:256, :], preferred_element_type=F32)
        product = product + jnp.dot(ATR[2 + hh], WO[256:512, :], preferred_element_type=F32)
        OS[2 * hh] = product[0:64].astype(BF)
        OS[2 * hh + 1] = product[64:128].astype(BF)
    for d in (2, 1, 3):
        send(OS.at[up(z, d)], OR.at[d - 1], RO_IN + d - 1, dev(s, t, up(z, d), y))
    pl.when(first)(own_res.wait)
    arrived(RES, RES_IN, second)
    state = RES[...].astype(F32)
    projected = OS[z].astype(F32)
    for d in (1, 3, 2):
        arrived(OR.at[d - 1], RO_IN + d - 1)
        projected = projected + OR[d - 1].astype(F32)
    ST[...] = (state + projected).astype(BF)

    my_rows = rows(64 * z, 64)
    for d in (2, 1, 3, 0):
        send(ST, X.at[my_rows], X_IN + z, dev(1, up(t, d), t, y), first)
    send(ST, RES, RES_IN, dev(1, t, z, y), first)

    sec = y // 2
    at_out = rows(256 * (y % 2) + 64 * z, 64)
    ca, cb = pl.ds(0, 512), pl.ds(512, 512)
    keep = second & (sec == 1)

    @pl.when(keep)
    def _():
        FIN[at_out, :] = ST[...]
    cross = second & (sec == 0)
    for d in (2, 1, 3):
        send(ST.at[:, ca], FIN.at[at_out, ca], FA_IN + d, dev(sec, t, up(z, d), y), second)
        send(ST.at[:, cb], FIN.at[at_out, cb], FB_IN + d, dev(sec, t, z, up(y, d)), second)
    send(ST.at[:, ca], FIN.at[at_out, ca], FA_IN, dev(sec, t, z, y), cross)
    send(ST.at[:, cb], FIN.at[at_out, cb], FB_IN, dev(sec, t, z, y), cross)

    holder = sec == s
    for d in (0, 1, 3, 2):
        at = rows(256 * (y % 2) + 64 * up(z, 4 - d), 64)
        arrived(FIN.at[at, ca], FA_IN + d, holder if d else holder & first)
    block_y = rows(256 * (y % 2), 256)
    for d in (2, 1, 3):
        send(FIN.at[block_y, ca], FIN.at[block_y, ca], FAY_IN + d - 1, dev(s, t, z, up(y, d)), holder)
    for d in (0, 1, 3, 2):
        y_from = up(y, 4 - d)
        here = y_from // 2 == s
        at = rows(256 * (y_from % 2) + 64 * z, 64)
        arrived(FIN.at[at, cb], FB_IN + d, here if d else here & first)
    for e in (2, 1, 3):
        for yy in range(2):
            at = rows(256 * yy + 64 * z, 64)
            send(FIN.at[at, cb], FIN.at[at, cb], FBZ_IN + 2 * (e - 1) + yy, dev(s, t, up(z, e), y))
    for d in (1, 3, 2):
        y_from = up(y, 4 - d)
        at = rows(256 * (y_from % 2), 256)
        arrived(FIN.at[at, ca], FAY_IN + d - 1, y_from // 2 == s)
    for e in (1, 3, 2):
        for yy in range(2):
            at = rows(256 * yy + 64 * up(z, 4 - e), 64)
            arrived(FIN.at[at, cb], FBZ_IN + 2 * (e - 1) + yy)
    result = pltpu.make_async_copy(FIN, out, local_sems.at[6])
    result.start()
    for c, when in pending:
        if when is None:
            c.wait_send()
        else:
            pl.when(when)(c.wait_send)
    result.wait()


def on_device(*arrays):
    hbm = pl.BlockSpec(memory_space=pl.ANY)
    vmem = pl.BlockSpec(memory_space=pltpu.VMEM)
    return pl.pallas_call(
        kernel,
        out_shape=jax.ShapeDtypeStruct((512, 1024), BF),
        in_specs=[hbm, vmem, hbm, hbm, hbm, hbm, pl.BlockSpec(memory_space=pltpu.SMEM)],
        out_specs=hbm,
        scratch_shapes=[
            pltpu.VMEM((1024, 512), BF),
            pltpu.VMEM((1024, 256), BF),
            pltpu.VMEM((1024, 256), BF),
            pltpu.VMEM((512, 1024), BF),
            pltpu.VMEM((256, 1024), BF),
            pltpu.VMEM((256, 1024), BF),
            pltpu.VMEM((256, 1024), F32),
            pltpu.VMEM((4, 128, 512), BF),
            pltpu.VMEM((3, 128, 512), BF),
            pltpu.VMEM((2, 8, 128), F32),
            pltpu.VMEM((3, 8, 128), F32),
            pltpu.VMEM((1024, 256), BF),
            pltpu.VMEM((128, 256), BF),
            pltpu.VMEM((4, 128, 256), BF),
            pltpu.VMEM((4, 64, 1024), BF),
            pltpu.VMEM((3, 64, 1024), BF),
            pltpu.VMEM((64, 1024), BF),
            pltpu.VMEM((64, 1024), BF),
            pltpu.VMEM((512, 1024), BF),
            pltpu.SemaphoreType.DMA((N_SEND,)),
            pltpu.SemaphoreType.DMA((N_RECV,)),
            pltpu.SemaphoreType.DMA((N_LOCAL,)),
            pltpu.SemaphoreType.REGULAR,
        ],
        compiler_params=pltpu.CompilerParams(
            collective_id=0, has_side_effects=True, vmem_limit_bytes=56 * 1024 * 1024
        ),
    )(*arrays)


def solution(mesh):
    in_specs = (
        P(None, "tp"),
        P("section", None),
        P("section", "rep", "tp"),
        P("section", "rep", "tp"),
        P("section", "rep", "tp"),
        P("section", "rep", "tp"),
        P(),
    )
    return jax.shard_map(
        on_device, mesh=mesh, in_specs=in_specs, out_specs=P("section", "tp"), check_vma=False
    )
```

```python
import math

import jax
import jax.numpy as jnp
from jax import lax
from jax.experimental import pallas as pl
from jax.experimental.pallas import tpu as pltpu
from jax.sharding import PartitionSpec as P

MESH = pl.DeviceIdType.MESH
BF = jnp.bfloat16
F32 = jnp.float32
D = 4096
GROUPS = 8
UNIT = 16
SCALE = 1.0 / math.sqrt(128)

KV_LEFT, KV_RIGHT, KV_FAR = 0, 2, 4
Q_LEFT, Q_RIGHT, Q_FAR = 6, 8, 10
O_LEFT, O_RIGHT, O_FAR = 12, 13, 14
X_IN = 16
RS_IN, SQ_IN, RQ_IN = 24, 27, 30
KV_IN = 33
AT_IN = 40
RO_IN = 44
RES_IN = 50
FIN_IN = 52
N_RECV = 84
N_SEND = 128
N_LOCAL = 8


def kernel(
    emb, gain, wq, wk, wv, wo, blocks, out,
    WKV, WQ, WO, X, XG, PK, PKR, PQ, PQR, SQ, SQR, KV, AT, ATR, OS, OR, RES, ST,
    send_sems, recv_sems, local_sems, go,
):
    s = lax.axis_index("section")
    t = lax.axis_index("tp")
    r = lax.axis_index("rep")
    z = r // 4
    y = r % 4
    g = z // 2
    zh = z % 2
    first = s == 0
    second = s == 1
    diagonal = z == t
    apart = jnp.logical_not(diagonal)

    def dev(s_, t_, z_, y_):
        return (s_, t_, z_ * 4 + y_)

    def up(v, d):
        return (v + d) % 4

    pending = []

    def send(src, dst, ridx, device, when=None):
        c = pltpu.make_async_remote_copy(
            src_ref=src, dst_ref=dst, send_sem=send_sems.at[len(pending)],
            recv_sem=recv_sems.at[ridx], device_id=device, device_id_type=MESH,
        )
        if when is None:
            c.start()
        else:
            pl.when(when)(c.start)
        pending.append((c, when))

    def arrived(ref, ridx, when=None):
        c = pltpu.make_async_remote_copy(
            src_ref=ref, dst_ref=ref, send_sem=send_sems.at[0],
            recv_sem=recv_sems.at[ridx], device_id=dev(1 - s, t, z, y), device_id_type=MESH,
        )
        if when is None:
            c.wait_recv()
        else:
            pl.when(when)(c.wait_recv)

    def rows(start, size):
        return pl.ds(pl.multiple_of(start, size), size)

    KV[...] = jnp.zeros_like(KV)

    at_y = rows(256 * y, 256)
    kc, vc = pl.ds(0, 256), pl.ds(256, 256)
    own = [
        pltpu.make_async_copy(wk.at[0], WKV.at[at_y, kc], local_sems.at[0]),
        pltpu.make_async_copy(wv.at[0], WKV.at[at_y, vc], local_sems.at[1]),
        pltpu.make_async_copy(wq.at[0], WQ.at[at_y], local_sems.at[2]),
        pltpu.make_async_copy(wo.at[0], WO.at[rows(128 * y, 128)], local_sems.at[3]),
    ]
    for c in own:
        c.start()
    my_emb = emb.at[rows(256 * y + 64 * z, 64)]
    my_rows = rows(64 * z, 64)
    own_x = pltpu.make_async_copy(my_emb, X.at[my_rows], local_sems.at[4])
    own_res = pltpu.make_async_copy(my_emb, RES, local_sems.at[5])
    pl.when(first & diagonal)(own_x.start)
    pl.when(first)(own_res.start)

    barrier = pltpu.get_barrier_semaphore()

    def greet(device):
        pl.semaphore_signal(barrier, inc=1, device_id=device, device_id_type=MESH)

    for d in (1, 2, 3):
        greet(dev(s, t, z, up(y, d)))
        greet(dev(s, t, up(z, d), y))
        greet(dev(s, t, z + 1 - 2 * zh, up(y, d)))
        greet(dev(1 - s, t, z, up(y, d)))
        greet(dev(1 - s, t, up(z, d), y))
        greet(dev(s, up(t, d), t, y))
        greet(dev(s, z, up(z, d), y))
    greet(dev(1 - s, t, z, y))

    @pl.when(apart)
    def _():
        greet(dev(s, t, t, y))
        greet(dev(s, z, z, y))

    for d in range(4):
        @pl.when(first)
        def _():
            greet(dev(1, d, t, y))

        @pl.when(second)
        def _():
            greet(dev(0, z, d, y))
    pl.semaphore_wait(barrier, 26 + 2 * (1 - diagonal.astype(jnp.int32)))

    right, left, far = up(y, 1), up(y, 3), up(y, 2)
    dev_r, dev_l = dev(s, t, z, right), dev(s, t, z, left)
    at_l, at_r, at_f = rows(256 * left, 256), rows(256 * right, 256), rows(256 * far, 256)

    half = (pl.ds(0, 512), pl.ds(512, 512))
    for d in (2, 1, 3):
        send(my_emb, X.at[my_rows], X_IN + z, dev(0, up(t, d), t, y), first)
    send(my_emb, X.at[my_rows], X_IN + z, dev(0, t, t, y), first & apart)

    @pl.when(second)
    def _():
        pl.semaphore_wait(go, 1)

    send(wk.at[0], WKV.at[at_y, kc], KV_LEFT, dev_r)
    send(wv.at[0], WKV.at[at_y, vc], KV_RIGHT + 1, dev_l)
    send(wv.at[0], WKV.at[at_y, vc], KV_LEFT + 1, dev_r)
    send(wk.at[0], WKV.at[at_y, kc], KV_RIGHT, dev_l)
    arrived(WKV.at[at_l, kc], KV_LEFT)
    send(WKV.at[at_l, kc], WKV.at[at_l, kc], KV_FAR, dev_r)
    arrived(WKV.at[at_r, vc], KV_RIGHT + 1)
    send(WKV.at[at_r, vc], WKV.at[at_r, vc], KV_FAR + 1, dev_l)

    def q_rows(block, h):
        return rows(256 * block + 128 * h, 128)

    q_src = (wq.at[0, pl.ds(0, 128)], wq.at[0, pl.ds(128, 128)])
    send(q_src[0], WQ.at[q_rows(y, 0)], Q_LEFT, dev_r)
    send(q_src[1], WQ.at[q_rows(y, 1)], Q_RIGHT + 1, dev_l)
    send(q_src[1], WQ.at[q_rows(y, 1)], Q_LEFT + 1, dev_r)
    send(q_src[0], WQ.at[q_rows(y, 0)], Q_RIGHT, dev_l)

    def forward_q(when):
        low, high = WQ.at[q_rows(left, 0)], WQ.at[q_rows(right, 1)]
        arrived(low, Q_LEFT, when)
        send(low, low, Q_FAR, dev_r, when)
        arrived(high, Q_RIGHT + 1, when)
        send(high, high, Q_FAR + 1, dev_l, when)

    ow_y = rows(128 * y, 128)
    ow_l, ow_r = rows(128 * left, 128), rows(128 * right, 128)

    def out_part(block, h):
        return WO.at[rows(128 * block + 64 * h, 64)]

    def send_out_weights(when):
        send(wo.at[0], WO.at[ow_y], O_LEFT, dev_r, when)
        send(wo.at[0], WO.at[ow_y], O_RIGHT, dev_l, when)

    def forward_out_weights(when):
        arrived(WO.at[ow_l], O_LEFT, when)
        send(out_part(left, 0), out_part(left, 0), O_FAR, dev_r, when)
        arrived(WO.at[ow_r], O_RIGHT, when)
        send(out_part(right, 1), out_part(right, 1), O_FAR + 1, dev_l, when)

    forward_q(second)
    send_out_weights(second)
    forward_out_weights(second)

    pl.when(first & diagonal)(own_x.wait)
    for zp in range(4):
        place = pl.ds(64 * zp, 64)
        arrived(X.at[place], X_IN + zp, first & jnp.logical_not(diagonal & (z == zp)))
    for c in range(2):
        for zp in range(4):
            arrived(X.at[pl.ds(64 * zp, 64), half[c]], X_IN + 4 * c + zp, second)
    x = X[...].astype(F32)
    XG[...] = (x * gain[:, rows(1024 * z, 1024)]).astype(BF)
    squares = jnp.sum(x * x, axis=1, keepdims=True)
    for h in range(2):
        column = jnp.broadcast_to(squares[128 * h:128 * h + 128], (128, 128))
        SQ[h] = jnp.transpose(column)[0:8]
    for d in (2, 1, 3):
        other = up(z, d)
        send(SQ.at[other % 2], SQR.at[d - 1], SQ_IN + d - 1, dev(s, t, other, y))

    def multiply(block, ref):
        at = rows(256 * block, 256)
        return jnp.dot(XG[:, at], ref[at, :], preferred_element_type=F32)

    for c in own:
        c.wait()
    part = multiply(y, WKV)
    arrived(WKV.at[at_l, vc], KV_LEFT + 1)
    part = part + multiply(left, WKV)
    arrived(WKV.at[at_r, kc], KV_RIGHT)
    part = part + multiply(right, WKV)
    arrived(WKV.at[at_f, kc], KV_FAR)
    arrived(WKV.at[at_f, vc], KV_FAR + 1)
    part = part + multiply(far, WKV)
    for gg in range(2):
        for hh in range(2):
            rows_of = part[128 * hh:128 * hh + 128]
            PK[2 * gg + hh, :, 0:128] = rows_of[:, 128 * gg:128 * gg + 128].astype(BF)
            PK[2 * gg + hh, :, 128:256] = rows_of[:, 256 + 128 * gg:384 + 128 * gg].astype(BF)
    for d in (2, 1, 3):
        other = up(z, d)
        send(PK.at[other], PKR.at[d - 1], RS_IN + d - 1, dev(s, t, other, y))

    forward_q(first)
    part = multiply(y, WQ)
    arrived(WQ.at[q_rows(left, 1)], Q_LEFT + 1)
    part = part + multiply(left, WQ)
    arrived(WQ.at[q_rows(right, 0)], Q_RIGHT)
    part = part + multiply(right, WQ)
    arrived(WQ.at[q_rows(far, 0)], Q_FAR)
    arrived(WQ.at[q_rows(far, 1)], Q_FAR + 1)
    part = part + multiply(far, WQ)
    for gg in range(2):
        for hh in range(2):
            PQ[2 * gg + hh] = part[128 * hh:128 * hh + 128, 256 * gg:256 * gg + 256].astype(BF)
    for d in (2, 1, 3):
        other = up(z, d)
        send(PQ.at[other], PQR.at[d - 1], RQ_IN + d - 1, dev(s, t, other, y))

    square = SQ[zh]
    for d in (1, 3, 2):
        arrived(SQR.at[d - 1], SQ_IN + d - 1)
        square = square + SQR[d - 1]
    inverse_row = lax.rsqrt(square * (1.0 / D) + 1e-5)
    inverse = jnp.transpose(jnp.broadcast_to(inverse_row[0:1], (128, 128)))
    wide = jnp.concatenate([inverse, inverse], axis=1)
    total = PK[z].astype(F32)
    for d in (1, 3, 2):
        arrived(PKR.at[d - 1], RS_IN + d - 1)
        total = total + PKR[d - 1].astype(F32)
    block = 2 * y + zh
    KV[rows(128 * block, 128), :] = (total * wide).astype(BF)
    mine = KV.at[rows(128 * block, 128)]
    for dy in (2, 1, 3, 0):
        for dz in range(2):
            if dy + dz == 0:
                continue
            y_to = up(y, dy)
            h_to = zh if dz == 0 else 1 - zh
            send(mine, mine, KV_IN + 2 * dy + dz - 1, dev(s, t, 2 * g + h_to, y_to), 2 * y_to + h_to > block)
    send_out_weights(first)

    places = 256 * y + 128 * zh + lax.broadcasted_iota(jnp.int32, (128, 1), 0)
    starts = []
    run = jnp.int32(0)
    for c in range(GROUPS):
        starts.append(run)
        run = run + blocks[c] * UNIT
    lowest = jnp.zeros((128, 1), jnp.int32)
    for c in range(GROUPS - 2):
        lowest = jnp.where(places >= starts[c + 2], starts[c], lowest)
    keys_at = lax.broadcasted_iota(jnp.int32, (128, 1024), 1)
    allowed = (keys_at <= places) & (keys_at >= lowest)

    total = PQ[z].astype(F32)
    for d in (1, 3, 2):
        arrived(PQR.at[d - 1], RQ_IN + d - 1)
        total = total + PQR[d - 1].astype(F32)
    queries = (total * wide).astype(BF)

    for dy in (1, 3, 2, 0):
        for dz in range(2):
            if dy + dz == 0:
                continue
            y_from = up(y, 4 - dy)
            h_from = zh if dz == 0 else 1 - zh
            theirs = 2 * y_from + h_from
            arrived(KV.at[rows(128 * theirs, 128)], KV_IN + 2 * dy + dz - 1, theirs < block)

    keys = KV[:, 0:128]
    values = KV[:, 128:256]
    for h in range(2):
        scores = lax.dot_general(
            queries[:, 128 * h:128 * h + 128], keys, (((1,), (1,)), ((), ())), preferred_element_type=F32
        ) * SCALE
        scores = jnp.where(allowed, scores, -jnp.inf)
        exps = jnp.exp(scores - jnp.max(scores, axis=1, keepdims=True))
        norm = jnp.sum(exps, axis=1, keepdims=True)
        heads = jnp.dot(exps.astype(BF), values, preferred_element_type=F32) / norm
        AT[:, 128 * h:128 * h + 128] = heads.astype(BF)

    for d in (2, 1, 3):
        send(AT, ATR.at[z], AT_IN + z, dev(s, up(t, d), t, y))
    send(AT, ATR.at[z], AT_IN + z, dev(s, t, t, y), apart)

    @pl.when(diagonal)
    def _():
        ATR[z] = AT[...]

    forward_out_weights(first)

    @pl.when(first)
    def _():
        pl.semaphore_signal(go, inc=1, device_id=dev(1, t, z, y), device_id_type=MESH)

    pl.when(first)(own_res.wait)
    for c in range(2):
        arrived(RES.at[:, half[c]], RES_IN + c, second)
    arrived(out_part(far, 0), O_FAR)
    arrived(out_part(far, 1), O_FAR + 1)
    for zp in range(4):
        arrived(ATR.at[zp], AT_IN + zp, jnp.logical_not(diagonal & (z == zp)))
    for c in range(2):
        for hh in range(2):
            product = jnp.dot(ATR[hh], WO[0:256, half[c]], preferred_element_type=F32)
            product = product + jnp.dot(ATR[2 + hh], WO[256:512, half[c]], preferred_element_type=F32)
            OS[c, 2 * hh] = product[0:64].astype(BF)
            OS[c, 2 * hh + 1] = product[64:128].astype(BF)
        for d in (2, 1, 3):
            send(OS.at[c, up(z, d)], OR.at[c, d - 1], RO_IN + 3 * c + d - 1, dev(s, t, up(z, d), y))

    sec = y // 2
    cross = second & (sec == 0)

    def out_rows(z_, y_):
        return rows(256 * (y_ % 2) + 64 * z_, 64)

    at_out = out_rows(z, y)

    def fin(c, dz, dy):
        return FIN_IN + 16 * c + 4 * dz + dy

    for c in range(2):
        new = RES[:, half[c]].astype(F32) + OS[c, z].astype(F32)
        for d in (1, 3, 2):
            arrived(OR.at[c, d - 1], RO_IN + 3 * c + d - 1)
            new = new + OR[c, d - 1].astype(F32)
        ST[:, half[c]] = new.astype(BF)
        mine = ST.at[:, half[c]]
        for d in (2, 1, 3, 0):
            send(mine, X.at[my_rows, half[c]], X_IN + 4 * c + z, dev(1, up(t, d), t, y), first)
        send(mine, RES.at[:, half[c]], RES_IN + c, dev(1, t, z, y), first)
        place = out.at[at_out, half[c]]
        for d in (2, 1, 3):
            send(mine, place, fin(c, d, 0), dev(sec, t, up(z, d), y), second)
            send(mine, place, fin(c, 0, d), dev(sec, t, z, up(y, d)), second)
        send(mine, place, fin(c, 0, 0), dev(sec, t, z, y), cross)

    @pl.when(second & (sec == 1))
    def _():
        out[at_out, :] = ST[...]

    holder = sec == s
    for d in (1, 3, 2):
        place = out.at[out_rows(up(z, 4 - d), y), half[0]]
        arrived(place, fin(0, d, 0), holder)
        for e in (2, 1, 3):
            send(place, place, fin(0, d, e), dev(s, t, z, up(y, e)), holder)
        y_from = up(y, 4 - d)
        here = y_from // 2 == s
        place = out.at[out_rows(z, y_from), half[1]]
        arrived(place, fin(1, 0, d), here)
        for e in (2, 1, 3):
            send(place, place, fin(1, e, d), dev(s, t, up(z, e), y), here)
    for c in range(2):
        arrived(out.at[at_out, half[c]], fin(c, 0, 0), holder & first)
    for d in (1, 3, 2):
        y_from = up(y, 4 - d)
        arrived(out.at[out_rows(z, y_from), half[0]], fin(0, 0, d), y_from // 2 == s)
        arrived(out.at[out_rows(up(z, 4 - d), y), half[1]], fin(1, d, 0), holder)
    for e in (1, 3, 2):
        for d in (1, 3, 2):
            y_from = up(y, 4 - d)
            z_from = up(z, 4 - e)
            for c in range(2):
                arrived(out.at[out_rows(z_from, y_from), half[c]], fin(c, e, d), y_from // 2 == s)
    for c, when in pending:
        if when is None:
            c.wait_send()
        else:
            pl.when(when)(c.wait_send)


def on_device(*arrays):
    hbm = pl.BlockSpec(memory_space=pl.ANY)
    vmem = pl.BlockSpec(memory_space=pltpu.VMEM)
    return pl.pallas_call(
        kernel,
        out_shape=pltpu.VMEM((512, 1024), BF),
        in_specs=[hbm, vmem, hbm, hbm, hbm, hbm, pl.BlockSpec(memory_space=pltpu.SMEM)],
        out_specs=vmem,
        scratch_shapes=[
            pltpu.VMEM((1024, 512), BF),
            pltpu.VMEM((1024, 512), BF),
            pltpu.VMEM((512, 1024), BF),
            pltpu.VMEM((256, 1024), BF),
            pltpu.VMEM((256, 1024), BF),
            pltpu.VMEM((4, 128, 256), BF),
            pltpu.VMEM((3, 128, 256), BF),
            pltpu.VMEM((4, 128, 256), BF),
            pltpu.VMEM((3, 128, 256), BF),
            pltpu.VMEM((2, 8, 128), F32),
            pltpu.VMEM((3, 8, 128), F32),
            pltpu.VMEM((1024, 256), BF),
            pltpu.VMEM((128, 256), BF),
            pltpu.VMEM((4, 128, 256), BF),
            pltpu.VMEM((2, 4, 64, 512), BF),
            pltpu.VMEM((2, 3, 64, 512), BF),
            pltpu.VMEM((64, 1024), BF),
            pltpu.VMEM((64, 1024), BF),
            pltpu.SemaphoreType.DMA((N_SEND,)),
            pltpu.SemaphoreType.DMA((N_RECV,)),
            pltpu.SemaphoreType.DMA((N_LOCAL,)),
            pltpu.SemaphoreType.REGULAR,
        ],
        compiler_params=pltpu.CompilerParams(
            collective_id=0, has_side_effects=True, vmem_limit_bytes=56 * 1024 * 1024
        ),
    )(*arrays)


def solution(mesh):
    in_specs = (
        P(None, "tp"),
        P("section", None),
        P("section", "rep", "tp"),
        P("section", "rep", "tp"),
        P("section", "rep", "tp"),
        P("section", "rep", "tp"),
        P(),
    )
    return jax.shard_map(
        on_device, mesh=mesh, in_specs=in_specs, out_specs=P("section", "tp"), check_vma=False
    )
```

```python
import math

import jax
import jax.numpy as jnp
from jax import lax
from jax.experimental import pallas as pl
from jax.experimental.pallas import tpu as pltpu
from jax.sharding import PartitionSpec as P

MESH = pl.DeviceIdType.MESH
BF = jnp.bfloat16
F32 = jnp.float32
D = 4096
GROUPS = 8
UNIT = 16
SCALE = 1.0 / math.sqrt(128)

KV_LEFT, KV_RIGHT, KV_FAR = 0, 2, 4
Q_LEFT, Q_RIGHT, Q_FAR = 6, 8, 10
O_LEFT, O_RIGHT, O_FAR = 12, 13, 14
X_IN = 16
RS_IN, SQ_IN, RQ_IN = 24, 27, 30
KV_IN = 33
AT_IN = 40
RO_IN = 48
RES_IN = 54
FIN_IN = 56
N_RECV = 88
N_SEND = 136
N_LOCAL = 8


def kernel(
    emb, gain, wq, wk, wv, wo, blocks, out,
    WKV, WQ, WO, X, XG, PK, PKR, PQ, PQR, SQ, SQR, KV, AT, ATR, OS, OR, RES, ST, GAIN,
    send_sems, recv_sems, local_sems, go,
):
    s = lax.axis_index("section")
    t = lax.axis_index("tp")
    r = lax.axis_index("rep")
    z = r // 4
    y = r % 4
    g = z // 2
    zh = z % 2
    first = s == 0
    second = s == 1
    diagonal = z == t
    apart = jnp.logical_not(diagonal)

    def dev(s_, t_, z_, y_):
        return (s_, t_, z_ * 4 + y_)

    def up(v, d):
        return (v + d) % 4

    pending = []

    def send(src, dst, ridx, device, when=None):
        c = pltpu.make_async_remote_copy(
            src_ref=src, dst_ref=dst, send_sem=send_sems.at[len(pending)],
            recv_sem=recv_sems.at[ridx], device_id=device, device_id_type=MESH,
        )
        if when is None:
            c.start()
        else:
            pl.when(when)(c.start)
        pending.append((c, when))

    finished = [0]

    def flush(count):
        for c, when in pending[finished[0]:count]:
            if when is None:
                c.wait_send()
            else:
                pl.when(when)(c.wait_send)
        finished[0] = max(finished[0], count)

    def arrived(ref, ridx, when=None):
        c = pltpu.make_async_remote_copy(
            src_ref=ref, dst_ref=ref, send_sem=send_sems.at[0],
            recv_sem=recv_sems.at[ridx], device_id=dev(1 - s, t, z, y), device_id_type=MESH,
        )
        if when is None:
            c.wait_recv()
        else:
            pl.when(when)(c.wait_recv)

    def rows(start, size):
        return pl.ds(pl.multiple_of(start, size), size)

    KV[...] = jnp.zeros_like(KV)

    barrier = pltpu.get_barrier_semaphore()

    def greet(device):
        pl.semaphore_signal(barrier, inc=1, device_id=device, device_id_type=MESH)

    for d in (1, 2, 3):
        greet(dev(s, t, z, up(y, d)))
        greet(dev(s, t, up(z, d), y))
        greet(dev(s, t, z + 1 - 2 * zh, up(y, d)))
        greet(dev(1 - s, t, z, up(y, d)))
        greet(dev(1 - s, t, up(z, d), y))
        greet(dev(s, up(t, d), t, y))
        greet(dev(s, z, up(z, d), y))
    greet(dev(1 - s, t, z, y))

    @pl.when(apart)
    def _():
        greet(dev(s, t, t, y))
        greet(dev(s, z, z, y))

    for d in range(4):
        @pl.when(first)
        def _():
            greet(dev(1, d, t, y))

        @pl.when(second)
        def _():
            greet(dev(0, z, d, y))
    at_y = rows(256 * y, 256)
    kc, vc = pl.ds(0, 256), pl.ds(256, 256)
    own = [
        pltpu.make_async_copy(wk.at[0], WKV.at[at_y, kc], local_sems.at[0]),
        pltpu.make_async_copy(wv.at[0], WKV.at[at_y, vc], local_sems.at[1]),
        pltpu.make_async_copy(wq.at[0], WQ.at[at_y], local_sems.at[2]),
        pltpu.make_async_copy(wo.at[0], WO.at[rows(128 * y, 128)], local_sems.at[3]),
        pltpu.make_async_copy(gain, GAIN, local_sems.at[6]),
    ]
    for c in own:
        c.start()
    my_emb = emb.at[rows(256 * y + 64 * z, 64)]
    my_rows = rows(64 * z, 64)
    own_x = pltpu.make_async_copy(my_emb, X.at[my_rows], local_sems.at[4])
    own_res = pltpu.make_async_copy(my_emb, RES, local_sems.at[5])
    pl.when(first & diagonal)(own_x.start)
    pl.when(first)(own_res.start)

    pl.semaphore_wait(barrier, 26 + 2 * (1 - diagonal.astype(jnp.int32)))

    right, left, far = up(y, 1), up(y, 3), up(y, 2)
    dev_r, dev_l = dev(s, t, z, right), dev(s, t, z, left)
    at_l, at_r, at_f = rows(256 * left, 256), rows(256 * right, 256), rows(256 * far, 256)

    half = (pl.ds(0, 512), pl.ds(512, 512))
    for d in (2, 1, 3):
        send(my_emb, X.at[my_rows], X_IN + z, dev(0, up(t, d), t, y), first)
    send(my_emb, X.at[my_rows], X_IN + z, dev(0, t, t, y), first & apart)

    @pl.when(second)
    def _():
        pl.semaphore_wait(go, 1)

    send(wk.at[0], WKV.at[at_y, kc], KV_LEFT, dev_r)
    send(wv.at[0], WKV.at[at_y, vc], KV_RIGHT + 1, dev_l)
    send(wv.at[0], WKV.at[at_y, vc], KV_LEFT + 1, dev_r)
    send(wk.at[0], WKV.at[at_y, kc], KV_RIGHT, dev_l)
    arrived(WKV.at[at_l, kc], KV_LEFT)
    send(WKV.at[at_l, kc], WKV.at[at_l, kc], KV_FAR, dev_r)
    arrived(WKV.at[at_r, vc], KV_RIGHT + 1)
    send(WKV.at[at_r, vc], WKV.at[at_r, vc], KV_FAR + 1, dev_l)

    def q_rows(block, h):
        return rows(256 * block + 128 * h, 128)

    q_src = (wq.at[0, pl.ds(0, 128)], wq.at[0, pl.ds(128, 128)])
    send(q_src[0], WQ.at[q_rows(y, 0)], Q_LEFT, dev_r)
    send(q_src[1], WQ.at[q_rows(y, 1)], Q_RIGHT + 1, dev_l)
    send(q_src[1], WQ.at[q_rows(y, 1)], Q_LEFT + 1, dev_r)
    send(q_src[0], WQ.at[q_rows(y, 0)], Q_RIGHT, dev_l)

    def forward_q(when):
        low, high = WQ.at[q_rows(left, 0)], WQ.at[q_rows(right, 1)]
        arrived(low, Q_LEFT, when)
        send(low, low, Q_FAR, dev_r, when)
        arrived(high, Q_RIGHT + 1, when)
        send(high, high, Q_FAR + 1, dev_l, when)

    ow_y = rows(128 * y, 128)
    ow_l, ow_r = rows(128 * left, 128), rows(128 * right, 128)

    def out_part(block, h):
        return WO.at[rows(128 * block + 64 * h, 64)]

    def send_out_weights(when):
        send(wo.at[0], WO.at[ow_y], O_LEFT, dev_r, when)
        send(wo.at[0], WO.at[ow_y], O_RIGHT, dev_l, when)

    def forward_out_weights(when):
        arrived(WO.at[ow_l], O_LEFT, when)
        send(out_part(left, 0), out_part(left, 0), O_FAR, dev_r, when)
        arrived(WO.at[ow_r], O_RIGHT, when)
        send(out_part(right, 1), out_part(right, 1), O_FAR + 1, dev_l, when)

    forward_q(second)
    send_out_weights(second)
    forward_out_weights(second)

    pl.when(first & diagonal)(own_x.wait)
    for zp in range(4):
        place = pl.ds(64 * zp, 64)
        arrived(X.at[place], X_IN + zp, first & jnp.logical_not(diagonal & (z == zp)))
    for c in range(2):
        for zp in range(4):
            arrived(X.at[pl.ds(64 * zp, 64), half[c]], X_IN + 4 * c + zp, second)
    for c in own:
        c.wait()
    x = X[...].astype(F32)
    XG[...] = (x * GAIN[:, rows(1024 * z, 1024)]).astype(BF)
    def multiply(block, ref):
        at = rows(256 * block, 256)
        return jnp.dot(XG[:, at], ref[at, :], preferred_element_type=F32)

    part = multiply(y, WKV)
    arrived(WKV.at[at_l, vc], KV_LEFT + 1)
    part = part + multiply(left, WKV)
    arrived(WKV.at[at_r, kc], KV_RIGHT)
    part = part + multiply(right, WKV)
    arrived(WKV.at[at_f, kc], KV_FAR)
    arrived(WKV.at[at_f, vc], KV_FAR + 1)
    part = part + multiply(far, WKV)
    for gg in range(2):
        for hh in range(2):
            rows_of = part[128 * hh:128 * hh + 128]
            PK[2 * gg + hh, :, 0:128] = rows_of[:, 128 * gg:128 * gg + 128].astype(BF)
            PK[2 * gg + hh, :, 128:256] = rows_of[:, 256 + 128 * gg:384 + 128 * gg].astype(BF)
    for d in (2, 1, 3):
        other = up(z, d)
        send(PK.at[other], PKR.at[d - 1], RS_IN + d - 1, dev(s, t, other, y))

    forward_q(first)
    send_out_weights(first)
    squares = jnp.sum(x * x, axis=1, keepdims=True)
    for h in range(2):
        column = jnp.broadcast_to(squares[128 * h:128 * h + 128], (128, 128))
        SQ[h] = jnp.transpose(column)[0:8]
    for d in (2, 1, 3):
        other = up(z, d)
        send(SQ.at[other % 2], SQR.at[d - 1], SQ_IN + d - 1, dev(s, t, other, y))

    part = multiply(y, WQ)
    arrived(WQ.at[q_rows(left, 1)], Q_LEFT + 1)
    part = part + multiply(left, WQ)
    arrived(WQ.at[q_rows(right, 0)], Q_RIGHT)
    part = part + multiply(right, WQ)
    arrived(WQ.at[q_rows(far, 0)], Q_FAR)
    arrived(WQ.at[q_rows(far, 1)], Q_FAR + 1)
    part = part + multiply(far, WQ)
    for gg in range(2):
        for hh in range(2):
            PQ[2 * gg + hh] = part[128 * hh:128 * hh + 128, 256 * gg:256 * gg + 256].astype(BF)
    for d in (2, 1, 3):
        other = up(z, d)
        send(PQ.at[other], PQR.at[d - 1], RQ_IN + d - 1, dev(s, t, other, y))

    square = SQ[zh]
    for d in (1, 3, 2):
        arrived(SQR.at[d - 1], SQ_IN + d - 1)
        square = square + SQR[d - 1]
    inverse_row = lax.rsqrt(square * (1.0 / D) + 1e-5)
    inverse = jnp.transpose(jnp.broadcast_to(inverse_row[0:1], (128, 128)))
    wide = jnp.concatenate([inverse, inverse], axis=1)
    total = PK[z].astype(F32)
    for d in (1, 3, 2):
        arrived(PKR.at[d - 1], RS_IN + d - 1)
        total = total + PKR[d - 1].astype(F32)
    block = 2 * y + zh
    KV[rows(128 * block, 128), :] = (total * wide).astype(BF)
    mine = KV.at[rows(128 * block, 128)]
    for dy in (2, 1, 3, 0):
        for dz in range(2):
            if dy + dz == 0:
                continue
            y_to = up(y, dy)
            h_to = zh if dz == 0 else 1 - zh
            send(mine, mine, KV_IN + 2 * dy + dz - 1, dev(s, t, 2 * g + h_to, y_to), 2 * y_to + h_to > block)
    front = len(pending)

    places = 256 * y + 128 * zh + lax.broadcasted_iota(jnp.int32, (128, 1), 0)
    starts = []
    run = jnp.int32(0)
    for c in range(GROUPS):
        starts.append(run)
        run = run + blocks[c] * UNIT
    lowest = jnp.zeros((128, 1), jnp.int32)
    for c in range(GROUPS - 2):
        lowest = jnp.where(places >= starts[c + 2], starts[c], lowest)
    keys_at = lax.broadcasted_iota(jnp.int32, (128, 1024), 1)
    allowed = (keys_at <= places) & (keys_at >= lowest)

    forward_out_weights(first)
    total = PQ[z].astype(F32)
    for d in (1, 3, 2):
        arrived(PQR.at[d - 1], RQ_IN + d - 1)
        total = total + PQR[d - 1].astype(F32)
    queries = (total * wide).astype(BF)

    for dy in (1, 3, 2, 0):
        for dz in range(2):
            if dy + dz == 0:
                continue
            y_from = up(y, 4 - dy)
            h_from = zh if dz == 0 else 1 - zh
            theirs = 2 * y_from + h_from
            arrived(KV.at[rows(128 * theirs, 128)], KV_IN + 2 * dy + dz - 1, theirs < block)

    keys = KV[:, 0:128]
    values = KV[:, 128:256]
    for h in range(2):
        scores = lax.dot_general(
            queries[:, 128 * h:128 * h + 128], keys, (((1,), (1,)), ((), ())), preferred_element_type=F32
        ) * SCALE
        scores = jnp.where(allowed, scores, -jnp.inf)
        exps = jnp.exp(scores - jnp.max(scores, axis=1, keepdims=True))
        norm = jnp.sum(exps, axis=1, keepdims=True)
        heads = jnp.dot(exps.astype(BF), values, preferred_element_type=F32) / norm
        AT[h] = heads.astype(BF)
        for d in (2, 1, 3):
            send(AT.at[h], ATR.at[z, h], AT_IN + 4 * h + z, dev(s, up(t, d), t, y))
        send(AT.at[h], ATR.at[z, h], AT_IN + 4 * h + z, dev(s, t, t, y), apart)

    @pl.when(diagonal)
    def _():
        ATR[z] = AT[...]

    flush(front)

    @pl.when(first)
    def _():
        pl.semaphore_signal(go, inc=1, device_id=dev(1, t, z, y), device_id_type=MESH)

    pl.when(first)(own_res.wait)
    for c in range(2):
        arrived(RES.at[:, half[c]], RES_IN + c, second)
    arrived(out_part(far, 0), O_FAR)
    arrived(out_part(far, 1), O_FAR + 1)
    for zp in range(4):
        for h in range(2):
            arrived(ATR.at[zp, h], AT_IN + 4 * h + zp, jnp.logical_not(diagonal & (z == zp)))
    for c in range(2):
        for hh in range(2):
            product = jnp.zeros((128, 512), F32)
            for q in range(4):
                product = product + jnp.dot(
                    ATR[2 * (q // 2) + hh, q % 2], WO[128 * q:128 * q + 128, half[c]], preferred_element_type=F32
                )
            OS[c, 2 * hh] = product[0:64].astype(BF)
            OS[c, 2 * hh + 1] = product[64:128].astype(BF)
        for d in (2, 1, 3):
            send(OS.at[c, up(z, d)], OR.at[c, d - 1], RO_IN + 3 * c + d - 1, dev(s, t, up(z, d), y))

    summed = len(pending)

    sec = y // 2
    cross = second & (sec == 0)

    def out_rows(z_, y_):
        return rows(256 * (y_ % 2) + 64 * z_, 64)

    at_out = out_rows(z, y)

    def fin(c, dz, dy):
        return FIN_IN + 16 * c + 4 * dz + dy

    for c in range(2):
        new = RES[:, half[c]].astype(F32) + OS[c, z].astype(F32)
        for d in (1, 3, 2):
            arrived(OR.at[c, d - 1], RO_IN + 3 * c + d - 1)
            new = new + OR[c, d - 1].astype(F32)
        ST[:, half[c]] = new.astype(BF)
        mine = ST.at[:, half[c]]
        for d in (2, 1, 3, 0):
            send(mine, X.at[my_rows, half[c]], X_IN + 4 * c + z, dev(1, up(t, d), t, y), first)
        send(mine, RES.at[:, half[c]], RES_IN + c, dev(1, t, z, y), first)
        place = out.at[at_out, half[c]]
        for d in (2, 1, 3):
            if c == 0:
                send(mine, place, fin(c, d, 0), dev(sec, t, up(z, d), y), second)
            else:
                send(mine, place, fin(c, 0, d), dev(sec, t, z, up(y, d)), second)
    for c in range(2):
        mine, place = ST.at[:, half[c]], out.at[at_out, half[c]]
        for d in (2, 1, 3):
            if c == 0:
                send(mine, place, fin(c, 0, d), dev(sec, t, z, up(y, d)), second)
            else:
                send(mine, place, fin(c, d, 0), dev(sec, t, up(z, d), y), second)
        send(mine, place, fin(c, 0, 0), dev(sec, t, z, y), cross)

    @pl.when(second & (sec == 1))
    def _():
        out[at_out, :] = ST[...]

    holder = sec == s
    for d in (1, 3, 2):
        place = out.at[out_rows(up(z, 4 - d), y), half[0]]
        arrived(place, fin(0, d, 0), holder)
        for e in (2, 1, 3):
            send(place, place, fin(0, d, e), dev(s, t, z, up(y, e)), holder)
        y_from = up(y, 4 - d)
        here = y_from // 2 == s
        place = out.at[out_rows(z, y_from), half[1]]
        arrived(place, fin(1, 0, d), here)
        for e in (2, 1, 3):
            send(place, place, fin(1, e, d), dev(s, t, up(z, e), y), here)
    flush(summed)
    for c in range(2):
        arrived(out.at[at_out, half[c]], fin(c, 0, 0), holder & first)
    for d in (1, 3, 2):
        y_from = up(y, 4 - d)
        arrived(out.at[out_rows(z, y_from), half[0]], fin(0, 0, d), y_from // 2 == s)
        arrived(out.at[out_rows(up(z, 4 - d), y), half[1]], fin(1, d, 0), holder)
    for e in (1, 3, 2):
        for d in (1, 3, 2):
            y_from = up(y, 4 - d)
            z_from = up(z, 4 - e)
            for c in range(2):
                arrived(out.at[out_rows(z_from, y_from), half[c]], fin(c, e, d), y_from // 2 == s)
    flush(len(pending))


def on_device(*arrays):
    hbm = pl.BlockSpec(memory_space=pl.ANY)
    vmem = pl.BlockSpec(memory_space=pltpu.VMEM)
    return pl.pallas_call(
        kernel,
        out_shape=pltpu.VMEM((512, 1024), BF),
        in_specs=[hbm, hbm, hbm, hbm, hbm, hbm, pl.BlockSpec(memory_space=pltpu.SMEM)],
        out_specs=vmem,
        scratch_shapes=[
            pltpu.VMEM((1024, 512), BF),
            pltpu.VMEM((1024, 512), BF),
            pltpu.VMEM((512, 1024), BF),
            pltpu.VMEM((256, 1024), BF),
            pltpu.VMEM((256, 1024), BF),
            pltpu.VMEM((4, 128, 256), BF),
            pltpu.VMEM((3, 128, 256), BF),
            pltpu.VMEM((4, 128, 256), BF),
            pltpu.VMEM((3, 128, 256), BF),
            pltpu.VMEM((2, 8, 128), F32),
            pltpu.VMEM((3, 8, 128), F32),
            pltpu.VMEM((1024, 256), BF),
            pltpu.VMEM((2, 128, 128), BF),
            pltpu.VMEM((4, 2, 128, 128), BF),
            pltpu.VMEM((2, 4, 64, 512), BF),
            pltpu.VMEM((2, 3, 64, 512), BF),
            pltpu.VMEM((64, 1024), BF),
            pltpu.VMEM((64, 1024), BF),
            pltpu.VMEM((1, 4096), F32),
            pltpu.SemaphoreType.DMA((N_SEND,)),
            pltpu.SemaphoreType.DMA((N_RECV,)),
            pltpu.SemaphoreType.DMA((N_LOCAL,)),
            pltpu.SemaphoreType.REGULAR,
        ],
        compiler_params=pltpu.CompilerParams(
            collective_id=0, has_side_effects=True, vmem_limit_bytes=56 * 1024 * 1024
        ),
    )(*arrays)


def solution(mesh):
    in_specs = (
        P(None, "tp"),
        P("section", None),
        P("section", "rep", "tp"),
        P("section", "rep", "tp"),
        P("section", "rep", "tp"),
        P("section", "rep", "tp"),
        P(),
    )
    return jax.shard_map(
        on_device, mesh=mesh, in_specs=in_specs, out_specs=P("section", "tp"), check_vma=False
    )
```

```python
import math

import jax
import jax.numpy as jnp
from jax import lax
from jax.experimental import pallas as pl
from jax.experimental.pallas import tpu as pltpu
from jax.sharding import PartitionSpec as P

MESH = pl.DeviceIdType.MESH
BF = jnp.bfloat16
F32 = jnp.float32
D = 4096
GROUPS = 8
UNIT = 16
SCALE = math.log2(math.e) / math.sqrt(128)

KV_LEFT, KV_RIGHT, KV_FAR = 0, 2, 4
Q_LEFT, Q_RIGHT, Q_FAR = 6, 8, 10
O_LEFT, O_RIGHT, O_FAR = 12, 13, 14
X_IN = 16
RS_IN, SQ_IN, RQ_IN = 24, 27, 30
KV_IN = 33
AT_IN = 40
RO_IN = 48
RES_IN = 54
FZ_IN, FY_IN, REST_IN = 55, 58, 61
N_RECV = 62
N_SEND = 104
N_LOCAL = 8


def kernel(
    emb, gain, wq, wk, wv, wo, blocks, out,
    WKV, WQ, WO, X, XG, ACC, PK, PKR, PQ, PQR, SQ, SQR, KV, AT, ATR, OS, OR, RES, ST, GAIN,
    send_sems, recv_sems, local_sems, go,
):
    s = lax.axis_index("section")
    t = lax.axis_index("tp")
    r = lax.axis_index("rep")
    z = r // 4
    y = r % 4
    g = z // 2
    zh = z % 2
    first = s == 0
    second = s == 1
    diagonal = z == t
    apart = jnp.logical_not(diagonal)

    def dev(s_, t_, z_, y_):
        return (s_, t_, z_ * 4 + y_)

    def up(v, d):
        return (v + d) % 4

    pending = []

    def send(src, dst, ridx, device, when=None, group=None):
        c = pltpu.make_async_remote_copy(
            src_ref=src, dst_ref=dst,
            send_sem=send_sems.at[len(pending) if group is None else N_SEND - 1 - group],
            recv_sem=recv_sems.at[ridx], device_id=device, device_id_type=MESH,
        )
        if when is None:
            c.start()
        else:
            pl.when(when)(c.start)
        if group is None:
            pending.append((c, when))

    finished = [0]

    def flush(count):
        for c, when in pending[finished[0]:count]:
            if when is None:
                c.wait_send()
            else:
                pl.when(when)(c.wait_send)
        finished[0] = max(finished[0], count)

    def arrived(ref, ridx, when=None):
        c = pltpu.make_async_remote_copy(
            src_ref=ref, dst_ref=ref, send_sem=send_sems.at[0],
            recv_sem=recv_sems.at[ridx], device_id=dev(1 - s, t, z, y), device_id_type=MESH,
        )
        if when is None:
            c.wait_recv()
        else:
            pl.when(when)(c.wait_recv)

    def sent(ref, group, when):
        c = pltpu.make_async_remote_copy(
            src_ref=ref, dst_ref=ref, send_sem=send_sems.at[N_SEND - 1 - group],
            recv_sem=recv_sems.at[0], device_id=dev(1 - s, t, z, y), device_id_type=MESH,
        )
        pl.when(when)(c.wait_send)

    def rows(start, size):
        return pl.ds(pl.multiple_of(start, size), size)

    KV[:, 128:256] = jnp.zeros((1024, 128), BF)

    barrier = pltpu.get_barrier_semaphore()

    def greet(device):
        pl.semaphore_signal(barrier, inc=1, device_id=device, device_id_type=MESH)

    for d in range(4):
        @pl.when(first)
        def _():
            greet(dev(1, d, t, y))

        @pl.when(second)
        def _():
            greet(dev(0, z, d, y))
    for d in (2, 1, 3):
        greet(dev(s, up(t, d), t, y))
        greet(dev(s, z, up(z, d), y))

    @pl.when(apart)
    def _():
        greet(dev(s, t, t, y))
        greet(dev(s, z, z, y))
    for d in (2, 1, 3):
        greet(dev(s, t, z + 1 - 2 * zh, up(y, d)))
        greet(dev(s, t, z, up(y, d)))
        greet(dev(s, t, up(z, d), y))
        greet(dev(1 - s, t, z, up(y, d)))
        greet(dev(1 - s, t, up(z, d), y))
    greet(dev(1 - s, t, z, y))

    at_y = rows(256 * y, 256)
    kc, vc = pl.ds(0, 256), pl.ds(256, 256)
    own = [
        pltpu.make_async_copy(wk.at[0], WKV.at[at_y, kc], local_sems.at[0]),
        pltpu.make_async_copy(wv.at[0], WKV.at[at_y, vc], local_sems.at[1]),
        pltpu.make_async_copy(wq.at[0], WQ.at[at_y], local_sems.at[2]),
        pltpu.make_async_copy(wo.at[0], WO.at[rows(128 * y, 128)], local_sems.at[3]),
        pltpu.make_async_copy(gain, GAIN, local_sems.at[6]),
    ]
    for c in own:
        c.start()
    my_emb = emb.at[rows(256 * y + 64 * z, 64)]
    my_rows = rows(64 * z, 64)
    own_x = pltpu.make_async_copy(my_emb, X.at[my_rows], local_sems.at[4])
    own_res = pltpu.make_async_copy(my_emb, RES, local_sems.at[5])
    pl.when(first & diagonal)(own_x.start)
    pl.when(first)(own_res.start)

    pl.semaphore_wait(barrier, 26 + 2 * (1 - diagonal.astype(jnp.int32)))

    right, left, far = up(y, 1), up(y, 3), up(y, 2)
    dev_r, dev_l = dev(s, t, z, right), dev(s, t, z, left)
    at_l, at_r, at_f = rows(256 * left, 256), rows(256 * right, 256), rows(256 * far, 256)

    @pl.when(second)
    def _():
        pl.semaphore_wait(go, 1)

    send(wk.at[0], WKV.at[at_y, kc], KV_LEFT, dev_r)
    send(wv.at[0], WKV.at[at_y, vc], KV_RIGHT + 1, dev_l)

    half = (pl.ds(0, 512), pl.ds(512, 512))
    for d in (2, 1, 3):
        send(my_emb, X.at[my_rows], X_IN + z, dev(0, up(t, d), t, y), first)
    send(my_emb, X.at[my_rows], X_IN + z, dev(0, t, t, y), first & apart)

    send(wv.at[0], WKV.at[at_y, vc], KV_LEFT + 1, dev_r)
    send(wk.at[0], WKV.at[at_y, kc], KV_RIGHT, dev_l)
    arrived(WKV.at[at_l, kc], KV_LEFT)
    send(WKV.at[at_l, kc], WKV.at[at_l, kc], KV_FAR, dev_r)
    arrived(WKV.at[at_r, vc], KV_RIGHT + 1)
    send(WKV.at[at_r, vc], WKV.at[at_r, vc], KV_FAR + 1, dev_l)

    def q_rows(block, h):
        return rows(256 * block + 128 * h, 128)

    q_src = (wq.at[0, pl.ds(0, 128)], wq.at[0, pl.ds(128, 128)])
    send(q_src[0], WQ.at[q_rows(y, 0)], Q_LEFT, dev_r)
    send(q_src[1], WQ.at[q_rows(y, 1)], Q_RIGHT + 1, dev_l)
    send(q_src[1], WQ.at[q_rows(y, 1)], Q_LEFT + 1, dev_r)
    send(q_src[0], WQ.at[q_rows(y, 0)], Q_RIGHT, dev_l)

    def forward_q(when):
        low, high = WQ.at[q_rows(left, 0)], WQ.at[q_rows(right, 1)]
        arrived(low, Q_LEFT, when)
        send(low, low, Q_FAR, dev_r, when)
        arrived(high, Q_RIGHT + 1, when)
        send(high, high, Q_FAR + 1, dev_l, when)

    ow_y = rows(128 * y, 128)
    ow_l, ow_r = rows(128 * left, 128), rows(128 * right, 128)

    def out_part(block, h):
        return WO.at[rows(128 * block + 64 * h, 64)]

    def send_out_weights(when):
        send(wo.at[0], WO.at[ow_y], O_LEFT, dev_r, when)
        send(wo.at[0], WO.at[ow_y], O_RIGHT, dev_l, when)

    def forward_out_weights(when):
        arrived(WO.at[ow_l], O_LEFT, when)
        send(out_part(left, 0), out_part(left, 0), O_FAR, dev_r, when)
        arrived(WO.at[ow_r], O_RIGHT, when)
        send(out_part(right, 1), out_part(right, 1), O_FAR + 1, dev_l, when)

    forward_q(second)
    send_out_weights(second)

    def multiply(block, ref):
        at = rows(256 * block, 256)
        return jnp.dot(XG[:, at], ref[at, :], preferred_element_type=F32)

    for c in own:
        c.wait()

    @pl.when(first)
    def _():
        pl.when(diagonal)(own_x.wait)
        for zp in range(4):
            arrived(X.at[pl.ds(64 * zp, 64)], X_IN + zp, jnp.logical_not(diagonal & (z == zp)))
        XG[...] = (X[...].astype(F32) * GAIN[:, rows(1024 * z, 1024)]).astype(BF)
        part = multiply(y, WKV)
        arrived(WKV.at[at_l, vc], KV_LEFT + 1)
        part = part + multiply(left, WKV)
        arrived(WKV.at[at_r, kc], KV_RIGHT)
        part = part + multiply(right, WKV)
        arrived(WKV.at[at_f, kc], KV_FAR)
        arrived(WKV.at[at_f, vc], KV_FAR + 1)
        ACC[...] = part + multiply(far, WKV)

    @pl.when(second)
    def _():
        arrived(WKV.at[at_l, vc], KV_LEFT + 1)
        arrived(WKV.at[at_r, kc], KV_RIGHT)
        arrived(WKV.at[at_f, kc], KV_FAR)
        arrived(WKV.at[at_f, vc], KV_FAR + 1)
        for c in range(2):
            for zp in range(4):
                arrived(X.at[pl.ds(64 * zp, 64), half[c]], X_IN + 4 * c + zp)
            scale = GAIN[:, rows(1024 * z + 512 * c, 512)]
            XG[:, half[c]] = (X[:, half[c]].astype(F32) * scale).astype(BF)
            part = jnp.dot(XG[:, half[c]], WKV[512 * c:512 * c + 512, :], preferred_element_type=F32)
            ACC[...] = part + ACC[...] if c else part

    for gg in range(2):
        for hh in range(2):
            rows_of = ACC[128 * hh:128 * hh + 128, :]
            PK[2 * gg + hh, :, 0:128] = rows_of[:, 128 * gg:128 * gg + 128].astype(BF)
            PK[2 * gg + hh, :, 128:256] = rows_of[:, 256 + 128 * gg:384 + 128 * gg].astype(BF)
    for d in (2, 1, 3):
        other = up(z, d)
        send(PK.at[other], PKR.at[d - 1], RS_IN + d - 1, dev(s, t, other, y))

    forward_q(first)
    send_out_weights(first)
    forward_out_weights(second)
    x = X[...].astype(F32)
    squares = jnp.sum(x * x, axis=1, keepdims=True)
    for h in range(2):
        column = jnp.broadcast_to(squares[128 * h:128 * h + 128], (128, 128))
        SQ[h] = jnp.transpose(column)[0:8]
    for d in (2, 1, 3):
        other = up(z, d)
        send(SQ.at[other % 2], SQR.at[d - 1], SQ_IN + d - 1, dev(s, t, other, y))

    part = multiply(y, WQ)
    arrived(WQ.at[q_rows(left, 1)], Q_LEFT + 1)
    part = part + multiply(left, WQ)
    arrived(WQ.at[q_rows(right, 0)], Q_RIGHT)
    part = part + multiply(right, WQ)
    arrived(WQ.at[q_rows(far, 0)], Q_FAR)
    arrived(WQ.at[q_rows(far, 1)], Q_FAR + 1)
    part = part + multiply(far, WQ)
    for gg in range(2):
        for hh in range(2):
            PQ[2 * gg + hh] = part[128 * hh:128 * hh + 128, 256 * gg:256 * gg + 256].astype(BF)
    for d in (2, 1, 3):
        other = up(z, d)
        send(PQ.at[other], PQR.at[d - 1], RQ_IN + d - 1, dev(s, t, other, y))

    square = SQ[zh]
    for d in (1, 3, 2):
        arrived(SQR.at[d - 1], SQ_IN + d - 1)
        square = square + SQR[d - 1]
    inverse_row = lax.rsqrt(square * (1.0 / D) + 1e-5)
    inverse = jnp.transpose(jnp.broadcast_to(inverse_row[0:1], (128, 128)))
    wide = jnp.concatenate([inverse, inverse], axis=1)
    total = PK[z].astype(F32)
    for d in (1, 3, 2):
        arrived(PKR.at[d - 1], RS_IN + d - 1)
        total = total + PKR[d - 1].astype(F32)
    block = 2 * y + zh
    KV[rows(128 * block, 128), :] = (total * wide).astype(BF)
    mine = KV.at[rows(128 * block, 128)]
    for dy in (2, 1, 3, 0):
        for dz in range(2):
            if dy + dz == 0:
                continue
            y_to = up(y, dy)
            h_to = zh if dz == 0 else 1 - zh
            send(mine, mine, KV_IN + 2 * dy + dz - 1, dev(s, t, 2 * g + h_to, y_to), 2 * y_to + h_to > block)
    front = len(pending)

    places = 256 * y + 128 * zh + lax.broadcasted_iota(jnp.int32, (128, 1), 0)
    starts = []
    run = jnp.int32(0)
    for c in range(GROUPS):
        starts.append(run)
        run = run + blocks[c] * UNIT
    lowest = jnp.zeros((128, 1), jnp.int32)
    for c in range(GROUPS - 2):
        lowest = jnp.where(places >= starts[c + 2], starts[c], lowest)
    keys_at = lax.broadcasted_iota(jnp.int32, (128, 1024), 1)
    allowed = (keys_at <= places) & (keys_at >= lowest)

    forward_out_weights(first)
    total = PQ[z].astype(F32)
    for d in (1, 3, 2):
        arrived(PQR.at[d - 1], RQ_IN + d - 1)
        total = total + PQR[d - 1].astype(F32)
    queries = (total * (wide * SCALE)).astype(BF)

    for dy in (1, 3, 2, 0):
        for dz in range(2):
            if dy + dz == 0:
                continue
            y_from = up(y, 4 - dy)
            h_from = zh if dz == 0 else 1 - zh
            theirs = 2 * y_from + h_from
            arrived(KV.at[rows(128 * theirs, 128)], KV_IN + 2 * dy + dz - 1, theirs < block)

    lanes = (pl.ds(0, 128), pl.ds(128, 128))
    keys = KV[:, 0:128]
    values = KV[:, 128:256]
    for h in range(2):
        scores = lax.dot_general(
            queries[:, 128 * h:128 * h + 128], keys, (((1,), (1,)), ((), ())), preferred_element_type=F32
        )
        scores = jnp.where(allowed, scores, -jnp.inf)
        exps = jnp.exp2(scores - jnp.max(scores, axis=1, keepdims=True))
        norm = jnp.sum(exps, axis=1, keepdims=True)
        heads = jnp.dot(exps.astype(BF), values, preferred_element_type=F32) / norm
        AT[h] = heads.astype(BF)
        for d in (2, 1, 3):
            send(AT.at[h], ATR.at[z, :, lanes[h]], AT_IN + 4 * h + z, dev(s, up(t, d), t, y))
        send(AT.at[h], ATR.at[z, :, lanes[h]], AT_IN + 4 * h + z, dev(s, t, t, y), apart)

    @pl.when(diagonal)
    def _():
        for h in range(2):
            ATR[z, :, lanes[h]] = AT[h]

    flush(front)

    @pl.when(first)
    def _():
        pl.semaphore_signal(go, inc=1, device_id=dev(1, t, z, y), device_id_type=MESH)

    pl.when(first)(own_res.wait)
    arrived(RES, RES_IN, second)
    arrived(out_part(far, 0), O_FAR)
    arrived(out_part(far, 1), O_FAR + 1)
    for zp in range(4):
        for h in range(2):
            arrived(ATR.at[zp, :, lanes[h]], AT_IN + 4 * h + zp, jnp.logical_not(diagonal & (z == zp)))
    for c in range(2):
        for hh in range(2):
            product = jnp.dot(ATR[hh], WO[0:256, half[c]], preferred_element_type=F32)
            product = product + jnp.dot(ATR[2 + hh], WO[256:512, half[c]], preferred_element_type=F32)
            OS[c, 2 * hh] = product[0:64].astype(BF)
            OS[c, 2 * hh + 1] = product[64:128].astype(BF)
        for d in (2, 1, 3):
            send(OS.at[c, up(z, d)], OR.at[c, d - 1], RO_IN + 3 * c + d - 1, dev(s, t, up(z, d), y))

    summed = len(pending)

    sec = y // 2
    cross = second & (sec == 0)

    def out_rows(z_, y_):
        return rows(256 * (y_ % 2) + 64 * z_, 64)

    at_out = out_rows(z, y)

    for c in range(2):
        new = RES[:, half[c]].astype(F32) + OS[c, z].astype(F32)
        for d in (1, 3, 2):
            arrived(OR.at[c, d - 1], RO_IN + 3 * c + d - 1)
            new = new + OR[c, d - 1].astype(F32)
        ST[:, half[c]] = new.astype(BF)
        mine = ST.at[:, half[c]]
        for d in (2, 1, 3, 0):
            send(mine, X.at[my_rows, half[c]], X_IN + 4 * c + z, dev(1, up(t, d), t, y), first)
        place = out.at[at_out, half[c]]
        for d in (2, 1, 3):
            if c == 0:
                send(mine, place, FZ_IN + d - 1, dev(sec, t, up(z, d), y), second, 0)
            else:
                send(mine, place, FY_IN + d - 1, dev(sec, t, z, up(y, d)), second, 0)
    for c in range(2):
        mine, place = ST.at[:, half[c]], out.at[at_out, half[c]]
        for d in (2, 1, 3):
            if c == 0:
                send(mine, place, REST_IN, dev(sec, t, z, up(y, d)), second, 0)
            else:
                send(mine, place, REST_IN, dev(sec, t, up(z, d), y), second, 0)
    send(ST, out.at[at_out], REST_IN, dev(sec, t, z, y), cross, 1)
    send(ST, RES, RES_IN, dev(1, t, z, y), first)

    @pl.when(second & (sec == 1))
    def _():
        out[at_out, :] = ST[...]

    holder = sec == s
    for d in (1, 3, 2):
        place = out.at[out_rows(up(z, 4 - d), y), half[0]]
        arrived(place, FZ_IN + d - 1, holder)
        for e in (2, 1, 3):
            send(place, place, REST_IN, dev(s, t, z, up(y, e)), holder, 2)
        y_from = up(y, 4 - d)
        here = y_from // 2 == s
        place = out.at[out_rows(z, y_from), half[1]]
        arrived(place, FY_IN + d - 1, here)
        for e in (2, 1, 3):
            send(place, place, REST_IN, dev(s, t, up(z, e), y), here, 2)
    flush(len(pending))
    sent(out.at[0:384], 0, second)
    sent(out.at[0:64], 1, cross)
    guest = jnp.logical_not(holder)
    arrived(out.at[0:320], REST_IN, holder & second)
    arrived(out.at[0:384], REST_IN, holder & first)
    arrived(out.at[0:448], REST_IN, guest)
    sent(out.at[0:384], 2, holder)
    sent(out.at[0:192], 2, guest)


def on_device(*arrays):
    hbm = pl.BlockSpec(memory_space=pl.ANY)
    vmem = pl.BlockSpec(memory_space=pltpu.VMEM)
    return pl.pallas_call(
        kernel,
        out_shape=pltpu.VMEM((512, 1024), BF),
        in_specs=[hbm, hbm, hbm, hbm, hbm, hbm, pl.BlockSpec(memory_space=pltpu.SMEM)],
        out_specs=vmem,
        scratch_shapes=[
            pltpu.VMEM((1024, 512), BF),
            pltpu.VMEM((1024, 512), BF),
            pltpu.VMEM((512, 1024), BF),
            pltpu.VMEM((256, 1024), BF),
            pltpu.VMEM((256, 1024), BF),
            pltpu.VMEM((256, 512), F32),
            pltpu.VMEM((4, 128, 256), BF),
            pltpu.VMEM((3, 128, 256), BF),
            pltpu.VMEM((4, 128, 256), BF),
            pltpu.VMEM((3, 128, 256), BF),
            pltpu.VMEM((2, 8, 128), F32),
            pltpu.VMEM((3, 8, 128), F32),
            pltpu.VMEM((1024, 256), BF),
            pltpu.VMEM((2, 128, 128), BF),
            pltpu.VMEM((4, 128, 256), BF),
            pltpu.VMEM((2, 4, 64, 512), BF),
            pltpu.VMEM((2, 3, 64, 512), BF),
            pltpu.VMEM((64, 1024), BF),
            pltpu.VMEM((64, 1024), BF),
            pltpu.VMEM((1, 4096), F32),
            pltpu.SemaphoreType.DMA((N_SEND,)),
            pltpu.SemaphoreType.DMA((N_RECV,)),
            pltpu.SemaphoreType.DMA((N_LOCAL,)),
            pltpu.SemaphoreType.REGULAR,
        ],
        compiler_params=pltpu.CompilerParams(
            collective_id=0, has_side_effects=True, vmem_limit_bytes=56 * 1024 * 1024
        ),
    )(*arrays)


def solution(mesh):
    in_specs = (
        P(None, "tp"),
        P("section", None),
        P("section", "rep", "tp"),
        P("section", "rep", "tp"),
        P("section", "rep", "tp"),
        P("section", "rep", "tp"),
        P(),
    )
    return jax.shard_map(
        on_device, mesh=mesh, in_specs=in_specs, out_specs=P("section", "tp"), check_vma=False
    )
```

```python
import math

import jax
import jax.numpy as jnp
from jax import lax
from jax.experimental import pallas as pl
from jax.experimental.pallas import tpu as pltpu
from jax.sharding import PartitionSpec as P

MESH = pl.DeviceIdType.MESH
BF = jnp.bfloat16
F32 = jnp.float32
D = 4096
GROUPS = 8
UNIT = 16
SCALE = math.log2(math.e) / math.sqrt(128)

KV_LEFT, KV_RIGHT, KV_FAR = 0, 2, 4
Q_LEFT, Q_RIGHT, Q_FAR = 6, 8, 10
O_LEFT, O_RIGHT, O_FAR = 12, 13, 14
X_IN = 77
RS_IN, SQ_IN, RQ_IN = 24, 27, 30
KV_IN = (33, 70)
AT_IN = 40
RO_IN = 93
RES_IN = 54
FZ_IN, FY_IN, REST_IN = 55, 58, 61
FINE = 62
N_RECV = 105
N_SEND = 136
N_LOCAL = 8


def kernel(
    emb, gain, wq, wk, wv, wo, blocks, out,
    WKV, WQ, WO, X, XG, ACC, PK, PKR, PQ, PQR, SQ, SQR, KV, AT, ATR, OS, OR, RES, ST, GAIN,
    send_sems, recv_sems, local_sems, go,
):
    s = lax.axis_index("section")
    t = lax.axis_index("tp")
    r = lax.axis_index("rep")
    z = r // 4
    y = r % 4
    g = z // 2
    zh = z % 2
    first = s == 0
    second = s == 1
    diagonal = z == t
    apart = jnp.logical_not(diagonal)

    def dev(s_, t_, z_, y_):
        return (s_, t_, z_ * 4 + y_)

    def up(v, d):
        return (v + d) % 4

    pending = []

    def send(src, dst, ridx, device, when=None, group=None):
        c = pltpu.make_async_remote_copy(
            src_ref=src, dst_ref=dst,
            send_sem=send_sems.at[len(pending) if group is None else N_SEND - 1 - group],
            recv_sem=recv_sems.at[ridx], device_id=device, device_id_type=MESH,
        )
        if when is None:
            c.start()
        else:
            pl.when(when)(c.start)
        if group is None:
            pending.append((c, when))

    finished = [0]

    def flush(count):
        for c, when in pending[finished[0]:count]:
            if when is None:
                c.wait_send()
            else:
                pl.when(when)(c.wait_send)
        finished[0] = max(finished[0], count)

    def arrived(ref, ridx, when=None):
        c = pltpu.make_async_remote_copy(
            src_ref=ref, dst_ref=ref, send_sem=send_sems.at[0],
            recv_sem=recv_sems.at[ridx], device_id=dev(1 - s, t, z, y), device_id_type=MESH,
        )
        if when is None:
            c.wait_recv()
        else:
            pl.when(when)(c.wait_recv)

    def sent(ref, group, when):
        c = pltpu.make_async_remote_copy(
            src_ref=ref, dst_ref=ref, send_sem=send_sems.at[N_SEND - 1 - group],
            recv_sem=recv_sems.at[0], device_id=dev(1 - s, t, z, y), device_id_type=MESH,
        )
        pl.when(when)(c.wait_send)

    def rows(start, size):
        return pl.ds(pl.multiple_of(start, size), size)

    KV[:, 128:256] = jnp.zeros((1024, 128), BF)

    barrier = pltpu.get_barrier_semaphore()

    def greet(device):
        pl.semaphore_signal(barrier, inc=1, device_id=device, device_id_type=MESH)

    for d in range(4):
        @pl.when(first)
        def _():
            greet(dev(1, d, t, y))

        @pl.when(second)
        def _():
            greet(dev(0, z, d, y))
    for d in (2, 1, 3):
        greet(dev(s, up(t, d), t, y))
        greet(dev(s, z, up(z, d), y))

    @pl.when(apart)
    def _():
        greet(dev(s, t, t, y))
        greet(dev(s, z, z, y))
    for d in (2, 1, 3):
        greet(dev(s, t, z + 1 - 2 * zh, up(y, d)))
        greet(dev(s, t, z, up(y, d)))
        greet(dev(s, t, up(z, d), y))
        greet(dev(1 - s, t, z, up(y, d)))
        greet(dev(1 - s, t, up(z, d), y))
    greet(dev(1 - s, t, z, y))

    at_y = rows(256 * y, 256)
    kc, vc = pl.ds(0, 256), pl.ds(256, 256)
    own = [
        pltpu.make_async_copy(wk.at[0], WKV.at[at_y, kc], local_sems.at[0]),
        pltpu.make_async_copy(wv.at[0], WKV.at[at_y, vc], local_sems.at[1]),
        pltpu.make_async_copy(wq.at[0], WQ.at[at_y], local_sems.at[2]),
        pltpu.make_async_copy(wo.at[0], WO.at[rows(128 * y, 128)], local_sems.at[3]),
        pltpu.make_async_copy(gain, GAIN, local_sems.at[6]),
    ]
    for c in own:
        c.start()
    my_emb = emb.at[rows(256 * y + 64 * z, 64)]
    my_rows = rows(64 * z, 64)
    own_x = pltpu.make_async_copy(my_emb, X.at[my_rows], local_sems.at[4])
    own_res = pltpu.make_async_copy(my_emb, RES, local_sems.at[5])
    pl.when(first & diagonal)(own_x.start)
    pl.when(first)(own_res.start)

    pl.semaphore_wait(barrier, 26 + 2 * (1 - diagonal.astype(jnp.int32)))

    right, left, far = up(y, 1), up(y, 3), up(y, 2)
    dev_r, dev_l = dev(s, t, z, right), dev(s, t, z, left)
    at_l, at_r, at_f = rows(256 * left, 256), rows(256 * right, 256), rows(256 * far, 256)

    @pl.when(second)
    def _():
        pl.semaphore_wait(go, 1)

    def kv_part(block, h, c):
        return WKV.at[rows(256 * block + 128 * h, 128), c]

    for h in range(2):
        send(wk.at[0, pl.ds(128 * h, 128)], kv_part(y, h, kc), FINE + h, dev_r)
        send(wv.at[0, pl.ds(128 * h, 128)], kv_part(y, h, vc), FINE + 2 + h, dev_l)

    half = (pl.ds(0, 512), pl.ds(512, 512))
    quarter = [pl.ds(256 * c, 256) for c in range(4)]
    for d in (2, 1, 3):
        send(my_emb, X.at[my_rows], X_IN + z, dev(0, up(t, d), t, y), first)
    send(my_emb, X.at[my_rows], X_IN + z, dev(0, t, t, y), first & apart)

    send(wv.at[0], WKV.at[at_y, vc], KV_LEFT + 1, dev_r)
    send(wk.at[0], WKV.at[at_y, kc], KV_RIGHT, dev_l)
    for h in range(2):
        part = kv_part(left, h, kc)
        arrived(part, FINE + h)
        send(part, part, FINE + 4 + h, dev_r)
        part = kv_part(right, h, vc)
        arrived(part, FINE + 2 + h)
        send(part, part, FINE + 6 + h, dev_l)

    def q_rows(block, h):
        return rows(256 * block + 128 * h, 128)

    q_src = (wq.at[0, pl.ds(0, 128)], wq.at[0, pl.ds(128, 128)])
    send(q_src[0], WQ.at[q_rows(y, 0)], Q_LEFT, dev_r)
    send(q_src[1], WQ.at[q_rows(y, 1)], Q_RIGHT + 1, dev_l)
    send(q_src[1], WQ.at[q_rows(y, 1)], Q_LEFT + 1, dev_r)
    send(q_src[0], WQ.at[q_rows(y, 0)], Q_RIGHT, dev_l)

    def forward_q(when):
        low, high = WQ.at[q_rows(left, 0)], WQ.at[q_rows(right, 1)]
        arrived(low, Q_LEFT, when)
        send(low, low, Q_FAR, dev_r, when)
        arrived(high, Q_RIGHT + 1, when)
        send(high, high, Q_FAR + 1, dev_l, when)

    ow_y = rows(128 * y, 128)
    ow_l, ow_r = rows(128 * left, 128), rows(128 * right, 128)

    def out_part(block, h):
        return WO.at[rows(128 * block + 64 * h, 64)]

    def send_out_weights(when):
        send(wo.at[0], WO.at[ow_y], O_LEFT, dev_r, when)
        send(wo.at[0], WO.at[ow_y], O_RIGHT, dev_l, when)

    def forward_out_weights(when):
        arrived(WO.at[ow_l], O_LEFT, when)
        send(out_part(left, 0), out_part(left, 0), O_FAR, dev_r, when)
        arrived(WO.at[ow_r], O_RIGHT, when)
        send(out_part(right, 1), out_part(right, 1), O_FAR + 1, dev_l, when)

    forward_q(second)
    send_out_weights(second)

    def multiply(block, ref):
        at = rows(256 * block, 256)
        return jnp.dot(XG[:, at], ref[at, :], preferred_element_type=F32)

    for c in own:
        c.wait()

    @pl.when(first)
    def _():
        pl.when(diagonal)(own_x.wait)
        for zp in range(4):
            arrived(X.at[pl.ds(64 * zp, 64)], X_IN + zp, jnp.logical_not(diagonal & (z == zp)))
        XG[...] = (X[...].astype(F32) * GAIN[:, rows(1024 * z, 1024)]).astype(BF)
        part = multiply(y, WKV)
        arrived(WKV.at[at_l, vc], KV_LEFT + 1)
        part = part + multiply(left, WKV)
        arrived(WKV.at[at_r, kc], KV_RIGHT)
        part = part + multiply(right, WKV)
        for h in range(2):
            arrived(kv_part(far, h, kc), FINE + 4 + h)
            arrived(kv_part(far, h, vc), FINE + 6 + h)
        ACC[...] = part + multiply(far, WKV)

    @pl.when(second)
    def _():
        arrived(WKV.at[at_l, vc], KV_LEFT + 1)
        arrived(WKV.at[at_r, kc], KV_RIGHT)
        for h in range(2):
            arrived(kv_part(far, h, kc), FINE + 4 + h)
            arrived(kv_part(far, h, vc), FINE + 6 + h)
        for c in range(4):
            for zp in range(4):
                arrived(X.at[pl.ds(64 * zp, 64), quarter[c]], X_IN + 4 * c + zp)
            scale = GAIN[:, rows(1024 * z + 256 * c, 256)]
            XG[:, quarter[c]] = (X[:, quarter[c]].astype(F32) * scale).astype(BF)
            part = jnp.dot(XG[:, quarter[c]], WKV[quarter[c], :], preferred_element_type=F32)
            ACC[...] = part + ACC[...] if c else part

    for gg in range(2):
        for hh in range(2):
            rows_of = ACC[128 * hh:128 * hh + 128, :]
            PK[2 * gg + hh, :, 0:128] = rows_of[:, 128 * gg:128 * gg + 128].astype(BF)
            PK[2 * gg + hh, :, 128:256] = rows_of[:, 256 + 128 * gg:384 + 128 * gg].astype(BF)
    for d in (2, 1, 3):
        other = up(z, d)
        send(PK.at[other], PKR.at[d - 1], RS_IN + d - 1, dev(s, t, other, y))

    forward_q(first)
    send_out_weights(first)
    forward_out_weights(second)
    x = X[...].astype(F32)
    squares = jnp.sum(x * x, axis=1, keepdims=True)
    for h in range(2):
        column = jnp.broadcast_to(squares[128 * h:128 * h + 128], (128, 128))
        SQ[h] = jnp.transpose(column)[0:8]
    for d in (2, 1, 3):
        other = up(z, d)
        send(SQ.at[other % 2], SQR.at[d - 1], SQ_IN + d - 1, dev(s, t, other, y))

    part = multiply(y, WQ)
    arrived(WQ.at[q_rows(left, 1)], Q_LEFT + 1)
    part = part + multiply(left, WQ)
    arrived(WQ.at[q_rows(right, 0)], Q_RIGHT)
    part = part + multiply(right, WQ)
    arrived(WQ.at[q_rows(far, 0)], Q_FAR)
    arrived(WQ.at[q_rows(far, 1)], Q_FAR + 1)
    part = part + multiply(far, WQ)
    for gg in range(2):
        for hh in range(2):
            PQ[2 * gg + hh] = part[128 * hh:128 * hh + 128, 256 * gg:256 * gg + 256].astype(BF)
    for d in (2, 1, 3):
        other = up(z, d)
        send(PQ.at[other], PQR.at[d - 1], RQ_IN + d - 1, dev(s, t, other, y))

    square = SQ[zh]
    for d in (1, 3, 2):
        arrived(SQR.at[d - 1], SQ_IN + d - 1)
        square = square + SQR[d - 1]
    inverse_row = lax.rsqrt(square * (1.0 / D) + 1e-5)
    inverse = jnp.transpose(jnp.broadcast_to(inverse_row[0:1], (128, 128)))
    wide = jnp.concatenate([inverse, inverse], axis=1)
    total = PK[z].astype(F32)
    for d in (1, 3, 2):
        arrived(PKR.at[d - 1], RS_IN + d - 1)
        total = total + PKR[d - 1].astype(F32)
    block = 2 * y + zh
    KV[rows(128 * block, 128), :] = (total * wide).astype(BF)
    lanes = (pl.ds(0, 128), pl.ds(128, 128))

    def cached(theirs, part):
        return KV.at[rows(128 * theirs, 128), lanes[part]]

    for part in range(2):
        for dy in (2, 1, 3, 0):
            for dz in range(2):
                if dy + dz == 0:
                    continue
                y_to = up(y, dy)
                h_to = zh if dz == 0 else 1 - zh
                mine = cached(block, part)
                send(
                    mine, mine, KV_IN[part] + 2 * dy + dz - 1,
                    dev(s, t, 2 * g + h_to, y_to), 2 * y_to + h_to > block,
                )
    front = len(pending)

    places = 256 * y + 128 * zh + lax.broadcasted_iota(jnp.int32, (128, 1), 0)
    starts = []
    run = jnp.int32(0)
    for c in range(GROUPS):
        starts.append(run)
        run = run + blocks[c] * UNIT
    lowest = jnp.zeros((128, 1), jnp.int32)
    for c in range(GROUPS - 2):
        lowest = jnp.where(places >= starts[c + 2], starts[c], lowest)
    keys_at = lax.broadcasted_iota(jnp.int32, (128, 1024), 1)
    allowed = (keys_at <= places) & (keys_at >= lowest)

    forward_out_weights(first)
    total = PQ[z].astype(F32)
    for d in (1, 3, 2):
        arrived(PQR.at[d - 1], RQ_IN + d - 1)
        total = total + PQR[d - 1].astype(F32)
    queries = (total * (wide * SCALE)).astype(BF)

    def wait_cached(part):
        for dy in (1, 3, 2, 0):
            for dz in range(2):
                if dy + dz == 0:
                    continue
                y_from = up(y, 4 - dy)
                h_from = zh if dz == 0 else 1 - zh
                theirs = 2 * y_from + h_from
                arrived(cached(theirs, part), KV_IN[part] + 2 * dy + dz - 1, theirs < block)

    wait_cached(0)
    keys = KV[:, 0:128]
    weights = []
    for h in range(2):
        scores = lax.dot_general(
            queries[:, 128 * h:128 * h + 128], keys, (((1,), (1,)), ((), ())), preferred_element_type=F32
        )
        scores = jnp.where(allowed, scores, -jnp.inf)
        exps = jnp.exp2(scores - jnp.max(scores, axis=1, keepdims=True))
        norm = jnp.sum(exps, axis=1, keepdims=True)
        weights.append((exps.astype(BF), norm))
    wait_cached(1)
    values = KV[:, 128:256]
    for h in range(2):
        exps, norm = weights[h]
        heads = jnp.dot(exps, values, preferred_element_type=F32) / norm
        AT[h] = heads.astype(BF)
        for d in (2, 1, 3):
            send(AT.at[h], ATR.at[z, :, lanes[h]], AT_IN + 4 * h + z, dev(s, up(t, d), t, y))
        send(AT.at[h], ATR.at[z, :, lanes[h]], AT_IN + 4 * h + z, dev(s, t, t, y), apart)

    @pl.when(diagonal)
    def _():
        for h in range(2):
            ATR[z, :, lanes[h]] = AT[h]

    flush(front)

    @pl.when(first)
    def _():
        pl.semaphore_signal(go, inc=1, device_id=dev(1, t, z, y), device_id_type=MESH)

    pl.when(first)(own_res.wait)
    arrived(RES, RES_IN, second)
    arrived(out_part(far, 0), O_FAR)
    arrived(out_part(far, 1), O_FAR + 1)
    for zp in range(4):
        for h in range(2):
            arrived(ATR.at[zp, :, lanes[h]], AT_IN + 4 * h + zp, jnp.logical_not(diagonal & (z == zp)))
    for c in range(4):
        for hh in range(2):
            product = jnp.dot(ATR[hh], WO[0:256, quarter[c]], preferred_element_type=F32)
            product = product + jnp.dot(ATR[2 + hh], WO[256:512, quarter[c]], preferred_element_type=F32)
            OS[c, 2 * hh] = product[0:64].astype(BF)
            OS[c, 2 * hh + 1] = product[64:128].astype(BF)
        for d in (2, 1, 3):
            send(OS.at[c, up(z, d)], OR.at[c, d - 1], RO_IN + 3 * c + d - 1, dev(s, t, up(z, d), y))
    summed = len(pending)

    sec = y // 2
    cross = second & (sec == 0)

    def out_rows(z_, y_):
        return rows(256 * (y_ % 2) + 64 * z_, 64)

    at_out = out_rows(z, y)

    for c in range(4):
        new = RES[:, quarter[c]].astype(F32) + OS[c, z].astype(F32)
        for d in (1, 3, 2):
            arrived(OR.at[c, d - 1], RO_IN + 3 * c + d - 1)
            new = new + OR[c, d - 1].astype(F32)
        ST[:, quarter[c]] = new.astype(BF)
        mine = ST.at[:, quarter[c]]
        for d in (2, 1, 3, 0):
            send(mine, X.at[my_rows, quarter[c]], X_IN + 4 * c + z, dev(1, up(t, d), t, y), first)
        if c % 2 == 0:
            continue
        mine, place = ST.at[:, half[c // 2]], out.at[at_out, half[c // 2]]
        for d in (2, 1, 3):
            if c == 1:
                send(mine, place, FZ_IN + d - 1, dev(sec, t, up(z, d), y), second, 0)
            else:
                send(mine, place, FY_IN + d - 1, dev(sec, t, z, up(y, d)), second, 0)
    for c in range(2):
        mine, place = ST.at[:, half[c]], out.at[at_out, half[c]]
        for d in (2, 1, 3):
            if c == 0:
                send(mine, place, REST_IN, dev(sec, t, z, up(y, d)), second, 0)
            else:
                send(mine, place, REST_IN, dev(sec, t, up(z, d), y), second, 0)
    send(ST, out.at[at_out], REST_IN, dev(sec, t, z, y), cross, 1)
    send(ST, RES, RES_IN, dev(1, t, z, y), first)

    @pl.when(second & (sec == 1))
    def _():
        out[at_out, :] = ST[...]

    holder = sec == s
    for d in (1, 3, 2):
        place = out.at[out_rows(up(z, 4 - d), y), half[0]]
        arrived(place, FZ_IN + d - 1, holder)
        for e in (2, 1, 3):
            send(place, place, REST_IN, dev(s, t, z, up(y, e)), holder, 2)
        y_from = up(y, 4 - d)
        here = y_from // 2 == s
        place = out.at[out_rows(z, y_from), half[1]]
        arrived(place, FY_IN + d - 1, here)
        for e in (2, 1, 3):
            send(place, place, REST_IN, dev(s, t, up(z, e), y), here, 2)
    assert len(pending) <= N_SEND - 3
    flush(len(pending))
    sent(out.at[0:384], 0, second)
    sent(out.at[0:64], 1, cross)
    guest = jnp.logical_not(holder)
    arrived(out.at[0:320], REST_IN, holder & second)
    arrived(out.at[0:384], REST_IN, holder & first)
    arrived(out.at[0:448], REST_IN, guest)
    sent(out.at[0:384], 2, holder)
    sent(out.at[0:192], 2, guest)


def on_device(*arrays):
    hbm = pl.BlockSpec(memory_space=pl.ANY)
    vmem = pl.BlockSpec(memory_space=pltpu.VMEM)
    return pl.pallas_call(
        kernel,
        out_shape=pltpu.VMEM((512, 1024), BF),
        in_specs=[hbm, hbm, hbm, hbm, hbm, hbm, pl.BlockSpec(memory_space=pltpu.SMEM)],
        out_specs=vmem,
        scratch_shapes=[
            pltpu.VMEM((1024, 512), BF),
            pltpu.VMEM((1024, 512), BF),
            pltpu.VMEM((512, 1024), BF),
            pltpu.VMEM((256, 1024), BF),
            pltpu.VMEM((256, 1024), BF),
            pltpu.VMEM((256, 512), F32),
            pltpu.VMEM((4, 128, 256), BF),
            pltpu.VMEM((3, 128, 256), BF),
            pltpu.VMEM((4, 128, 256), BF),
            pltpu.VMEM((3, 128, 256), BF),
            pltpu.VMEM((2, 8, 128), F32),
            pltpu.VMEM((3, 8, 128), F32),
            pltpu.VMEM((1024, 256), BF),
            pltpu.VMEM((2, 128, 128), BF),
            pltpu.VMEM((4, 128, 256), BF),
            pltpu.VMEM((4, 4, 64, 256), BF),
            pltpu.VMEM((4, 3, 64, 256), BF),
            pltpu.VMEM((64, 1024), BF),
            pltpu.VMEM((64, 1024), BF),
            pltpu.VMEM((1, 4096), F32),
            pltpu.SemaphoreType.DMA((N_SEND,)),
            pltpu.SemaphoreType.DMA((N_RECV,)),
            pltpu.SemaphoreType.DMA((N_LOCAL,)),
            pltpu.SemaphoreType.REGULAR,
        ],
        compiler_params=pltpu.CompilerParams(
            collective_id=0, has_side_effects=True, vmem_limit_bytes=56 * 1024 * 1024
        ),
    )(*arrays)


def solution(mesh):
    in_specs = (
        P(None, "tp"),
        P("section", None),
        P("section", "rep", "tp"),
        P("section", "rep", "tp"),
        P("section", "rep", "tp"),
        P("section", "rep", "tp"),
        P(),
    )
    return jax.shard_map(
        on_device, mesh=mesh, in_specs=in_specs, out_specs=P("section", "tp"), check_vma=False
    )
```

```python
import math

import jax
import jax.numpy as jnp
from jax import lax
from jax.experimental import pallas as pl
from jax.experimental.pallas import tpu as pltpu
from jax.sharding import PartitionSpec as P

MESH = pl.DeviceIdType.MESH
BF = jnp.bfloat16
F32 = jnp.float32
D = 4096
GROUPS = 8
UNIT = 16
LARGEST = 3.0e38
SCALE = math.log2(math.e) / math.sqrt(128)

KV_LEFT, KV_RIGHT, KV_FAR = 0, 2, 4
Q_LEFT, Q_RIGHT, Q_FAR = 6, 8, 10
O_LEFT, O_RIGHT, O_FAR = 12, 13, 14
X_IN = 77
RS_IN, SQ_IN, RQ_IN = (24, 105), 27, 30
KV_IN = (33, 70)
AT_IN = 40
RO_IN = 93
RES_IN = 54
FZ_IN, FY_IN, REST_IN = 55, 58, 61
FINE = 62
N_RECV = 108
N_SEND = 140
N_LOCAL = 8


def kernel(
    emb, gain, wq, wk, wv, wo, blocks, out,
    WKV, WQ, WO, X, XG, ACC, PK, PKR, PQ, PQR, SQ, SQR, KV, AT, ATR, OS, OR, RES, ST, GAIN,
    send_sems, recv_sems, local_sems, go,
):
    s = lax.axis_index("section")
    t = lax.axis_index("tp")
    r = lax.axis_index("rep")
    z = r // 4
    y = r % 4
    g = z // 2
    zh = z % 2
    first = s == 0
    second = s == 1
    diagonal = z == t
    apart = jnp.logical_not(diagonal)

    def dev(s_, t_, z_, y_):
        return (s_, t_, z_ * 4 + y_)

    def up(v, d):
        return (v + d) % 4

    pending = []

    def send(src, dst, ridx, device, when=None, group=None):
        c = pltpu.make_async_remote_copy(
            src_ref=src, dst_ref=dst,
            send_sem=send_sems.at[len(pending) if group is None else N_SEND - 1 - group],
            recv_sem=recv_sems.at[ridx], device_id=device, device_id_type=MESH,
        )
        if when is None:
            c.start()
        else:
            pl.when(when)(c.start)
        if group is None:
            pending.append((c, when))

    finished = [0]

    def flush(count):
        for c, when in pending[finished[0]:count]:
            if when is None:
                c.wait_send()
            else:
                pl.when(when)(c.wait_send)
        finished[0] = max(finished[0], count)

    def arrived(ref, ridx, when=None):
        c = pltpu.make_async_remote_copy(
            src_ref=ref, dst_ref=ref, send_sem=send_sems.at[0],
            recv_sem=recv_sems.at[ridx], device_id=dev(1 - s, t, z, y), device_id_type=MESH,
        )
        if when is None:
            c.wait_recv()
        else:
            pl.when(when)(c.wait_recv)

    def sent(ref, group, when):
        c = pltpu.make_async_remote_copy(
            src_ref=ref, dst_ref=ref, send_sem=send_sems.at[N_SEND - 1 - group],
            recv_sem=recv_sems.at[0], device_id=dev(1 - s, t, z, y), device_id_type=MESH,
        )
        pl.when(when)(c.wait_send)

    def rows(start, size):
        return pl.ds(pl.multiple_of(start, size), size)

    KV[:, 128:256] = jnp.zeros((1024, 128), BF)

    barrier = pltpu.get_barrier_semaphore()

    def greet(device):
        pl.semaphore_signal(barrier, inc=1, device_id=device, device_id_type=MESH)

    for d in range(4):
        @pl.when(first)
        def _():
            greet(dev(1, d, t, y))

        @pl.when(second)
        def _():
            greet(dev(0, z, d, y))
    for d in (2, 1, 3):
        greet(dev(s, up(t, d), t, y))
        greet(dev(s, z, up(z, d), y))

    @pl.when(apart)
    def _():
        greet(dev(s, t, t, y))
        greet(dev(s, z, z, y))
    for d in (2, 1, 3):
        greet(dev(s, t, z + 1 - 2 * zh, up(y, d)))
        greet(dev(s, t, z, up(y, d)))
        greet(dev(s, t, up(z, d), y))
        greet(dev(1 - s, t, z, up(y, d)))
        greet(dev(1 - s, t, up(z, d), y))
    greet(dev(1 - s, t, z, y))

    at_y = rows(256 * y, 256)
    kc, vc = pl.ds(0, 256), pl.ds(256, 256)
    own = [
        pltpu.make_async_copy(wk.at[0], WKV.at[at_y, kc], local_sems.at[0]),
        pltpu.make_async_copy(wv.at[0], WKV.at[at_y, vc], local_sems.at[1]),
        pltpu.make_async_copy(wq.at[0], WQ.at[at_y], local_sems.at[2]),
        pltpu.make_async_copy(wo.at[0], WO.at[rows(128 * y, 128)], local_sems.at[3]),
        pltpu.make_async_copy(gain, GAIN, local_sems.at[6]),
    ]
    for c in own:
        c.start()
    my_emb = emb.at[rows(256 * y + 64 * z, 64)]
    my_rows = rows(64 * z, 64)
    own_x = pltpu.make_async_copy(my_emb, X.at[my_rows], local_sems.at[4])
    own_res = pltpu.make_async_copy(my_emb, RES, local_sems.at[5])
    pl.when(first & diagonal)(own_x.start)
    pl.when(first)(own_res.start)

    pl.semaphore_wait(barrier, 26 + 2 * (1 - diagonal.astype(jnp.int32)))

    right, left, far = up(y, 1), up(y, 3), up(y, 2)
    dev_r, dev_l = dev(s, t, z, right), dev(s, t, z, left)
    at_l, at_r, at_f = rows(256 * left, 256), rows(256 * right, 256), rows(256 * far, 256)

    @pl.when(second)
    def _():
        pl.semaphore_wait(go, 1)

    def kv_part(block, h, c):
        return WKV.at[rows(256 * block + 128 * h, 128), c]

    for h in range(2):
        send(wk.at[0, pl.ds(128 * h, 128)], kv_part(y, h, kc), FINE + h, dev_r)
        send(wv.at[0, pl.ds(128 * h, 128)], kv_part(y, h, vc), FINE + 2 + h, dev_l)

    half = (pl.ds(0, 512), pl.ds(512, 512))
    quarter = [pl.ds(256 * c, 256) for c in range(4)]
    for d in (2, 1, 3):
        send(my_emb, X.at[my_rows], X_IN + z, dev(0, up(t, d), t, y), first)
    send(my_emb, X.at[my_rows], X_IN + z, dev(0, t, t, y), first & apart)

    send(wv.at[0], WKV.at[at_y, vc], KV_LEFT + 1, dev_r)
    send(wk.at[0], WKV.at[at_y, kc], KV_RIGHT, dev_l)
    for h in range(2):
        part = kv_part(left, h, kc)
        arrived(part, FINE + h)
        send(part, part, FINE + 4 + h, dev_r)
        part = kv_part(right, h, vc)
        arrived(part, FINE + 2 + h)
        send(part, part, FINE + 6 + h, dev_l)

    def q_rows(block, h):
        return rows(256 * block + 128 * h, 128)

    q_src = (wq.at[0, pl.ds(0, 128)], wq.at[0, pl.ds(128, 128)])
    send(q_src[0], WQ.at[q_rows(y, 0)], Q_LEFT, dev_r)
    send(q_src[1], WQ.at[q_rows(y, 1)], Q_RIGHT + 1, dev_l)
    send(q_src[1], WQ.at[q_rows(y, 1)], Q_LEFT + 1, dev_r)
    send(q_src[0], WQ.at[q_rows(y, 0)], Q_RIGHT, dev_l)

    def forward_q(when):
        low, high = WQ.at[q_rows(left, 0)], WQ.at[q_rows(right, 1)]
        arrived(low, Q_LEFT, when)
        send(low, low, Q_FAR, dev_r, when)
        arrived(high, Q_RIGHT + 1, when)
        send(high, high, Q_FAR + 1, dev_l, when)

    ow_y = rows(128 * y, 128)
    ow_l, ow_r = rows(128 * left, 128), rows(128 * right, 128)

    def out_part(block, h):
        return WO.at[rows(128 * block + 64 * h, 64)]

    def send_out_weights(when):
        send(wo.at[0], WO.at[ow_y], O_LEFT, dev_r, when)
        send(wo.at[0], WO.at[ow_y], O_RIGHT, dev_l, when)

    def forward_out_weights(when):
        arrived(WO.at[ow_l], O_LEFT, when)
        send(out_part(left, 0), out_part(left, 0), O_FAR, dev_r, when)
        arrived(WO.at[ow_r], O_RIGHT, when)
        send(out_part(right, 1), out_part(right, 1), O_FAR + 1, dev_l, when)

    forward_q(second)
    send_out_weights(second)

    def multiply(block, ref, columns):
        at = rows(256 * block, 256)
        return jnp.dot(XG[:, at], ref[at, columns], preferred_element_type=F32)

    def pack(part):
        for gg in range(2):
            for hh in range(2):
                piece = ACC[128 * hh:128 * hh + 128, 256 * part + 128 * gg:256 * part + 128 * gg + 128]
                PK[part, 2 * gg + hh] = piece.astype(BF)
        for d in (2, 1, 3):
            other = up(z, d)
            send(PK.at[part, other], PKR.at[part, d - 1], RS_IN[part] + d - 1, dev(s, t, other, y))

    def scale_rows(squares):
        scale = lax.rsqrt(squares * (1.0 / D) + 1e-5)
        XG[...] = (X[...].astype(F32) * scale * GAIN[:, rows(1024 * z, 1024)]).astype(BF)
        for h in range(2):
            column = jnp.broadcast_to(squares[128 * h:128 * h + 128], (128, 128))
            SQ[h] = jnp.transpose(column)[0:8]

    for c in own:
        c.wait()

    @pl.when(first)
    def _():
        pl.when(diagonal)(own_x.wait)
        for zp in range(4):
            arrived(X.at[pl.ds(64 * zp, 64)], X_IN + zp, jnp.logical_not(diagonal & (z == zp)))
        x = X[...].astype(F32)
        scale_rows(jnp.sum(x * x, axis=1, keepdims=True))
        part = multiply(y, WKV, kc) + multiply(left, WKV, kc)
        arrived(WKV.at[at_r, kc], KV_RIGHT)
        part = part + multiply(right, WKV, kc)
        for h in range(2):
            arrived(kv_part(far, h, kc), FINE + 4 + h)
        ACC[:, kc] = part + multiply(far, WKV, kc)

    @pl.when(second)
    def _():
        arrived(WKV.at[at_l, vc], KV_LEFT + 1)
        arrived(WKV.at[at_r, kc], KV_RIGHT)
        for h in range(2):
            arrived(kv_part(far, h, kc), FINE + 4 + h)
            arrived(kv_part(far, h, vc), FINE + 6 + h)
        squares = jnp.zeros((256, 1), F32)
        for c in range(4):
            for zp in range(4):
                arrived(X.at[pl.ds(64 * zp, 64), quarter[c]], X_IN + 4 * c + zp)
            x = X[:, quarter[c]].astype(F32)
            squares = squares + jnp.sum(x * x, axis=1, keepdims=True)
        scale_rows(squares)
        ACC[:, kc] = jnp.dot(XG[...], WKV[:, kc], preferred_element_type=F32)

    for d in (2, 1, 3):
        other = up(z, d)
        send(SQ.at[other % 2], SQR.at[d - 1], SQ_IN + d - 1, dev(s, t, other, y))
    pack(0)

    @pl.when(first)
    def _():
        arrived(WKV.at[at_l, vc], KV_LEFT + 1)
        part = multiply(y, WKV, vc) + multiply(left, WKV, vc) + multiply(right, WKV, vc)
        for h in range(2):
            arrived(kv_part(far, h, vc), FINE + 6 + h)
        ACC[:, vc] = part + multiply(far, WKV, vc)

    @pl.when(second)
    def _():
        ACC[:, vc] = jnp.dot(XG[...], WKV[:, vc], preferred_element_type=F32)

    pack(1)

    forward_q(first)
    send_out_weights(first)
    all_q = pl.ds(0, 512)
    part = multiply(y, WQ, all_q)
    arrived(WQ.at[q_rows(left, 1)], Q_LEFT + 1)
    part = part + multiply(left, WQ, all_q)
    arrived(WQ.at[q_rows(right, 0)], Q_RIGHT)
    part = part + multiply(right, WQ, all_q)
    arrived(WQ.at[q_rows(far, 0)], Q_FAR)
    arrived(WQ.at[q_rows(far, 1)], Q_FAR + 1)
    part = part + multiply(far, WQ, all_q)
    for gg in range(2):
        for hh in range(2):
            PQ[2 * gg + hh] = part[128 * hh:128 * hh + 128, 256 * gg:256 * gg + 256].astype(BF)
    for d in (2, 1, 3):
        other = up(z, d)
        send(PQ.at[other], PQR.at[d - 1], RQ_IN + d - 1, dev(s, t, other, y))

    means = [SQ[zh] * (1.0 / D)]
    for d in (1, 2, 3):
        arrived(SQR.at[d - 1], SQ_IN + d - 1)
        means.append(SQR[d - 1] * (1.0 / D))
    inverse = lax.rsqrt(means[0] + means[1] + means[2] + means[3] + 1e-5)
    shares = []
    for mean in means:
        share = inverse * jnp.sqrt(jnp.minimum(mean + 1e-5, LARGEST))
        shares.append(jnp.transpose(jnp.broadcast_to(share[0:1], (128, 128))))
    block = 2 * y + zh
    lanes = (pl.ds(0, 128), pl.ds(128, 128))

    def cached(theirs, part):
        return KV.at[rows(128 * theirs, 128), lanes[part]]

    for part in range(2):
        total = PK[part, z].astype(F32) * shares[0]
        for d in (1, 3, 2):
            arrived(PKR.at[part, d - 1], RS_IN[part] + d - 1)
            total = total + PKR[part, d - 1].astype(F32) * shares[d]
        mine = cached(block, part)
        mine[...] = total.astype(BF)
        for dy in (2, 1, 3, 0):
            for dz in range(2):
                if dy + dz == 0:
                    continue
                y_to = up(y, dy)
                h_to = zh if dz == 0 else 1 - zh
                send(
                    mine, mine, KV_IN[part] + 2 * dy + dz - 1,
                    dev(s, t, 2 * g + h_to, y_to), 2 * y_to + h_to > block,
                )
    front = len(pending)

    places = 256 * y + 128 * zh + lax.broadcasted_iota(jnp.int32, (128, 1), 0)
    starts = []
    run = jnp.int32(0)
    for c in range(GROUPS):
        starts.append(run)
        run = run + blocks[c] * UNIT
    lowest = jnp.zeros((128, 1), jnp.int32)
    for c in range(GROUPS - 2):
        lowest = jnp.where(places >= starts[c + 2], starts[c], lowest)
    keys_at = lax.broadcasted_iota(jnp.int32, (128, 1024), 1)
    allowed = (keys_at <= places) & (keys_at >= lowest)

    forward_out_weights(first)
    forward_out_weights(second)
    wide = [jnp.concatenate([share, share], axis=1) for share in shares]
    total = PQ[z].astype(F32) * wide[0]
    for d in (1, 3, 2):
        arrived(PQR.at[d - 1], RQ_IN + d - 1)
        total = total + PQR[d - 1].astype(F32) * wide[d]
    queries = (total * SCALE).astype(BF)

    def wait_cached(part):
        for dy in (1, 3, 2, 0):
            for dz in range(2):
                if dy + dz == 0:
                    continue
                y_from = up(y, 4 - dy)
                h_from = zh if dz == 0 else 1 - zh
                theirs = 2 * y_from + h_from
                arrived(cached(theirs, part), KV_IN[part] + 2 * dy + dz - 1, theirs < block)

    wait_cached(0)
    keys = KV[:, 0:128]
    weights = []
    for h in range(2):
        scores = lax.dot_general(
            queries[:, 128 * h:128 * h + 128], keys, (((1,), (1,)), ((), ())), preferred_element_type=F32
        )
        scores = jnp.where(allowed, scores, -jnp.inf)
        exps = jnp.exp2(scores - jnp.max(scores, axis=1, keepdims=True))
        norm = jnp.sum(exps, axis=1, keepdims=True)
        weights.append((exps.astype(BF), norm))
    wait_cached(1)
    values = KV[:, 128:256]
    for h in range(2):
        exps, norm = weights[h]
        heads = jnp.dot(exps, values, preferred_element_type=F32) / norm
        AT[h] = heads.astype(BF)
        for d in (2, 1, 3):
            send(AT.at[h], ATR.at[z, :, lanes[h]], AT_IN + 4 * h + z, dev(s, up(t, d), t, y))
        send(AT.at[h], ATR.at[z, :, lanes[h]], AT_IN + 4 * h + z, dev(s, t, t, y), apart)

    @pl.when(diagonal)
    def _():
        for h in range(2):
            ATR[z, :, lanes[h]] = AT[h]

    flush(front)

    @pl.when(first)
    def _():
        pl.semaphore_signal(go, inc=1, device_id=dev(1, t, z, y), device_id_type=MESH)

    pl.when(first)(own_res.wait)
    arrived(RES, RES_IN, second)
    arrived(out_part(far, 0), O_FAR)
    arrived(out_part(far, 1), O_FAR + 1)
    for zp in range(4):
        for h in range(2):
            arrived(ATR.at[zp, :, lanes[h]], AT_IN + 4 * h + zp, jnp.logical_not(diagonal & (z == zp)))
    for c in range(4):
        for hh in range(2):
            product = jnp.dot(ATR[hh], WO[0:256, quarter[c]], preferred_element_type=F32)
            product = product + jnp.dot(ATR[2 + hh], WO[256:512, quarter[c]], preferred_element_type=F32)
            OS[c, 2 * hh] = product[0:64].astype(BF)
            OS[c, 2 * hh + 1] = product[64:128].astype(BF)
        for d in (2, 1, 3):
            send(OS.at[c, up(z, d)], OR.at[c, d - 1], RO_IN + 3 * c + d - 1, dev(s, t, up(z, d), y))
    summed = len(pending)

    sec = y // 2
    cross = second & (sec == 0)

    def out_rows(z_, y_):
        return rows(256 * (y_ % 2) + 64 * z_, 64)

    at_out = out_rows(z, y)

    for c in range(4):
        new = RES[:, quarter[c]].astype(F32) + OS[c, z].astype(F32)
        for d in (1, 3, 2):
            arrived(OR.at[c, d - 1], RO_IN + 3 * c + d - 1)
            new = new + OR[c, d - 1].astype(F32)
        ST[:, quarter[c]] = new.astype(BF)
        mine = ST.at[:, quarter[c]]
        for d in (2, 1, 3, 0):
            send(mine, X.at[my_rows, quarter[c]], X_IN + 4 * c + z, dev(1, up(t, d), t, y), first)
        if c % 2 == 0:
            continue
        mine, place = ST.at[:, half[c // 2]], out.at[at_out, half[c // 2]]
        for d in (2, 1, 3):
            if c == 1:
                send(mine, place, FZ_IN + d - 1, dev(sec, t, up(z, d), y), second, 0)
            else:
                send(mine, place, FY_IN + d - 1, dev(sec, t, z, up(y, d)), second, 0)
    for c in range(2):
        mine, place = ST.at[:, half[c]], out.at[at_out, half[c]]
        for d in (2, 1, 3):
            if c == 0:
                send(mine, place, REST_IN, dev(sec, t, z, up(y, d)), second, 0)
            else:
                send(mine, place, REST_IN, dev(sec, t, up(z, d), y), second, 0)
    send(ST, out.at[at_out], REST_IN, dev(sec, t, z, y), cross, 1)
    send(ST, RES, RES_IN, dev(1, t, z, y), first)

    @pl.when(second & (sec == 1))
    def _():
        out[at_out, :] = ST[...]

    holder = sec == s
    for d in (1, 3, 2):
        place = out.at[out_rows(up(z, 4 - d), y), half[0]]
        arrived(place, FZ_IN + d - 1, holder)
        for e in (2, 1, 3):
            send(place, place, REST_IN, dev(s, t, z, up(y, e)), holder, 2)
        y_from = up(y, 4 - d)
        here = y_from // 2 == s
        place = out.at[out_rows(z, y_from), half[1]]
        arrived(place, FY_IN + d - 1, here)
        for e in (2, 1, 3):
            send(place, place, REST_IN, dev(s, t, up(z, e), y), here, 2)
    assert len(pending) <= N_SEND - 3
    flush(len(pending))
    sent(out.at[0:384], 0, second)
    sent(out.at[0:64], 1, cross)
    guest = jnp.logical_not(holder)
    arrived(out.at[0:320], REST_IN, holder & second)
    arrived(out.at[0:384], REST_IN, holder & first)
    arrived(out.at[0:448], REST_IN, guest)
    sent(out.at[0:384], 2, holder)
    sent(out.at[0:192], 2, guest)


def on_device(*arrays):
    hbm = pl.BlockSpec(memory_space=pl.ANY)
    vmem = pl.BlockSpec(memory_space=pltpu.VMEM)
    return pl.pallas_call(
        kernel,
        out_shape=pltpu.VMEM((512, 1024), BF),
        in_specs=[hbm, hbm, hbm, hbm, hbm, hbm, pl.BlockSpec(memory_space=pltpu.SMEM)],
        out_specs=vmem,
        scratch_shapes=[
            pltpu.VMEM((1024, 512), BF),
            pltpu.VMEM((1024, 512), BF),
            pltpu.VMEM((512, 1024), BF),
            pltpu.VMEM((256, 1024), BF),
            pltpu.VMEM((256, 1024), BF),
            pltpu.VMEM((256, 512), F32),
            pltpu.VMEM((2, 4, 128, 128), BF),
            pltpu.VMEM((2, 3, 128, 128), BF),
            pltpu.VMEM((4, 128, 256), BF),
            pltpu.VMEM((3, 128, 256), BF),
            pltpu.VMEM((2, 8, 128), F32),
            pltpu.VMEM((3, 8, 128), F32),
            pltpu.VMEM((1024, 256), BF),
            pltpu.VMEM((2, 128, 128), BF),
            pltpu.VMEM((4, 128, 256), BF),
            pltpu.VMEM((4, 4, 64, 256), BF),
            pltpu.VMEM((4, 3, 64, 256), BF),
            pltpu.VMEM((64, 1024), BF),
            pltpu.VMEM((64, 1024), BF),
            pltpu.VMEM((1, 4096), F32),
            pltpu.SemaphoreType.DMA((N_SEND,)),
            pltpu.SemaphoreType.DMA((N_RECV,)),
            pltpu.SemaphoreType.DMA((N_LOCAL,)),
            pltpu.SemaphoreType.REGULAR,
        ],
        compiler_params=pltpu.CompilerParams(
            collective_id=0, has_side_effects=True, vmem_limit_bytes=56 * 1024 * 1024
        ),
    )(*arrays)


def solution(mesh):
    in_specs = (
        P(None, "tp"),
        P("section", None),
        P("section", "rep", "tp"),
        P("section", "rep", "tp"),
        P("section", "rep", "tp"),
        P("section", "rep", "tp"),
        P(),
    )
    return jax.shard_map(
        on_device, mesh=mesh, in_specs=in_specs, out_specs=P("section", "tp"), check_vma=False
    )
```

```python
import math

import jax
import jax.numpy as jnp
from jax import lax
from jax.experimental import pallas as pl
from jax.experimental.pallas import tpu as pltpu
from jax.sharding import PartitionSpec as P

MESH = pl.DeviceIdType.MESH
BF = jnp.bfloat16
F32 = jnp.float32
D = 4096
GROUPS = 8
UNIT = 16
LARGEST = 3.0e38
SCALE = math.log2(math.e) / math.sqrt(128)

KV_LEFT, KV_RIGHT, KV_FAR = 0, 2, 4
Q_LEFT, Q_RIGHT, Q_FAR = 6, 8, 10
O_LEFT, O_RIGHT, O_FAR = 12, 13, 14
X_IN = 77
RS_IN, SQ_IN, RQ_IN = (24, 105), 27, 30
KV_IN = (33, 70)
AT_IN = 40
RO_IN = 93
RES_IN = 54
FZ_IN, FY_IN, REST_IN = 55, 58, 61
FINE = 62
N_RECV = 108
N_SEND = 140
N_LOCAL = 8


def kernel(
    emb, gain, wq, wk, wv, wo, blocks, out,
    WKV, WQ, WO, X, XG, ACC, PK, PKR, PQ, PQR, SQ, SQR, KV, AT, ATR, OS, OR, RES, ST, GAIN,
    send_sems, recv_sems, local_sems, go,
):
    s = lax.axis_index("section")
    t = lax.axis_index("tp")
    r = lax.axis_index("rep")
    z = r // 4
    y = r % 4
    g = z // 2
    zh = z % 2
    first = s == 0
    second = s == 1
    diagonal = z == t
    apart = jnp.logical_not(diagonal)

    def dev(s_, t_, z_, y_):
        return (s_, t_, z_ * 4 + y_)

    def up(v, d):
        return (v + d) % 4

    pending = []

    def send(src, dst, ridx, device, when=None, group=None):
        c = pltpu.make_async_remote_copy(
            src_ref=src, dst_ref=dst,
            send_sem=send_sems.at[len(pending) if group is None else N_SEND - 1 - group],
            recv_sem=recv_sems.at[ridx], device_id=device, device_id_type=MESH,
        )
        if when is None:
            c.start()
        else:
            pl.when(when)(c.start)
        if group is None:
            pending.append((c, when))

    finished = [0]

    def flush(count):
        for c, when in pending[finished[0]:count]:
            if when is None:
                c.wait_send()
            else:
                pl.when(when)(c.wait_send)
        finished[0] = max(finished[0], count)

    def arrived(ref, ridx, when=None):
        c = pltpu.make_async_remote_copy(
            src_ref=ref, dst_ref=ref, send_sem=send_sems.at[0],
            recv_sem=recv_sems.at[ridx], device_id=dev(1 - s, t, z, y), device_id_type=MESH,
        )
        if when is None:
            c.wait_recv()
        else:
            pl.when(when)(c.wait_recv)

    def sent(ref, group, when):
        c = pltpu.make_async_remote_copy(
            src_ref=ref, dst_ref=ref, send_sem=send_sems.at[N_SEND - 1 - group],
            recv_sem=recv_sems.at[0], device_id=dev(1 - s, t, z, y), device_id_type=MESH,
        )
        pl.when(when)(c.wait_send)

    def rows(start, size):
        return pl.ds(pl.multiple_of(start, size), size)

    KV[:, 128:256] = jnp.zeros((1024, 128), BF)

    barrier = pltpu.get_barrier_semaphore()

    def greet(device):
        pl.semaphore_signal(barrier, inc=1, device_id=device, device_id_type=MESH)

    for d in range(4):
        @pl.when(first)
        def _():
            greet(dev(1, d, t, y))

        @pl.when(second)
        def _():
            greet(dev(0, z, d, y))
    for d in (2, 1, 3):
        greet(dev(s, up(t, d), t, y))
        greet(dev(s, z, up(z, d), y))

    @pl.when(apart)
    def _():
        greet(dev(s, t, t, y))
        greet(dev(s, z, z, y))
    for d in (2, 1, 3):
        greet(dev(s, t, z + 1 - 2 * zh, up(y, d)))
        greet(dev(s, t, z, up(y, d)))
        greet(dev(s, t, up(z, d), y))
        greet(dev(1 - s, t, z, up(y, d)))
        greet(dev(1 - s, t, up(z, d), y))
    greet(dev(1 - s, t, z, y))

    at_y = rows(256 * y, 256)
    kc, vc = pl.ds(0, 256), pl.ds(256, 256)
    own = [
        pltpu.make_async_copy(wk.at[0], WKV.at[at_y, kc], local_sems.at[0]),
        pltpu.make_async_copy(wv.at[0], WKV.at[at_y, vc], local_sems.at[1]),
        pltpu.make_async_copy(wq.at[0], WQ.at[at_y], local_sems.at[2]),
        pltpu.make_async_copy(wo.at[0], WO.at[rows(128 * y, 128)], local_sems.at[3]),
        pltpu.make_async_copy(gain, GAIN, local_sems.at[6]),
    ]
    for c in own:
        c.start()
    my_emb = emb.at[rows(256 * y + 64 * z, 64)]
    my_rows = rows(64 * z, 64)
    own_x = pltpu.make_async_copy(my_emb, X.at[my_rows], local_sems.at[4])
    own_res = pltpu.make_async_copy(my_emb, RES, local_sems.at[5])
    pl.when(first & diagonal)(own_x.start)
    pl.when(first)(own_res.start)

    pl.semaphore_wait(barrier, 26 + 2 * (1 - diagonal.astype(jnp.int32)))

    right, left, far = up(y, 1), up(y, 3), up(y, 2)
    dev_r, dev_l = dev(s, t, z, right), dev(s, t, z, left)
    at_l, at_r, at_f = rows(256 * left, 256), rows(256 * right, 256), rows(256 * far, 256)

    @pl.when(second)
    def _():
        pl.semaphore_wait(go, 1)

    def kv_part(block, h, c):
        return WKV.at[rows(256 * block + 128 * h, 128), c]

    for h in range(2):
        send(wk.at[0, pl.ds(128 * h, 128)], kv_part(y, h, kc), FINE + h, dev_r)
        send(wv.at[0, pl.ds(128 * h, 128)], kv_part(y, h, vc), FINE + 2 + h, dev_l)

    half = (pl.ds(0, 512), pl.ds(512, 512))
    quarter = [pl.ds(256 * c, 256) for c in range(4)]
    for d in (2, 1, 3):
        send(my_emb, X.at[my_rows], X_IN + z, dev(0, up(t, d), t, y), first)
    send(my_emb, X.at[my_rows], X_IN + z, dev(0, t, t, y), first & apart)

    send(wv.at[0], WKV.at[at_y, vc], KV_LEFT + 1, dev_r)
    send(wk.at[0], WKV.at[at_y, kc], KV_RIGHT, dev_l)
    for h in range(2):
        part = kv_part(left, h, kc)
        arrived(part, FINE + h)
        send(part, part, FINE + 4 + h, dev_r)
        part = kv_part(right, h, vc)
        arrived(part, FINE + 2 + h)
        send(part, part, FINE + 6 + h, dev_l)

    def q_rows(block, h):
        return rows(256 * block + 128 * h, 128)

    q_src = (wq.at[0, pl.ds(0, 128)], wq.at[0, pl.ds(128, 128)])
    send(q_src[0], WQ.at[q_rows(y, 0)], Q_LEFT, dev_r)
    send(q_src[1], WQ.at[q_rows(y, 1)], Q_RIGHT + 1, dev_l)
    send(q_src[1], WQ.at[q_rows(y, 1)], Q_LEFT + 1, dev_r)
    send(q_src[0], WQ.at[q_rows(y, 0)], Q_RIGHT, dev_l)

    def forward_q(when):
        low, high = WQ.at[q_rows(left, 0)], WQ.at[q_rows(right, 1)]
        arrived(low, Q_LEFT, when)
        send(low, low, Q_FAR, dev_r, when)
        arrived(high, Q_RIGHT + 1, when)
        send(high, high, Q_FAR + 1, dev_l, when)

    ow_y = rows(128 * y, 128)
    ow_l, ow_r = rows(128 * left, 128), rows(128 * right, 128)

    def out_part(block, h):
        return WO.at[rows(128 * block + 64 * h, 64)]

    def send_out_weights(when):
        send(wo.at[0], WO.at[ow_y], O_LEFT, dev_r, when)
        send(wo.at[0], WO.at[ow_y], O_RIGHT, dev_l, when)

    def forward_out_weights(when):
        arrived(WO.at[ow_l], O_LEFT, when)
        send(out_part(left, 0), out_part(left, 0), O_FAR, dev_r, when)
        arrived(WO.at[ow_r], O_RIGHT, when)
        send(out_part(right, 1), out_part(right, 1), O_FAR + 1, dev_l, when)

    forward_q(second)
    send_out_weights(second)

    def multiply(block, ref, columns):
        at = rows(256 * block, 256)
        return jnp.dot(XG[:, at], ref[at, columns], preferred_element_type=F32)

    def pack(part):
        for gg in range(2):
            for hh in range(2):
                piece = ACC[128 * hh:128 * hh + 128, 256 * part + 128 * gg:256 * part + 128 * gg + 128]
                PK[part, 2 * gg + hh] = piece.astype(BF)
        for d in (2, 1, 3):
            other = up(z, d)
            send(PK.at[part, other], PKR.at[part, d - 1], RS_IN[part] + d - 1, dev(s, t, other, y))

    def scale_rows(squares):
        scale = lax.rsqrt(squares * (1.0 / D) + 1e-5)
        XG[...] = (X[...].astype(F32) * scale * GAIN[:, rows(1024 * z, 1024)]).astype(BF)
        for h in range(2):
            column = jnp.broadcast_to(squares[128 * h:128 * h + 128], (128, 128))
            SQ[h] = jnp.transpose(column)[0:8]

    for c in own:
        c.wait()

    @pl.when(first)
    def _():
        pl.when(diagonal)(own_x.wait)
        for zp in range(4):
            arrived(X.at[pl.ds(64 * zp, 64)], X_IN + zp, jnp.logical_not(diagonal & (z == zp)))
        x = X[...].astype(F32)
        scale_rows(jnp.sum(x * x, axis=1, keepdims=True))
        part = multiply(y, WKV, kc) + multiply(left, WKV, kc)
        arrived(WKV.at[at_r, kc], KV_RIGHT)
        part = part + multiply(right, WKV, kc)
        for h in range(2):
            arrived(kv_part(far, h, kc), FINE + 4 + h)
        ACC[:, kc] = part + multiply(far, WKV, kc)

    @pl.when(second)
    def _():
        arrived(WKV.at[at_l, vc], KV_LEFT + 1)
        arrived(WKV.at[at_r, kc], KV_RIGHT)
        for h in range(2):
            arrived(kv_part(far, h, kc), FINE + 4 + h)
            arrived(kv_part(far, h, vc), FINE + 6 + h)
        squares = jnp.zeros((256, 1), F32)
        for c in range(4):
            for zp in range(4):
                arrived(X.at[pl.ds(64 * zp, 64), quarter[c]], X_IN + 4 * c + zp)
            x = X[:, quarter[c]].astype(F32)
            squares = squares + jnp.sum(x * x, axis=1, keepdims=True)
        scale_rows(squares)
        ACC[:, kc] = jnp.dot(XG[...], WKV[:, kc], preferred_element_type=F32)

    for d in (2, 1, 3):
        other = up(z, d)
        send(SQ.at[other % 2], SQR.at[d - 1], SQ_IN + d - 1, dev(s, t, other, y))
    pack(0)

    @pl.when(first)
    def _():
        arrived(WKV.at[at_l, vc], KV_LEFT + 1)
        part = multiply(y, WKV, vc) + multiply(left, WKV, vc) + multiply(right, WKV, vc)
        for h in range(2):
            arrived(kv_part(far, h, vc), FINE + 6 + h)
        ACC[:, vc] = part + multiply(far, WKV, vc)

    @pl.when(second)
    def _():
        ACC[:, vc] = jnp.dot(XG[...], WKV[:, vc], preferred_element_type=F32)

    pack(1)

    forward_q(first)
    send_out_weights(first)
    all_q = pl.ds(0, 512)
    part = multiply(y, WQ, all_q)
    arrived(WQ.at[q_rows(left, 1)], Q_LEFT + 1)
    part = part + multiply(left, WQ, all_q)
    arrived(WQ.at[q_rows(right, 0)], Q_RIGHT)
    part = part + multiply(right, WQ, all_q)
    arrived(WQ.at[q_rows(far, 0)], Q_FAR)
    arrived(WQ.at[q_rows(far, 1)], Q_FAR + 1)
    part = part + multiply(far, WQ, all_q)
    for gg in range(2):
        for hh in range(2):
            PQ[2 * gg + hh] = part[128 * hh:128 * hh + 128, 256 * gg:256 * gg + 256].astype(BF)
    for d in (2, 1, 3):
        other = up(z, d)
        send(PQ.at[other], PQR.at[d - 1], RQ_IN + d - 1, dev(s, t, other, y))

    means = [SQ[zh] * (1.0 / D)]
    for d in (1, 2, 3):
        arrived(SQR.at[d - 1], SQ_IN + d - 1)
        means.append(SQR[d - 1] * (1.0 / D))
    inverse = lax.rsqrt(means[0] + means[1] + means[2] + means[3] + 1e-5)
    shares = []
    for mean in means:
        share = inverse * jnp.sqrt(jnp.minimum(mean + 1e-5, LARGEST))
        shares.append(jnp.transpose(jnp.broadcast_to(share[0:1], (128, 128))))
    block = 2 * y + zh
    lanes = (pl.ds(0, 128), pl.ds(128, 128))

    def cached(theirs, part):
        return KV.at[rows(128 * theirs, 128), lanes[part]]

    for part in range(2):
        total = PK[part, z].astype(F32) * shares[0]
        for d in (1, 3, 2):
            arrived(PKR.at[part, d - 1], RS_IN[part] + d - 1)
            total = total + PKR[part, d - 1].astype(F32) * shares[d]
        mine = cached(block, part)
        mine[...] = total.astype(BF)
        for dy in (2, 1, 3, 0):
            for dz in range(2):
                if dy + dz == 0:
                    continue
                y_to = up(y, dy)
                h_to = zh if dz == 0 else 1 - zh
                send(
                    mine, mine, KV_IN[part] + 2 * dy + dz - 1,
                    dev(s, t, 2 * g + h_to, y_to), (2 * y_to + h_to > block) & (2 * y_to + h_to < block + 7),
                )
    front = len(pending)

    places = 256 * y + 128 * zh + lax.broadcasted_iota(jnp.int32, (128, 1), 0)
    starts = []
    run = jnp.int32(0)
    for c in range(GROUPS):
        starts.append(run)
        run = run + blocks[c] * UNIT
    lowest = jnp.zeros((128, 1), jnp.int32)
    for c in range(GROUPS - 2):
        lowest = jnp.where(places >= starts[c + 2], starts[c], lowest)
    keys_at = lax.broadcasted_iota(jnp.int32, (128, 1024), 1)
    allowed = (keys_at <= places) & (keys_at >= lowest)

    forward_out_weights(first)
    wide = [jnp.concatenate([share, share], axis=1) for share in shares]
    total = PQ[z].astype(F32) * wide[0]
    for d in (1, 3, 2):
        arrived(PQR.at[d - 1], RQ_IN + d - 1)
        total = total + PQR[d - 1].astype(F32) * wide[d]
    queries = (total * SCALE).astype(BF)

    def wait_cached(part):
        for dy in (1, 3, 2, 0):
            for dz in range(2):
                if dy + dz == 0:
                    continue
                y_from = up(y, 4 - dy)
                h_from = zh if dz == 0 else 1 - zh
                theirs = 2 * y_from + h_from
                arrived(cached(theirs, part), KV_IN[part] + 2 * dy + dz - 1, (theirs < block) & (theirs > block - 7))

    wait_cached(0)
    keys = KV[:, 0:128]
    weights = []
    for h in range(2):
        scores = lax.dot_general(
            queries[:, 128 * h:128 * h + 128], keys, (((1,), (1,)), ((), ())), preferred_element_type=F32
        )
        scores = jnp.where(allowed, scores, -jnp.inf)
        exps = jnp.exp2(scores - jnp.max(scores, axis=1, keepdims=True))
        norm = jnp.sum(exps, axis=1, keepdims=True)
        weights.append((exps.astype(BF), norm))
    wait_cached(1)
    values = KV[:, 128:256]
    for h in range(2):
        exps, norm = weights[h]
        heads = jnp.dot(exps, values, preferred_element_type=F32) / norm
        AT[h] = heads.astype(BF)
        for d in (2, 1, 3):
            send(AT.at[h], ATR.at[z, :, lanes[h]], AT_IN + 4 * h + z, dev(s, up(t, d), t, y))
        send(AT.at[h], ATR.at[z, :, lanes[h]], AT_IN + 4 * h + z, dev(s, t, t, y), apart)

    @pl.when(diagonal)
    def _():
        for h in range(2):
            ATR[z, :, lanes[h]] = AT[h]

    forward_out_weights(second)
    flush(front)

    @pl.when(first)
    def _():
        pl.semaphore_signal(go, inc=1, device_id=dev(1, t, z, y), device_id_type=MESH)

    pl.when(first)(own_res.wait)
    arrived(RES, RES_IN, second)
    arrived(out_part(far, 0), O_FAR)
    arrived(out_part(far, 1), O_FAR + 1)
    for zp in range(4):
        for h in range(2):
            arrived(ATR.at[zp, :, lanes[h]], AT_IN + 4 * h + zp, jnp.logical_not(diagonal & (z == zp)))
    for c in range(4):
        for hh in range(2):
            product = jnp.dot(ATR[hh], WO[0:256, quarter[c]], preferred_element_type=F32)
            product = product + jnp.dot(ATR[2 + hh], WO[256:512, quarter[c]], preferred_element_type=F32)
            OS[c, 2 * hh] = product[0:64].astype(BF)
            OS[c, 2 * hh + 1] = product[64:128].astype(BF)
        for d in (2, 1, 3):
            send(OS.at[c, up(z, d)], OR.at[c, d - 1], RO_IN + 3 * c + d - 1, dev(s, t, up(z, d), y))
    summed = len(pending)

    sec = y // 2
    cross = second & (sec == 0)

    def out_rows(z_, y_):
        return rows(256 * (y_ % 2) + 64 * z_, 64)

    at_out = out_rows(z, y)

    for c in range(4):
        new = RES[:, quarter[c]].astype(F32) + OS[c, z].astype(F32)
        for d in (1, 3, 2):
            arrived(OR.at[c, d - 1], RO_IN + 3 * c + d - 1)
            new = new + OR[c, d - 1].astype(F32)
        ST[:, quarter[c]] = new.astype(BF)
        mine = ST.at[:, quarter[c]]
        for d in (2, 1, 3, 0):
            send(mine, X.at[my_rows, quarter[c]], X_IN + 4 * c + z, dev(1, up(t, d), t, y), first)
        if c % 2 == 0:
            continue
        mine, place = ST.at[:, half[c // 2]], out.at[at_out, half[c // 2]]
        for d in (2, 1, 3):
            if c == 1:
                send(mine, place, FZ_IN + d - 1, dev(sec, t, up(z, d), y), second, 0)
            else:
                send(mine, place, FY_IN + d - 1, dev(sec, t, z, up(y, d)), second, 0)
    for c in range(2):
        mine, place = ST.at[:, half[c]], out.at[at_out, half[c]]
        for d in (2, 1, 3):
            if c == 0:
                send(mine, place, REST_IN, dev(sec, t, z, up(y, d)), second, 0)
            else:
                send(mine, place, REST_IN, dev(sec, t, up(z, d), y), second, 0)
    send(ST, out.at[at_out], REST_IN, dev(sec, t, z, y), cross, 1)
    send(ST, RES, RES_IN, dev(1, t, z, y), first)

    @pl.when(second & (sec == 1))
    def _():
        out[at_out, :] = ST[...]

    holder = sec == s
    for d in (1, 3, 2):
        place = out.at[out_rows(up(z, 4 - d), y), half[0]]
        arrived(place, FZ_IN + d - 1, holder)
        for e in (2, 1, 3):
            send(place, place, REST_IN, dev(s, t, z, up(y, e)), holder, 2)
        y_from = up(y, 4 - d)
        here = y_from // 2 == s
        place = out.at[out_rows(z, y_from), half[1]]
        arrived(place, FY_IN + d - 1, here)
        for e in (2, 1, 3):
            send(place, place, REST_IN, dev(s, t, up(z, e), y), here, 2)
    assert len(pending) <= N_SEND - 3
    flush(len(pending))
    sent(out.at[0:384], 0, second)
    sent(out.at[0:64], 1, cross)
    guest = jnp.logical_not(holder)
    arrived(out.at[0:320], REST_IN, holder & second)
    arrived(out.at[0:384], REST_IN, holder & first)
    arrived(out.at[0:448], REST_IN, guest)
    sent(out.at[0:384], 2, holder)
    sent(out.at[0:192], 2, guest)


def on_device(*arrays):
    hbm = pl.BlockSpec(memory_space=pl.ANY)
    vmem = pl.BlockSpec(memory_space=pltpu.VMEM)
    return pl.pallas_call(
        kernel,
        out_shape=pltpu.VMEM((512, 1024), BF),
        in_specs=[hbm, hbm, hbm, hbm, hbm, hbm, pl.BlockSpec(memory_space=pltpu.SMEM)],
        out_specs=vmem,
        scratch_shapes=[
            pltpu.VMEM((1024, 512), BF),
            pltpu.VMEM((1024, 512), BF),
            pltpu.VMEM((512, 1024), BF),
            pltpu.VMEM((256, 1024), BF),
            pltpu.VMEM((256, 1024), BF),
            pltpu.VMEM((256, 512), F32),
            pltpu.VMEM((2, 4, 128, 128), BF),
            pltpu.VMEM((2, 3, 128, 128), BF),
            pltpu.VMEM((4, 128, 256), BF),
            pltpu.VMEM((3, 128, 256), BF),
            pltpu.VMEM((2, 8, 128), F32),
            pltpu.VMEM((3, 8, 128), F32),
            pltpu.VMEM((1024, 256), BF),
            pltpu.VMEM((2, 128, 128), BF),
            pltpu.VMEM((4, 128, 256), BF),
            pltpu.VMEM((4, 4, 64, 256), BF),
            pltpu.VMEM((4, 3, 64, 256), BF),
            pltpu.VMEM((64, 1024), BF),
            pltpu.VMEM((64, 1024), BF),
            pltpu.VMEM((1, 4096), F32),
            pltpu.SemaphoreType.DMA((N_SEND,)),
            pltpu.SemaphoreType.DMA((N_RECV,)),
            pltpu.SemaphoreType.DMA((N_LOCAL,)),
            pltpu.SemaphoreType.REGULAR,
        ],
        compiler_params=pltpu.CompilerParams(
            collective_id=0, has_side_effects=True, vmem_limit_bytes=56 * 1024 * 1024
        ),
    )(*arrays)


def solution(mesh):
    in_specs = (
        P(None, "tp"),
        P("section", None),
        P("section", "rep", "tp"),
        P("section", "rep", "tp"),
        P("section", "rep", "tp"),
        P("section", "rep", "tp"),
        P(),
    )
    return jax.shard_map(
        on_device, mesh=mesh, in_specs=in_specs, out_specs=P("section", "tp"), check_vma=False
    )
```

```python
import math

import jax
import jax.numpy as jnp
from jax import lax
from jax.experimental import pallas as pl
from jax.experimental.pallas import tpu as pltpu
from jax.sharding import PartitionSpec as P

MESH = pl.DeviceIdType.MESH
BF = jnp.bfloat16
F32 = jnp.float32
D = 4096
GROUPS = 8
UNIT = 16
LARGEST = 3.0e38
SCALE = math.log2(math.e) / math.sqrt(128)

KV_LEFT, KV_RIGHT, KV_FAR = 0, 2, 4
Q_LEFT, Q_RIGHT, Q_FAR = 6, 8, 10
O_LEFT, O_RIGHT, O_FAR = 12, 13, 14
X_IN = 77
RS_IN, SQ_IN, RQ_IN = (24, 105), 27, 30
KV_IN = (33, 70)
AT_IN = 40
RO_IN = 93
RES_IN = 54
FZ_IN, FY_IN, REST_IN = 55, 58, 61
FINE = 62
N_RECV = 108
N_SEND = 140
N_LOCAL = 8


def kernel(
    emb, gain, wq, wk, wv, wo, blocks, out,
    WKV, WQ, WO, X, XG, ACC, PK, PKR, PQ, PQR, SQ, SQR, KV, AT, ATR, OS, OR, RES, ST, GAIN,
    send_sems, recv_sems, local_sems, go,
):
    s = lax.axis_index("section")
    t = lax.axis_index("tp")
    r = lax.axis_index("rep")
    z = r // 4
    y = r % 4
    g = z // 2
    zh = z % 2
    first = s == 0
    second = s == 1
    diagonal = z == t
    apart = jnp.logical_not(diagonal)

    def dev(s_, t_, z_, y_):
        return (s_, t_, z_ * 4 + y_)

    def up(v, d):
        return (v + d) % 4

    pending = []

    def send(src, dst, ridx, device, when=None, group=None):
        c = pltpu.make_async_remote_copy(
            src_ref=src, dst_ref=dst,
            send_sem=send_sems.at[len(pending) if group is None else N_SEND - 1 - group],
            recv_sem=recv_sems.at[ridx], device_id=device, device_id_type=MESH,
        )
        if when is None:
            c.start()
        else:
            pl.when(when)(c.start)
        if group is None:
            pending.append((c, when))

    finished = [0]

    def flush(count):
        for c, when in pending[finished[0]:count]:
            if when is None:
                c.wait_send()
            else:
                pl.when(when)(c.wait_send)
        finished[0] = max(finished[0], count)

    def arrived(ref, ridx, when=None):
        c = pltpu.make_async_remote_copy(
            src_ref=ref, dst_ref=ref, send_sem=send_sems.at[0],
            recv_sem=recv_sems.at[ridx], device_id=dev(1 - s, t, z, y), device_id_type=MESH,
        )
        if when is None:
            c.wait_recv()
        else:
            pl.when(when)(c.wait_recv)

    def sent(ref, group, when):
        c = pltpu.make_async_remote_copy(
            src_ref=ref, dst_ref=ref, send_sem=send_sems.at[N_SEND - 1 - group],
            recv_sem=recv_sems.at[0], device_id=dev(1 - s, t, z, y), device_id_type=MESH,
        )
        pl.when(when)(c.wait_send)

    def rows(start, size):
        return pl.ds(pl.multiple_of(start, size), size)

    KV[:, 128:256] = jnp.zeros((1024, 128), BF)

    barrier = pltpu.get_barrier_semaphore()

    def greet(device):
        pl.semaphore_signal(barrier, inc=1, device_id=device, device_id_type=MESH)

    for d in range(4):
        @pl.when(first)
        def _():
            greet(dev(1, d, t, y))

        @pl.when(second)
        def _():
            greet(dev(0, z, d, y))
    for d in (2, 1, 3):
        greet(dev(s, up(t, d), t, y))
        greet(dev(s, z, up(z, d), y))

    @pl.when(apart)
    def _():
        greet(dev(s, t, t, y))
        greet(dev(s, z, z, y))
    for d in (2, 1, 3):
        greet(dev(s, t, z + 1 - 2 * zh, up(y, d)))
        greet(dev(s, t, z, up(y, d)))
        greet(dev(s, t, up(z, d), y))
        greet(dev(1 - s, t, z, up(y, d)))
        greet(dev(1 - s, t, up(z, d), y))
    greet(dev(1 - s, t, z, y))
    greet(dev(1 - s, t, up(z, 2), up(y, 2)))

    @pl.when(second)
    def _():
        greet(dev(1, t, up(z, 2), up(y, 2)))

    at_y = rows(256 * y, 256)
    kc, vc = pl.ds(0, 256), pl.ds(256, 256)
    own = [
        pltpu.make_async_copy(wk.at[0], WKV.at[at_y, kc], local_sems.at[0]),
        pltpu.make_async_copy(wv.at[0], WKV.at[at_y, vc], local_sems.at[1]),
        pltpu.make_async_copy(wq.at[0], WQ.at[at_y], local_sems.at[2]),
        pltpu.make_async_copy(wo.at[0], WO.at[rows(128 * y, 128)], local_sems.at[3]),
        pltpu.make_async_copy(gain, GAIN, local_sems.at[6]),
    ]
    for c in own:
        c.start()
    my_emb = emb.at[rows(256 * y + 64 * z, 64)]
    my_rows = rows(64 * z, 64)
    own_x = pltpu.make_async_copy(my_emb, X.at[my_rows], local_sems.at[4])
    own_res = pltpu.make_async_copy(my_emb, RES, local_sems.at[5])
    pl.when(first & diagonal)(own_x.start)
    pl.when(first)(own_res.start)

    pl.semaphore_wait(barrier, 27 + s + 2 * (1 - diagonal.astype(jnp.int32)))

    right, left, far = up(y, 1), up(y, 3), up(y, 2)
    dev_r, dev_l = dev(s, t, z, right), dev(s, t, z, left)
    at_l, at_r, at_f = rows(256 * left, 256), rows(256 * right, 256), rows(256 * far, 256)

    @pl.when(second)
    def _():
        pl.semaphore_wait(go, 1)

    def kv_part(block, h, c):
        return WKV.at[rows(256 * block + 128 * h, 128), c]

    for h in range(2):
        send(wk.at[0, pl.ds(128 * h, 128)], kv_part(y, h, kc), FINE + h, dev_r)
        send(wv.at[0, pl.ds(128 * h, 128)], kv_part(y, h, vc), FINE + 2 + h, dev_l)

    half = (pl.ds(0, 512), pl.ds(512, 512))
    quarter = [pl.ds(256 * c, 256) for c in range(4)]
    for d in (2, 1, 3):
        send(my_emb, X.at[my_rows], X_IN + z, dev(0, up(t, d), t, y), first)
    send(my_emb, X.at[my_rows], X_IN + z, dev(0, t, t, y), first & apart)

    send(wv.at[0], WKV.at[at_y, vc], KV_LEFT + 1, dev_r)
    send(wk.at[0], WKV.at[at_y, kc], KV_RIGHT, dev_l)
    for h in range(2):
        part = kv_part(left, h, kc)
        arrived(part, FINE + h)
        send(part, part, FINE + 4 + h, dev_r)
        part = kv_part(right, h, vc)
        arrived(part, FINE + 2 + h)
        send(part, part, FINE + 6 + h, dev_l)

    def q_rows(block, h):
        return rows(256 * block + 128 * h, 128)

    q_src = (wq.at[0, pl.ds(0, 128)], wq.at[0, pl.ds(128, 128)])
    send(q_src[0], WQ.at[q_rows(y, 0)], Q_LEFT, dev_r)
    send(q_src[1], WQ.at[q_rows(y, 1)], Q_RIGHT + 1, dev_l)
    send(q_src[1], WQ.at[q_rows(y, 1)], Q_LEFT + 1, dev_r)
    send(q_src[0], WQ.at[q_rows(y, 0)], Q_RIGHT, dev_l)

    def forward_q(when):
        low, high = WQ.at[q_rows(left, 0)], WQ.at[q_rows(right, 1)]
        arrived(low, Q_LEFT, when)
        send(low, low, Q_FAR, dev_r, when)
        arrived(high, Q_RIGHT + 1, when)
        send(high, high, Q_FAR + 1, dev_l, when)

    ow_y = rows(128 * y, 128)
    ow_l, ow_r = rows(128 * left, 128), rows(128 * right, 128)

    def out_part(block, h):
        return WO.at[rows(128 * block + 64 * h, 64)]

    def send_out_weights(when):
        send(wo.at[0], WO.at[ow_y], O_LEFT, dev_r, when)
        send(wo.at[0], WO.at[ow_y], O_RIGHT, dev_l, when)

    def forward_out_weights(when):
        arrived(WO.at[ow_l], O_LEFT, when)
        send(out_part(left, 0), out_part(left, 0), O_FAR, dev_r, when)
        arrived(WO.at[ow_r], O_RIGHT, when)
        send(out_part(right, 1), out_part(right, 1), O_FAR + 1, dev_l, when)

    forward_q(second)
    send_out_weights(second)

    def multiply(block, ref, columns):
        at = rows(256 * block, 256)
        return jnp.dot(XG[:, at], ref[at, columns], preferred_element_type=F32)

    def pack(part):
        for gg in range(2):
            for hh in range(2):
                piece = ACC[128 * hh:128 * hh + 128, 256 * part + 128 * gg:256 * part + 128 * gg + 128]
                PK[part, 2 * gg + hh] = piece.astype(BF)
        for d in (2, 1, 3):
            other = up(z, d)
            send(PK.at[part, other], PKR.at[part, d - 1], RS_IN[part] + d - 1, dev(s, t, other, y))

    def scale_rows(squares):
        scale = lax.rsqrt(squares * (1.0 / D) + 1e-5)
        XG[...] = (X[...].astype(F32) * scale * GAIN[:, rows(1024 * z, 1024)]).astype(BF)
        for h in range(2):
            column = jnp.broadcast_to(squares[128 * h:128 * h + 128], (128, 128))
            SQ[h] = jnp.transpose(column)[0:8]

    for c in own:
        c.wait()

    @pl.when(first)
    def _():
        pl.when(diagonal)(own_x.wait)
        for zp in range(4):
            arrived(X.at[pl.ds(64 * zp, 64)], X_IN + zp, jnp.logical_not(diagonal & (z == zp)))
        x = X[...].astype(F32)
        scale_rows(jnp.sum(x * x, axis=1, keepdims=True))
        part = multiply(y, WKV, kc) + multiply(left, WKV, kc)
        arrived(WKV.at[at_r, kc], KV_RIGHT)
        part = part + multiply(right, WKV, kc)
        for h in range(2):
            arrived(kv_part(far, h, kc), FINE + 4 + h)
        ACC[:, kc] = part + multiply(far, WKV, kc)

    @pl.when(second)
    def _():
        arrived(WKV.at[at_l, vc], KV_LEFT + 1)
        arrived(WKV.at[at_r, kc], KV_RIGHT)
        for h in range(2):
            arrived(kv_part(far, h, kc), FINE + 4 + h)
            arrived(kv_part(far, h, vc), FINE + 6 + h)
        squares = jnp.zeros((256, 1), F32)
        for c in range(4):
            for zp in range(4):
                arrived(X.at[pl.ds(64 * zp, 64), quarter[c]], X_IN + 4 * c + zp)
            x = X[:, quarter[c]].astype(F32)
            squares = squares + jnp.sum(x * x, axis=1, keepdims=True)
        scale_rows(squares)
        ACC[:, kc] = jnp.dot(XG[...], WKV[:, kc], preferred_element_type=F32)

    for d in (2, 1, 3):
        other = up(z, d)
        send(SQ.at[other % 2], SQR.at[d - 1], SQ_IN + d - 1, dev(s, t, other, y))
    pack(0)

    @pl.when(first)
    def _():
        arrived(WKV.at[at_l, vc], KV_LEFT + 1)
        part = multiply(y, WKV, vc) + multiply(left, WKV, vc) + multiply(right, WKV, vc)
        for h in range(2):
            arrived(kv_part(far, h, vc), FINE + 6 + h)
        ACC[:, vc] = part + multiply(far, WKV, vc)

    @pl.when(second)
    def _():
        ACC[:, vc] = jnp.dot(XG[...], WKV[:, vc], preferred_element_type=F32)

    pack(1)

    forward_q(first)
    send_out_weights(first)
    all_q = pl.ds(0, 512)
    part = multiply(y, WQ, all_q)
    arrived(WQ.at[q_rows(left, 1)], Q_LEFT + 1)
    part = part + multiply(left, WQ, all_q)
    arrived(WQ.at[q_rows(right, 0)], Q_RIGHT)
    part = part + multiply(right, WQ, all_q)
    arrived(WQ.at[q_rows(far, 0)], Q_FAR)
    arrived(WQ.at[q_rows(far, 1)], Q_FAR + 1)
    part = part + multiply(far, WQ, all_q)
    for gg in range(2):
        for hh in range(2):
            PQ[2 * gg + hh] = part[128 * hh:128 * hh + 128, 256 * gg:256 * gg + 256].astype(BF)
    for d in (2, 1, 3):
        other = up(z, d)
        send(PQ.at[other], PQR.at[d - 1], RQ_IN + d - 1, dev(s, t, other, y))

    means = [SQ[zh] * (1.0 / D)]
    for d in (1, 2, 3):
        arrived(SQR.at[d - 1], SQ_IN + d - 1)
        means.append(SQR[d - 1] * (1.0 / D))
    inverse = lax.rsqrt(means[0] + means[1] + means[2] + means[3] + 1e-5)
    shares = []
    for mean in means:
        share = inverse * jnp.sqrt(jnp.minimum(mean + 1e-5, LARGEST))
        shares.append(jnp.transpose(jnp.broadcast_to(share[0:1], (128, 128))))
    block = 2 * y + zh
    lanes = (pl.ds(0, 128), pl.ds(128, 128))

    def cached(theirs, part):
        return KV.at[rows(128 * theirs, 128), lanes[part]]

    for part in range(2):
        total = PK[part, z].astype(F32) * shares[0]
        for d in (1, 3, 2):
            arrived(PKR.at[part, d - 1], RS_IN[part] + d - 1)
            total = total + PKR[part, d - 1].astype(F32) * shares[d]
        mine = cached(block, part)
        mine[...] = total.astype(BF)
        for dy in (2, 1, 3, 0):
            for dz in range(2):
                if dy + dz == 0:
                    continue
                y_to = up(y, dy)
                h_to = zh if dz == 0 else 1 - zh
                send(
                    mine, mine, KV_IN[part] + 2 * dy + dz - 1,
                    dev(s, t, 2 * g + h_to, y_to), (2 * y_to + h_to > block) & (2 * y_to + h_to < block + 7),
                )
    front = len(pending)

    places = 256 * y + 128 * zh + lax.broadcasted_iota(jnp.int32, (128, 1), 0)
    starts = []
    run = jnp.int32(0)
    for c in range(GROUPS):
        starts.append(run)
        run = run + blocks[c] * UNIT
    lowest = jnp.zeros((128, 1), jnp.int32)
    for c in range(GROUPS - 2):
        lowest = jnp.where(places >= starts[c + 2], starts[c], lowest)
    keys_at = lax.broadcasted_iota(jnp.int32, (128, 1024), 1)
    allowed = (keys_at <= places) & (keys_at >= lowest)

    forward_out_weights(first)
    wide = [jnp.concatenate([share, share], axis=1) for share in shares]
    total = PQ[z].astype(F32) * wide[0]
    for d in (1, 3, 2):
        arrived(PQR.at[d - 1], RQ_IN + d - 1)
        total = total + PQR[d - 1].astype(F32) * wide[d]
    queries = (total * SCALE).astype(BF)

    def wait_cached(part):
        for dy in (1, 3, 2, 0):
            for dz in range(2):
                if dy + dz == 0:
                    continue
                y_from = up(y, 4 - dy)
                h_from = zh if dz == 0 else 1 - zh
                theirs = 2 * y_from + h_from
                arrived(cached(theirs, part), KV_IN[part] + 2 * dy + dz - 1, (theirs < block) & (theirs > block - 7))

    wait_cached(0)
    keys = KV[:, 0:128]
    weights = []
    for h in range(2):
        scores = lax.dot_general(
            queries[:, 128 * h:128 * h + 128], keys, (((1,), (1,)), ((), ())), preferred_element_type=F32
        )
        scores = jnp.where(allowed, scores, -jnp.inf)
        exps = jnp.exp2(scores - jnp.max(scores, axis=1, keepdims=True))
        norm = jnp.sum(exps, axis=1, keepdims=True)
        weights.append((exps.astype(BF), norm))
    wait_cached(1)
    values = KV[:, 128:256]
    for h in range(2):
        exps, norm = weights[h]
        heads = jnp.dot(exps, values, preferred_element_type=F32) / norm
        AT[h] = heads.astype(BF)
        for d in (2, 1, 3):
            send(AT.at[h], ATR.at[z, :, lanes[h]], AT_IN + 4 * h + z, dev(s, up(t, d), t, y))
        send(AT.at[h], ATR.at[z, :, lanes[h]], AT_IN + 4 * h + z, dev(s, t, t, y), apart)

    @pl.when(diagonal)
    def _():
        for h in range(2):
            ATR[z, :, lanes[h]] = AT[h]

    forward_out_weights(second)
    flush(front)

    @pl.when(first)
    def _():
        pl.semaphore_signal(go, inc=1, device_id=dev(1, t, z, y), device_id_type=MESH)

    pl.when(first)(own_res.wait)
    arrived(RES, RES_IN, second)
    arrived(out_part(far, 0), O_FAR)
    arrived(out_part(far, 1), O_FAR + 1)
    for zp in range(4):
        for h in range(2):
            arrived(ATR.at[zp, :, lanes[h]], AT_IN + 4 * h + zp, jnp.logical_not(diagonal & (z == zp)))
    for c in range(4):
        for hh in range(2):
            product = jnp.dot(ATR[hh], WO[0:256, quarter[c]], preferred_element_type=F32)
            product = product + jnp.dot(ATR[2 + hh], WO[256:512, quarter[c]], preferred_element_type=F32)
            OS[c, 2 * hh] = product[0:64].astype(BF)
            OS[c, 2 * hh + 1] = product[64:128].astype(BF)
        for d in (2, 1, 3):
            send(OS.at[c, up(z, d)], OR.at[c, d - 1], RO_IN + 3 * c + d - 1, dev(s, t, up(z, d), y))
    summed = len(pending)

    sec = y // 2
    cross = second & (sec == 0)

    def out_rows(z_, y_):
        return rows(256 * (y_ % 2) + 64 * z_, 64)

    at_out = out_rows(z, y)

    for c in range(4):
        new = RES[:, quarter[c]].astype(F32) + OS[c, z].astype(F32)
        for d in (1, 3, 2):
            arrived(OR.at[c, d - 1], RO_IN + 3 * c + d - 1)
            new = new + OR[c, d - 1].astype(F32)
        ST[:, quarter[c]] = new.astype(BF)
        mine = ST.at[:, quarter[c]]
        for d in (2, 1, 3, 0):
            send(mine, X.at[my_rows, quarter[c]], X_IN + 4 * c + z, dev(1, up(t, d), t, y), first)
        if c % 2 == 0:
            continue
        mine, place = ST.at[:, half[c // 2]], out.at[at_out, half[c // 2]]
        for d in (2, 1, 3):
            if c == 1:
                send(mine, place, FZ_IN + d - 1, dev(sec, t, up(z, d), y), second, 0)
            else:
                send(mine, place, FY_IN + d - 1, dev(sec, t, z, up(y, d)), second, 0)
    for c in range(2):
        mine, place = ST.at[:, half[c]], out.at[at_out, half[c]]
        for d in (2, 1, 3):
            if c == 0:
                send(mine, place, REST_IN, dev(sec, t, z, up(y, d)), second, 0)
            else:
                send(mine, place, REST_IN, dev(sec, t, up(z, d), y), second, 0)
    send(ST, out.at[at_out], REST_IN, dev(sec, t, up(z, 2), up(y, 2)), second)
    send(ST, out.at[at_out], REST_IN, dev(sec, t, z, y), cross, 1)
    send(ST, RES, RES_IN, dev(1, t, z, y), first)

    @pl.when(second & (sec == 1))
    def _():
        out[at_out, :] = ST[...]

    holder = sec == s
    for d in (1, 3, 2):
        place = out.at[out_rows(up(z, 4 - d), y), half[0]]
        arrived(place, FZ_IN + d - 1, holder)
        for e in (2, 1, 3) if d != 2 else (1, 3):
            send(place, place, REST_IN, dev(s, t, z, up(y, e)), holder, 2)
        y_from = up(y, 4 - d)
        here = y_from // 2 == s
        place = out.at[out_rows(z, y_from), half[1]]
        arrived(place, FY_IN + d - 1, here)
        for e in (2, 1, 3) if d != 2 else (1, 3):
            send(place, place, REST_IN, dev(s, t, up(z, e), y), here, 2)
    assert len(pending) <= N_SEND - 3
    flush(len(pending))
    sent(out.at[0:384], 0, second)
    sent(out.at[0:64], 1, cross)
    guest = jnp.logical_not(holder)
    arrived(out.at[0:320], REST_IN, holder & second)
    arrived(out.at[0:384], REST_IN, holder & first)
    arrived(out.at[0:448], REST_IN, guest)
    sent(out.at[0:352], 2, holder)
    sent(out.at[0:160], 2, guest)


def on_device(*arrays):
    hbm = pl.BlockSpec(memory_space=pl.ANY)
    vmem = pl.BlockSpec(memory_space=pltpu.VMEM)
    return pl.pallas_call(
        kernel,
        out_shape=pltpu.VMEM((512, 1024), BF),
        in_specs=[hbm, hbm, hbm, hbm, hbm, hbm, pl.BlockSpec(memory_space=pltpu.SMEM)],
        out_specs=vmem,
        scratch_shapes=[
            pltpu.VMEM((1024, 512), BF),
            pltpu.VMEM((1024, 512), BF),
            pltpu.VMEM((512, 1024), BF),
            pltpu.VMEM((256, 1024), BF),
            pltpu.VMEM((256, 1024), BF),
            pltpu.VMEM((256, 512), F32),
            pltpu.VMEM((2, 4, 128, 128), BF),
            pltpu.VMEM((2, 3, 128, 128), BF),
            pltpu.VMEM((4, 128, 256), BF),
            pltpu.VMEM((3, 128, 256), BF),
            pltpu.VMEM((2, 8, 128), F32),
            pltpu.VMEM((3, 8, 128), F32),
            pltpu.VMEM((1024, 256), BF),
            pltpu.VMEM((2, 128, 128), BF),
            pltpu.VMEM((4, 128, 256), BF),
            pltpu.VMEM((4, 4, 64, 256), BF),
            pltpu.VMEM((4, 3, 64, 256), BF),
            pltpu.VMEM((64, 1024), BF),
            pltpu.VMEM((64, 1024), BF),
            pltpu.VMEM((1, 4096), F32),
            pltpu.SemaphoreType.DMA((N_SEND,)),
            pltpu.SemaphoreType.DMA((N_RECV,)),
            pltpu.SemaphoreType.DMA((N_LOCAL,)),
            pltpu.SemaphoreType.REGULAR,
        ],
        compiler_params=pltpu.CompilerParams(
            collective_id=0, has_side_effects=True, vmem_limit_bytes=56 * 1024 * 1024
        ),
    )(*arrays)


def solution(mesh):
    in_specs = (
        P(None, "tp"),
        P("section", None),
        P("section", "rep", "tp"),
        P("section", "rep", "tp"),
        P("section", "rep", "tp"),
        P("section", "rep", "tp"),
        P(),
    )
    return jax.shard_map(
        on_device, mesh=mesh, in_specs=in_specs, out_specs=P("section", "tp"), check_vma=False
    )
```

```python
import math

import jax
import jax.numpy as jnp
from jax import lax
from jax.experimental import pallas as pl
from jax.experimental.pallas import tpu as pltpu
from jax.sharding import PartitionSpec as P

MESH = pl.DeviceIdType.MESH
BF = jnp.bfloat16
F32 = jnp.float32
D = 4096
GROUPS = 8
UNIT = 16
LARGEST = 3.0e38
SCALE = math.log2(math.e) / math.sqrt(128)

KV_LEFT, KV_RIGHT, KV_FAR = 0, 2, 4
Q_LEFT, Q_RIGHT, Q_FAR = 6, 8, 10
O_LEFT, O_RIGHT, O_FAR = 12, 13, 14
X_IN = 77
RS_IN, SQ_IN, RQ_IN = (24, 105), 27, 30
KV_IN = (33, 70)
AT_IN = 40
RO_IN = 93
RES_IN = 54
FZ_IN, FY_IN, REST_IN = 55, 58, 61
FINE = 62
N_RECV = 108
N_SEND = 140
N_LOCAL = 8


def kernel(
    emb, gain, wq, wk, wv, wo, blocks, out,
    WKV, WQ, WO, X, XG, ACC, PK, PKR, PQ, PQR, SQ, SQR, KV, AT, ATR, OS, OR, RES, ST, GAIN,
    send_sems, recv_sems, local_sems, go,
):
    s = lax.axis_index("section")
    t = lax.axis_index("tp")
    r = lax.axis_index("rep")
    z = r // 4
    y = r % 4
    g = z // 2
    zh = z % 2
    first = s == 0
    second = s == 1
    diagonal = z == t
    apart = jnp.logical_not(diagonal)

    def dev(s_, t_, z_, y_):
        return (s_, t_, z_ * 4 + y_)

    def up(v, d):
        return (v + d) % 4

    pending = []

    def send(src, dst, ridx, device, when=None, group=None):
        c = pltpu.make_async_remote_copy(
            src_ref=src, dst_ref=dst,
            send_sem=send_sems.at[len(pending) if group is None else N_SEND - 1 - group],
            recv_sem=recv_sems.at[ridx], device_id=device, device_id_type=MESH,
        )
        if when is None:
            c.start()
        else:
            pl.when(when)(c.start)
        if group is None:
            pending.append((c, when))

    finished = [0]

    def flush(count):
        for c, when in pending[finished[0]:count]:
            if when is None:
                c.wait_send()
            else:
                pl.when(when)(c.wait_send)
        finished[0] = max(finished[0], count)

    def arrived(ref, ridx, when=None):
        c = pltpu.make_async_remote_copy(
            src_ref=ref, dst_ref=ref, send_sem=send_sems.at[0],
            recv_sem=recv_sems.at[ridx], device_id=dev(1 - s, t, z, y), device_id_type=MESH,
        )
        if when is None:
            c.wait_recv()
        else:
            pl.when(when)(c.wait_recv)

    def sent(ref, group, when):
        c = pltpu.make_async_remote_copy(
            src_ref=ref, dst_ref=ref, send_sem=send_sems.at[N_SEND - 1 - group],
            recv_sem=recv_sems.at[0], device_id=dev(1 - s, t, z, y), device_id_type=MESH,
        )
        pl.when(when)(c.wait_send)

    def rows(start, size):
        return pl.ds(pl.multiple_of(start, size), size)

    KV[:, 128:256] = jnp.zeros((1024, 128), BF)

    barrier = pltpu.get_barrier_semaphore()

    def greet(device):
        pl.semaphore_signal(barrier, inc=1, device_id=device, device_id_type=MESH)

    for d in range(4):
        @pl.when(first)
        def _():
            greet(dev(1, d, t, y))

        @pl.when(second)
        def _():
            greet(dev(0, z, d, y))
    for d in (2, 1, 3):
        greet(dev(s, up(t, d), t, y))
        greet(dev(s, z, up(z, d), y))

    @pl.when(apart)
    def _():
        greet(dev(s, t, t, y))
        greet(dev(s, z, z, y))
    for d in (2, 1, 3):
        greet(dev(s, t, z + 1 - 2 * zh, up(y, d)))
        greet(dev(s, t, z, up(y, d)))
        greet(dev(s, t, up(z, d), y))
        greet(dev(1 - s, t, z, up(y, d)))
        greet(dev(1 - s, t, up(z, d), y))
    greet(dev(1 - s, t, z, y))

    at_y = rows(256 * y, 256)
    kc, vc = pl.ds(0, 256), pl.ds(256, 256)
    own = [
        pltpu.make_async_copy(wk.at[0], WKV.at[at_y, kc], local_sems.at[0]),
        pltpu.make_async_copy(wv.at[0], WKV.at[at_y, vc], local_sems.at[1]),
        pltpu.make_async_copy(wq.at[0], WQ.at[at_y], local_sems.at[2]),
        pltpu.make_async_copy(wo.at[0], WO.at[rows(128 * y, 128)], local_sems.at[3]),
        pltpu.make_async_copy(gain, GAIN, local_sems.at[6]),
    ]
    for c in own:
        c.start()
    my_emb = emb.at[rows(256 * y + 64 * z, 64)]
    my_rows = rows(64 * z, 64)
    own_x = pltpu.make_async_copy(my_emb, X.at[my_rows], local_sems.at[4])
    own_res = pltpu.make_async_copy(my_emb, RES, local_sems.at[5])
    pl.when(first & diagonal)(own_x.start)
    pl.when(first)(own_res.start)

    pl.semaphore_wait(barrier, 26 + 2 * (1 - diagonal.astype(jnp.int32)))

    right, left, far = up(y, 1), up(y, 3), up(y, 2)
    dev_r, dev_l = dev(s, t, z, right), dev(s, t, z, left)
    at_l, at_r, at_f = rows(256 * left, 256), rows(256 * right, 256), rows(256 * far, 256)

    @pl.when(second)
    def _():
        pl.semaphore_wait(go, 1)

    def kv_part(block, h, c):
        return WKV.at[rows(256 * block + 128 * h, 128), c]

    for h in range(2):
        send(wk.at[0, pl.ds(128 * h, 128)], kv_part(y, h, kc), FINE + h, dev_r)
        send(wv.at[0, pl.ds(128 * h, 128)], kv_part(y, h, vc), FINE + 2 + h, dev_l)

    half = (pl.ds(0, 512), pl.ds(512, 512))
    quarter = [pl.ds(256 * c, 256) for c in range(4)]
    for d in (2, 1, 3):
        send(my_emb, X.at[my_rows], X_IN + z, dev(0, up(t, d), t, y), first)
    send(my_emb, X.at[my_rows], X_IN + z, dev(0, t, t, y), first & apart)

    send(wv.at[0], WKV.at[at_y, vc], KV_LEFT + 1, dev_r)
    send(wk.at[0], WKV.at[at_y, kc], KV_RIGHT, dev_l)
    for h in range(2):
        part = kv_part(left, h, kc)
        arrived(part, FINE + h)
        send(part, part, FINE + 4 + h, dev_r)
        part = kv_part(right, h, vc)
        arrived(part, FINE + 2 + h)
        send(part, part, FINE + 6 + h, dev_l)

    def q_rows(block, h):
        return rows(256 * block + 128 * h, 128)

    q_src = (wq.at[0, pl.ds(0, 128)], wq.at[0, pl.ds(128, 128)])
    send(q_src[0], WQ.at[q_rows(y, 0)], Q_LEFT, dev_r)
    send(q_src[1], WQ.at[q_rows(y, 1)], Q_RIGHT + 1, dev_l)
    send(q_src[1], WQ.at[q_rows(y, 1)], Q_LEFT + 1, dev_r)
    send(q_src[0], WQ.at[q_rows(y, 0)], Q_RIGHT, dev_l)

    def forward_q(when):
        low, high = WQ.at[q_rows(left, 0)], WQ.at[q_rows(right, 1)]
        arrived(low, Q_LEFT, when)
        send(low, low, Q_FAR, dev_r, when)
        arrived(high, Q_RIGHT + 1, when)
        send(high, high, Q_FAR + 1, dev_l, when)

    ow_y = rows(128 * y, 128)
    ow_l, ow_r = rows(128 * left, 128), rows(128 * right, 128)

    def out_part(block, h):
        return WO.at[rows(128 * block + 64 * h, 64)]

    def send_out_weights(when):
        send(wo.at[0], WO.at[ow_y], O_LEFT, dev_r, when)
        send(wo.at[0], WO.at[ow_y], O_RIGHT, dev_l, when)

    def forward_out_weights(when):
        arrived(WO.at[ow_l], O_LEFT, when)
        send(out_part(left, 0), out_part(left, 0), O_FAR, dev_r, when)
        arrived(WO.at[ow_r], O_RIGHT, when)
        send(out_part(right, 1), out_part(right, 1), O_FAR + 1, dev_l, when)

    forward_q(second)
    send_out_weights(second)

    def multiply(block, ref, columns):
        at = rows(256 * block, 256)
        return jnp.dot(XG[:, at], ref[at, columns], preferred_element_type=F32)

    def pack(part):
        for gg in range(2):
            for hh in range(2):
                piece = ACC[128 * hh:128 * hh + 128, 256 * part + 128 * gg:256 * part + 128 * gg + 128]
                PK[part, 2 * gg + hh] = piece.astype(BF)
        for d in (2, 1, 3):
            other = up(z, d)
            send(PK.at[part, other], PKR.at[part, d - 1], RS_IN[part] + d - 1, dev(s, t, other, y))

    def scale_rows(squares):
        scale = lax.rsqrt(squares * (1.0 / D) + 1e-5)
        XG[...] = (X[...].astype(F32) * scale * GAIN[:, rows(1024 * z, 1024)]).astype(BF)
        for h in range(2):
            column = jnp.broadcast_to(squares[128 * h:128 * h + 128], (128, 128))
            SQ[h] = jnp.transpose(column)[0:8]

    for c in own:
        c.wait()

    @pl.when(first)
    def _():
        pl.when(diagonal)(own_x.wait)
        for zp in range(4):
            arrived(X.at[pl.ds(64 * zp, 64)], X_IN + zp, jnp.logical_not(diagonal & (z == zp)))
        x = X[...].astype(F32)
        scale_rows(jnp.sum(x * x, axis=1, keepdims=True))
        part = multiply(y, WKV, kc) + multiply(left, WKV, kc)
        arrived(WKV.at[at_r, kc], KV_RIGHT)
        part = part + multiply(right, WKV, kc)
        for h in range(2):
            arrived(kv_part(far, h, kc), FINE + 4 + h)
        ACC[:, kc] = part + multiply(far, WKV, kc)

    @pl.when(second)
    def _():
        arrived(WKV.at[at_l, vc], KV_LEFT + 1)
        arrived(WKV.at[at_r, kc], KV_RIGHT)
        for h in range(2):
            arrived(kv_part(far, h, kc), FINE + 4 + h)
            arrived(kv_part(far, h, vc), FINE + 6 + h)
        squares = jnp.zeros((256, 1), F32)
        for c in range(4):
            for zp in range(4):
                arrived(X.at[pl.ds(64 * zp, 64), quarter[c]], X_IN + 4 * c + zp)
            x = X[:, quarter[c]].astype(F32)
            squares = squares + jnp.sum(x * x, axis=1, keepdims=True)
        scale_rows(squares)
        ACC[:, kc] = jnp.dot(XG[...], WKV[:, kc], preferred_element_type=F32)

    for d in (2, 1, 3):
        other = up(z, d)
        send(SQ.at[other % 2], SQR.at[d - 1], SQ_IN + d - 1, dev(s, t, other, y))
    pack(0)

    @pl.when(first)
    def _():
        arrived(WKV.at[at_l, vc], KV_LEFT + 1)
        part = multiply(y, WKV, vc) + multiply(left, WKV, vc) + multiply(right, WKV, vc)
        for h in range(2):
            arrived(kv_part(far, h, vc), FINE + 6 + h)
        ACC[:, vc] = part + multiply(far, WKV, vc)

    @pl.when(second)
    def _():
        ACC[:, vc] = jnp.dot(XG[...], WKV[:, vc], preferred_element_type=F32)

    pack(1)

    forward_q(first)
    send_out_weights(first)
    all_q = pl.ds(0, 512)
    part = multiply(y, WQ, all_q)
    arrived(WQ.at[q_rows(left, 1)], Q_LEFT + 1)
    part = part + multiply(left, WQ, all_q)
    arrived(WQ.at[q_rows(right, 0)], Q_RIGHT)
    part = part + multiply(right, WQ, all_q)
    arrived(WQ.at[q_rows(far, 0)], Q_FAR)
    arrived(WQ.at[q_rows(far, 1)], Q_FAR + 1)
    part = part + multiply(far, WQ, all_q)
    for gg in range(2):
        for hh in range(2):
            PQ[2 * gg + hh] = part[128 * hh:128 * hh + 128, 256 * gg:256 * gg + 256].astype(BF)
    for d in (2, 1, 3):
        other = up(z, d)
        send(PQ.at[other], PQR.at[d - 1], RQ_IN + d - 1, dev(s, t, other, y))

    means = [SQ[zh] * (1.0 / D)]
    for d in (1, 2, 3):
        arrived(SQR.at[d - 1], SQ_IN + d - 1)
        means.append(SQR[d - 1] * (1.0 / D))
    inverse = lax.rsqrt(means[0] + means[1] + means[2] + means[3] + 1e-5)
    shares = []
    for mean in means:
        share = inverse * jnp.sqrt(jnp.minimum(mean + 1e-5, LARGEST))
        shares.append(jnp.transpose(jnp.broadcast_to(share[0:1], (128, 128))))
    block = 2 * y + zh
    lanes = (pl.ds(0, 128), pl.ds(128, 128))

    def cached(theirs, part):
        return KV.at[rows(128 * theirs, 128), lanes[part]]

    for part in range(2):
        total = PK[part, z].astype(F32) * shares[0]
        for d in (1, 3, 2):
            arrived(PKR.at[part, d - 1], RS_IN[part] + d - 1)
            total = total + PKR[part, d - 1].astype(F32) * shares[d]
        mine = cached(block, part)
        mine[...] = total.astype(BF)
        for dy in (2, 1, 3, 0):
            for dz in range(2):
                if dy + dz == 0:
                    continue
                y_to = up(y, dy)
                h_to = zh if dz == 0 else 1 - zh
                send(
                    mine, mine, KV_IN[part] + 2 * dy + dz - 1,
                    dev(s, t, 2 * g + h_to, y_to), (2 * y_to + h_to > block) & (2 * y_to + h_to < block + 7),
                )
    front = len(pending)

    places = 256 * y + 128 * zh + lax.broadcasted_iota(jnp.int32, (128, 1), 0)
    starts = []
    run = jnp.int32(0)
    for c in range(GROUPS):
        starts.append(run)
        run = run + blocks[c] * UNIT
    lowest = jnp.zeros((128, 1), jnp.int32)
    for c in range(GROUPS - 2):
        lowest = jnp.where(places >= starts[c + 2], starts[c], lowest)
    keys_at = lax.broadcasted_iota(jnp.int32, (128, 1024), 1)
    allowed = (keys_at <= places) & (keys_at >= lowest)

    forward_out_weights(first)
    forward_out_weights(second)
    wide = [jnp.concatenate([share, share], axis=1) for share in shares]
    total = PQ[z].astype(F32) * wide[0]
    for d in (1, 3, 2):
        arrived(PQR.at[d - 1], RQ_IN + d - 1)
        total = total + PQR[d - 1].astype(F32) * wide[d]
    queries = (total * SCALE).astype(BF)

    def wait_cached(part):
        for dy in (1, 3, 2, 0):
            for dz in range(2):
                if dy + dz == 0:
                    continue
                y_from = up(y, 4 - dy)
                h_from = zh if dz == 0 else 1 - zh
                theirs = 2 * y_from + h_from
                arrived(cached(theirs, part), KV_IN[part] + 2 * dy + dz - 1, (theirs < block) & (theirs > block - 7))

    wait_cached(0)
    keys = KV[:, 0:128]
    weights = []
    for h in range(2):
        scores = lax.dot_general(
            queries[:, 128 * h:128 * h + 128], keys, (((1,), (1,)), ((), ())), preferred_element_type=F32
        )
        scores = jnp.where(allowed, scores, -jnp.inf)
        exps = jnp.exp2(scores - jnp.max(scores, axis=1, keepdims=True))
        norm = jnp.sum(exps, axis=1, keepdims=True)
        weights.append((exps.astype(BF), norm))
    wait_cached(1)
    values = KV[:, 128:256]
    for h in range(2):
        exps, norm = weights[h]
        heads = jnp.dot(exps, values, preferred_element_type=F32) / norm
        AT[h] = heads.astype(BF)
        for d in (2, 1, 3):
            send(AT.at[h], ATR.at[z, :, lanes[h]], AT_IN + 4 * h + z, dev(s, up(t, d), t, y))
        send(AT.at[h], ATR.at[z, :, lanes[h]], AT_IN + 4 * h + z, dev(s, t, t, y), apart)

    @pl.when(diagonal)
    def _():
        for h in range(2):
            ATR[z, :, lanes[h]] = AT[h]

    flush(front)

    @pl.when(first)
    def _():
        pl.semaphore_signal(go, inc=1, device_id=dev(1, t, z, y), device_id_type=MESH)

    pl.when(first)(own_res.wait)
    arrived(RES, RES_IN, second)
    arrived(out_part(far, 0), O_FAR)
    arrived(out_part(far, 1), O_FAR + 1)
    for zp in range(4):
        for h in range(2):
            arrived(ATR.at[zp, :, lanes[h]], AT_IN + 4 * h + zp, jnp.logical_not(diagonal & (z == zp)))
    for c in range(4):
        for hh in range(2):
            product = jnp.dot(ATR[hh], WO[0:256, quarter[c]], preferred_element_type=F32)
            product = product + jnp.dot(ATR[2 + hh], WO[256:512, quarter[c]], preferred_element_type=F32)
            OS[c, 2 * hh] = product[0:64].astype(BF)
            OS[c, 2 * hh + 1] = product[64:128].astype(BF)
        for d in (2, 1, 3):
            send(OS.at[c, up(z, d)], OR.at[c, d - 1], RO_IN + 3 * c + d - 1, dev(s, t, up(z, d), y))
    summed = len(pending)

    sec = y // 2
    cross = second & (sec == 0)

    def out_rows(z_, y_):
        return rows(256 * (y_ % 2) + 64 * z_, 64)

    at_out = out_rows(z, y)

    for c in range(4):
        new = RES[:, quarter[c]].astype(F32) + OS[c, z].astype(F32)
        for d in (1, 3, 2):
            arrived(OR.at[c, d - 1], RO_IN + 3 * c + d - 1)
            new = new + OR[c, d - 1].astype(F32)
        ST[:, quarter[c]] = new.astype(BF)
        mine = ST.at[:, quarter[c]]
        for d in (2, 1, 3, 0):
            send(mine, X.at[my_rows, quarter[c]], X_IN + 4 * c + z, dev(1, up(t, d), t, y), first)
        if c % 2 == 0:
            continue
        mine, place = ST.at[:, half[c // 2]], out.at[at_out, half[c // 2]]
        for d in (2, 1, 3):
            if c == 1:
                send(mine, place, FZ_IN + d - 1, dev(sec, t, up(z, d), y), second, 0)
            else:
                send(mine, place, FY_IN + d - 1, dev(sec, t, z, up(y, d)), second, 0)
    for c in range(2):
        mine, place = ST.at[:, half[c]], out.at[at_out, half[c]]
        for d in (2, 1, 3):
            if c == 0:
                send(mine, place, REST_IN, dev(sec, t, z, up(y, d)), second, 0)
            else:
                send(mine, place, REST_IN, dev(sec, t, up(z, d), y), second, 0)
    send(ST, out.at[at_out], REST_IN, dev(sec, t, z, y), cross, 1)
    send(ST, RES, RES_IN, dev(1, t, z, y), first)

    @pl.when(second & (sec == 1))
    def _():
        out[at_out, :] = ST[...]

    holder = sec == s
    for d in (1, 3, 2):
        place = out.at[out_rows(up(z, 4 - d), y), half[0]]
        arrived(place, FZ_IN + d - 1, holder)
        for e in (2, 1, 3):
            send(place, place, REST_IN, dev(s, t, z, up(y, e)), holder, 2)
        y_from = up(y, 4 - d)
        here = y_from // 2 == s
        place = out.at[out_rows(z, y_from), half[1]]
        arrived(place, FY_IN + d - 1, here)
        for e in (2, 1, 3):
            send(place, place, REST_IN, dev(s, t, up(z, e), y), here, 2)
    assert len(pending) <= N_SEND - 3
    flush(len(pending))
    sent(out.at[0:384], 0, second)
    sent(out.at[0:64], 1, cross)
    guest = jnp.logical_not(holder)
    arrived(out.at[0:320], REST_IN, holder & second)
    arrived(out.at[0:384], REST_IN, holder & first)
    arrived(out.at[0:448], REST_IN, guest)
    sent(out.at[0:384], 2, holder)
    sent(out.at[0:192], 2, guest)


def on_device(*arrays):
    hbm = pl.BlockSpec(memory_space=pl.ANY)
    vmem = pl.BlockSpec(memory_space=pltpu.VMEM)
    return pl.pallas_call(
        kernel,
        out_shape=pltpu.VMEM((512, 1024), BF),
        in_specs=[hbm, hbm, hbm, hbm, hbm, hbm, pl.BlockSpec(memory_space=pltpu.SMEM)],
        out_specs=vmem,
        scratch_shapes=[
            pltpu.VMEM((1024, 512), BF),
            pltpu.VMEM((1024, 512), BF),
            pltpu.VMEM((512, 1024), BF),
            pltpu.VMEM((256, 1024), BF),
            pltpu.VMEM((256, 1024), BF),
            pltpu.VMEM((256, 512), F32),
            pltpu.VMEM((2, 4, 128, 128), BF),
            pltpu.VMEM((2, 3, 128, 128), BF),
            pltpu.VMEM((4, 128, 256), BF),
            pltpu.VMEM((3, 128, 256), BF),
            pltpu.VMEM((2, 8, 128), F32),
            pltpu.VMEM((3, 8, 128), F32),
            pltpu.VMEM((1024, 256), BF),
            pltpu.VMEM((2, 128, 128), BF),
            pltpu.VMEM((4, 128, 256), BF),
            pltpu.VMEM((4, 4, 64, 256), BF),
            pltpu.VMEM((4, 3, 64, 256), BF),
            pltpu.VMEM((64, 1024), BF),
            pltpu.VMEM((64, 1024), BF),
            pltpu.VMEM((1, 4096), F32),
            pltpu.SemaphoreType.DMA((N_SEND,)),
            pltpu.SemaphoreType.DMA((N_RECV,)),
            pltpu.SemaphoreType.DMA((N_LOCAL,)),
            pltpu.SemaphoreType.REGULAR,
        ],
        compiler_params=pltpu.CompilerParams(
            collective_id=0, has_side_effects=True, vmem_limit_bytes=56 * 1024 * 1024
        ),
    )(*arrays)


def solution(mesh):
    in_specs = (
        P(None, "tp"),
        P("section", None),
        P("section", "rep", "tp"),
        P("section", "rep", "tp"),
        P("section", "rep", "tp"),
        P("section", "rep", "tp"),
        P(),
    )
    return jax.shard_map(
        on_device, mesh=mesh, in_specs=in_specs, out_specs=P("section", "tp"), check_vma=False
    )
```
